256 devices in a mesh: ctx: 64 (over z, x, core), exp: 4 (over y).
Axes of the slice: x: 4, y: 4, z: 8, core: 2. Of those that a mesh axis runs over, the one named last changes fastest.
Arguments:
- queries: bfloat16 [16384, 4096], P('ctx', 'exp'), may hold values from -6 to 6
- keys: bfloat16 [16384, 4096], P('ctx', 'exp'), may hold values from -6 to 6
- values: bfloat16 [16384, 4096], P('ctx', 'exp'), may hold values from -6 to 6
- gates: bfloat16 [16384, 4096], P('ctx', 'exp'), may hold values from -6 to 6
- decay_rate: float32 [32], P('exp'), may hold values from 1.2207031e-06 to 0.05
- norm_gain: float32 [4096], P('exp'), may hold values from 0.1 to 1.9
- moe_rows: bfloat16 [2048, 3072], P('exp'), may hold values from -6 to 6
- tile_expert: int32 [16, 1], P('exp'), may hold values from 0 to 3; in each aligned block of 4 rows (0 to 3, 4 to 7, ...) at most 2 rows name the same one
- row_weight: float32 [2048], P('exp'), may hold values from 0.2 to 1
- w_gate: bfloat16 [4, 3072, 9216], P('exp', None, 'ctx'), may hold values from -0.109375 to 0.109375
- w_up: bfloat16 [4, 3072, 9216], P('exp', None, 'ctx'), may hold values from -0.109375 to 0.109375
- w_down: bfloat16 [4, 9216, 3072], P('exp', 'ctx'), may hold values from -0.1875 to 0.1875
Outputs:
- attention_out: bfloat16 [16384, 4096], P('ctx', 'exp')
- moe_out: bfloat16 [2048, 3072], P('exp', 'ctx')
The draws below stay inside these ranges and needn't reach their ends.
Inputs may be any that keep to these rules, and one draw needn't show every extreme that they name: `tile_expert`: among the 4 tiles of one index of exp at most 2 name the same expert, and some index has exactly 2 tiles for one expert.
All inputs are finite; a program needn't handle non-finite values.
Results may differ from the reference program's by a relative error of at most 0.0057.
Values may be sent and summed in bfloat16 or wider, within the bound.
No kernel may reach another device: no remote copies, remote signals or barrier semaphores. Data moves between devices by JAX's collectives and lax.ppermute only.
A program may use at most 128 MiB of HBM per device.

```python
import math
import jax
import jax.numpy as jnp
import numpy as np
from jax import lax

HEADS = 32
HEAD_DIM = 128
D = 3072
FFE = 9216
TILE = 128
TOK_DEV = 256
TILES_DEV = 4
CAP = 2
EXPERTS = 4
SEQ = 16384
NTILES = 16
ROWS = 2048
N_CTX = 64


def spiked(drawn, rng, source, target, parts, factor):
    owner, partner = [(jnp.arange(drawn.shape[position]) // (drawn.shape[position] // parts)).reshape([-1 if axis == position else 1 for axis in range(drawn.ndim)]) for position in (source, target)]
    chosen = jax.random.permutation(rng, parts)[partner]
    strong = (owner == chosen) | (owner == (partner + parts // 2) % parts)
    return jnp.where(strong, factor * drawn, drawn)


def block_scale(stream_key, extent, pieces, low, high):
    def one(axis_at, blocks):
        heights = jax.random.uniform(jax.random.fold_in(jax.random.fold_in(stream_key, 6), axis_at), (blocks,), jnp.float32, low / len(pieces), high / len(pieces))
        return jnp.repeat(jnp.exp(heights), extent[axis_at] // blocks).reshape((-1,) + (1,) * (len(extent) - axis_at - 1))

    factor_of = one(*pieces[0])
    for cut in pieces[1:]:
        factor_of = factor_of * one(*cut)
    return factor_of


def deal_out(key, own, number, rows, amount, top, limit, skew):
    sequence = jax.random.permutation(key, amount)
    packed, ordinary = load_shares(amount, rows * top, limit, skew, True), load_shares(amount, rows * top, limit, skew, False)
    places = jnp.arange(amount)

    def named(tallies, rotation):
        used = int((tallies > 0).sum())
        fixed = max(1, used // 4)
        moved = fixed + (places - fixed + rotation * (used - fixed)) % max(1, amount - fixed)
        return jnp.zeros((amount,), jnp.int32).at[sequence[jnp.where(places < fixed, places, moved)]].set(jnp.asarray(tallies, jnp.int32))

    tallies = jnp.where(number % 4 == 0, named(packed, number // 4), named(ordinary, number - number // 4 - 1))
    mixed = jax.random.permutation(jax.random.fold_in(own, 3), amount)
    source_of, taker = mixed[0:amount // 2 * 2:2], mixed[1:amount // 2 * 2:2]
    slack = jnp.minimum(tallies[source_of] - 1, limit - tallies[taker]) // 2
    slack = jnp.where((source_of == sequence[0]) | (taker == sequence[0]) | (tallies[taker] == 0), 0, jnp.maximum(slack, 0))
    moved = jax.random.randint(jax.random.fold_in(own, 4), (amount // 2,), 0, 1 << 20) % (slack + 1)
    tallies = tallies.at[source_of].add(-moved).at[taker].add(moved)
    items = jnp.searchsorted(jnp.cumsum(tallies), jnp.arange(rows * top), side="right").astype(jnp.int32)
    table = items.reshape(top, rows).T
    table = table[jax.random.permutation(jax.random.fold_in(own, 1), rows)]
    rotation = jax.random.randint(jax.random.fold_in(own, 2), (rows, 1), 0, top)
    return jnp.take_along_axis(table, (jnp.arange(top)[None, :] + rotation) % top, axis=1)


def load_shares(count, total, reach, slope, full):
    portions = [(1 << 20) // math.isqrt(rank ** slope) + 1 for rank in range(1, count + 1)]
    largest = reach if full else min(reach, max(-(-total // count), total * portions[0] // sum(portions)))
    least = 1 if total - largest >= count - 1 else 0
    given, rest = [largest] + [least] * (count - 1), total - largest - least * (count - 1)
    while rest > 0:
        candidates = [i for i in range(1, count) if given[i] < largest] or [i for i in range(1, count) if given[i] < reach]
        whole, left = sum([portions[i] for i in candidates]), rest
        for i in candidates:
            more = min(reach - given[i], max(1, left * portions[i] // whole), rest)
            given[i] = given[i] + more
            rest = rest - more
    return np.array(given)


def centred(own_key, extent, deviation, reach, cuts=(), kind=jnp.bfloat16):
    values = jax.random.normal(own_key, extent, jnp.float32) * deviation
    if len(cuts) > 0:
        values = block_scale(own_key, extent, cuts, -0.22, 0.18) * values
    return jnp.clip(values, min=-reach, max=reach).astype(kind)


def heavy_noise(own_key, extent, deviation, limit, split, heavy, kind=jnp.bfloat16):
    values = deviation * jax.random.normal(own_key, extent, jnp.float32)
    if split:
        values = values * block_scale(own_key, extent, split, -0.22, 0.18)
    return jnp.clip(spiked(values, jax.random.fold_in(own_key, 3), *heavy), -limit, limit).astype(kind)


def setup_inputs(seed: int = 0) -> dict:
    splits = jax.random.split(jax.random.key(seed), 13)
    queries = centred(splits[0], (SEQ, HEADS * HEAD_DIM), 1.0, 6.0, ((0, 64), (1, 4)))
    keys = centred(splits[1], (SEQ, HEADS * HEAD_DIM), 1.0, 6.0, ((0, 64), (1, 4)))
    values = centred(splits[2], (SEQ, HEADS * HEAD_DIM), 1.0, 6.0, ((0, 64), (1, 4)))
    gates = centred(splits[3], (SEQ, HEADS * HEAD_DIM), 1.5, 6.0, ((0, 64), (1, 4)))
    decay_rate = jnp.clip(jnp.exp(math.log(0.05) - 10.620351 * jax.random.uniform(splits[4], (HEADS,), jnp.float32) ** block_scale(splits[4], (HEADS,), ((0, 4),), -0.2, 0.2)), 1.220703097715159e-06, 0.05)
    norm_gain = jnp.clip(1.0 + 0.18 * jax.random.normal(splits[5], (HEADS * HEAD_DIM,), jnp.float32), 0.1, 1.9)
    moe_rows = centred(splits[6], (ROWS, D), 1.0, 6.0, ((0, 4),))
    tile_expert_keys = jax.random.split(jax.random.fold_in(splits[7], 1), NTILES // TILES_DEV)
    tile_expert_turns = jax.random.permutation(jax.random.fold_in(splits[7], 3), NTILES // TILES_DEV)
    tile_expert = jax.vmap(lambda own, number: deal_out(jax.random.fold_in(splits[7], 2), own, number, TILES_DEV, EXPERTS, 1, CAP, 2))(tile_expert_keys, tile_expert_turns).reshape((NTILES, 1))
    row_weight = jnp.clip(0.2 + 0.8 * jax.random.uniform(splits[8], (ROWS,), jnp.float32) ** block_scale(splits[8], (ROWS,), ((0, 4),), -0.2, 0.2), 0.2, 1.0)
    w_gate = centred(splits[9], (EXPERTS, D, FFE), D ** -0.5, 0.109375, ((0, 4), (2, 64)))
    w_up = centred(splits[10], (EXPERTS, D, FFE), D ** -0.5, 0.109375, ((0, 4), (2, 64)))
    w_down = heavy_noise(splits[11], (EXPERTS, FFE, D), FFE ** -0.5, 0.1875, ((0, 4), (1, 64)), (1, 2, 64, 4.0))
    return dict(queries=queries, keys=keys, values=values, gates=gates, decay_rate=decay_rate, norm_gain=norm_gain, moe_rows=moe_rows, tile_expert=tile_expert, row_weight=row_weight, w_gate=w_gate, w_up=w_up, w_down=w_down)


def attention_part(queries, keys, values, gates, decay_rate, norm_gain):
    positions = jnp.arange(TOK_DEV, dtype=jnp.float32)
    offsets = positions[:, None] - positions[None, :]
    within = jnp.exp(-decay_rate[:, None, None] * jnp.maximum(offsets, 0.0)[None])
    within = jnp.where((offsets >= 0.0)[None], within, 0.0)
    query_decay = jnp.exp(-decay_rate[None, :] * positions[:, None])
    key_decay = jnp.exp(-decay_rate[None, :] * (TOK_DEV - positions)[:, None])
    block_decay = jnp.exp(-decay_rate * TOK_DEV)
    shape_blocks = (N_CTX, TOK_DEV, HEADS, HEAD_DIM)
    query_blocks = queries.reshape(shape_blocks)
    key_blocks = keys.reshape(shape_blocks)
    value_blocks = values.reshape(shape_blocks)

    def one_block(prefix, block):
        query_heads, key_heads, value_heads = block
        query_wide = query_heads.astype(jnp.float32)
        key_wide = key_heads.astype(jnp.float32)
        value_wide = value_heads.astype(jnp.float32)
        scores = (jnp.einsum('the,she->hts', query_wide, key_wide) * within).astype(jnp.bfloat16)
        intra = jnp.einsum('hts,she->the', scores.astype(jnp.float32), value_wide)
        prefix_low = prefix.astype(jnp.bfloat16).astype(jnp.float32)
        inter = jnp.einsum('the,hef->thf', query_wide, prefix_low) * query_decay[:, :, None]
        key_scaled = (key_wide * key_decay[:, :, None]).astype(jnp.bfloat16)
        local_state = jnp.einsum('the,thf->hef', key_scaled.astype(jnp.float32), value_wide)
        next_prefix = prefix * block_decay[:, None, None] + local_state
        return (next_prefix, intra + inter)
    start_state = jnp.zeros((HEADS, HEAD_DIM, HEAD_DIM), jnp.float32)
    final_state, mixed = lax.scan(one_block, start_state, (query_blocks, key_blocks, value_blocks))
    mixed = mixed.reshape(SEQ, HEADS * HEAD_DIM)
    mean_square = lax.optimization_barrier(jnp.mean(mixed * mixed, axis=1))
    scaled = mixed * lax.rsqrt(mean_square + 1e-06)[:, None] * norm_gain[None, :]
    return (scaled * jax.nn.sigmoid(gates.astype(jnp.float32))).astype(jnp.bfloat16)

def expert_part(moe_rows, tile_expert, row_weight, w_gate, w_up, w_down):
    row_tiles = moe_rows.reshape(NTILES, TILE, D)
    tile_ids = tile_expert[:, 0].astype(jnp.int32)

    def one_tile(pair):
        rows, which = pair
        gate_matrix = lax.dynamic_index_in_dim(w_gate, which, 0, keepdims=False)
        up_matrix = lax.dynamic_index_in_dim(w_up, which, 0, keepdims=False)
        down_matrix = lax.dynamic_index_in_dim(w_down, which, 0, keepdims=False)
        gate_part = jnp.dot(rows, gate_matrix, preferred_element_type=jnp.float32)
        up_part = jnp.dot(rows, up_matrix, preferred_element_type=jnp.float32)
        hidden = (jax.nn.silu(gate_part) * up_part).astype(jnp.bfloat16)
        return jnp.dot(hidden, down_matrix, preferred_element_type=jnp.float32).astype(jnp.bfloat16)
    expert_out = lax.map(one_tile, (row_tiles, tile_ids))
    expert_out = lax.optimization_barrier(expert_out)
    weighted = expert_out.astype(jnp.float32) * row_weight.reshape(NTILES, TILE)[:, :, None]
    return weighted.astype(jnp.bfloat16).reshape(ROWS, D)

def reference(queries, keys, values, gates, decay_rate, norm_gain, moe_rows, tile_expert, row_weight, w_gate, w_up, w_down):
    attention_out = attention_part(queries, keys, values, gates, decay_rate, norm_gain)
    moe_out = expert_part(moe_rows, tile_expert, row_weight, w_gate, w_up, w_down)
    return (attention_out, moe_out)
```

```python
import jax
import jax.numpy as jnp
from jax import lax
from jax.experimental import pallas as pl
from jax.experimental.pallas import tpu as pltpu
from jax.sharding import Mesh
from jax.sharding import PartitionSpec as P

BF = jnp.bfloat16
F32 = jnp.float32
CTX = ("z", "x", "core")
HEAD = 128
TILE = 128


def _state_kernel(rate, k, v, out):
    tokens = k.shape[0]
    r = rate[pl.program_id(0)]
    t = lax.broadcasted_iota(jnp.int32, (tokens, HEAD), 0).astype(F32)
    scaled = (k[...].astype(F32) * jnp.exp(-r * (tokens - t))).astype(BF)
    out[...] = lax.dot_general(
        scaled, v[...], (((0,), (0,)), ((), ())), preferred_element_type=F32
    ).astype(BF)


def local_states(rate, keys, values):
    tokens, width = keys.shape
    heads = width // HEAD
    return pl.pallas_call(
        _state_kernel,
        grid=(heads,),
        in_specs=[
            pl.BlockSpec(memory_space=pltpu.SMEM),
            pl.BlockSpec((tokens, HEAD), lambda h: (0, h)),
            pl.BlockSpec((tokens, HEAD), lambda h: (0, h)),
        ],
        out_specs=pl.BlockSpec((HEAD, HEAD), lambda h: (h, 0)),
        out_shape=jax.ShapeDtypeStruct((width, HEAD), BF),
        name="local_states",
    )(rate, keys, values)


def _scan_kernel(decay, states, out):
    lam = decay[0]
    blocks = states.shape[0]
    carry = jnp.zeros(states.shape[1:], F32)
    for b in range(blocks):
        out[b] = carry.astype(BF)
        carry = carry * lam + states[b].astype(F32)


def scan_states(decay, states):
    return pl.pallas_call(
        _scan_kernel,
        in_specs=[
            pl.BlockSpec(memory_space=pltpu.SMEM),
            pl.BlockSpec(memory_space=pltpu.VMEM),
        ],
        out_specs=pl.BlockSpec(memory_space=pltpu.VMEM),
        out_shape=jax.ShapeDtypeStruct(states.shape, BF),
        name="scan_states",
    )(decay, states)


def _intra_kernel(rate, q, k, v, out):
    tokens = q.shape[0]
    r = rate[pl.program_id(0)]
    i = lax.broadcasted_iota(jnp.int32, (tokens, tokens), 0)
    j = lax.broadcasted_iota(jnp.int32, (tokens, tokens), 1)
    off = (i - j).astype(F32)
    within = jnp.where(off >= 0.0, jnp.exp(-r * jnp.maximum(off, 0.0)), 0.0)
    scores = lax.dot_general(
        q[...], k[...], (((1,), (1,)), ((), ())), preferred_element_type=F32
    )
    out[...] = jnp.dot(
        (scores * within).astype(BF), v[...], preferred_element_type=F32
    )


def intra_part(rate, queries, keys, values):
    tokens, width = keys.shape
    heads = width // HEAD
    spec = pl.BlockSpec((tokens, HEAD), lambda h: (0, h))
    return pl.pallas_call(
        _intra_kernel,
        grid=(heads,),
        in_specs=[pl.BlockSpec(memory_space=pltpu.SMEM), spec, spec, spec],
        out_specs=spec,
        out_shape=jax.ShapeDtypeStruct((tokens, width), F32),
        name="intra_part",
    )(rate, queries, keys, values)


def _mix_kernel(rate, intra, q, prefix, mixed, squares):
    tokens = q.shape[0]
    h = pl.program_id(0)
    r = rate[h]
    t = lax.broadcasted_iota(jnp.int32, (tokens, HEAD), 0).astype(F32)
    inter = jnp.dot(q[...], prefix[...], preferred_element_type=F32)
    value = intra[...] + inter * jnp.exp(-r * t)
    mixed[...] = value

    @pl.when(h == 0)
    def _():
        squares[...] = jnp.zeros_like(squares)

    squares[...] += jnp.sum(jnp.transpose(value * value), axis=0, keepdims=True)


def mix_part(rate, intra, queries, prefix):
    tokens, width = queries.shape
    heads = width // HEAD
    spec = pl.BlockSpec((tokens, HEAD), lambda h: (0, h))
    return pl.pallas_call(
        _mix_kernel,
        grid=(heads,),
        in_specs=[
            pl.BlockSpec(memory_space=pltpu.SMEM),
            spec,
            spec,
            pl.BlockSpec((HEAD, HEAD), lambda h: (h, 0)),
        ],
        out_specs=[spec, pl.BlockSpec((1, tokens), lambda h: (0, 0))],
        out_shape=[
            jax.ShapeDtypeStruct((tokens, width), F32),
            jax.ShapeDtypeStruct((1, tokens), F32),
        ],
        name="mix_part",
    )(rate, intra, queries, prefix)


def _norm_kernel(features, total, mixed, gain, gates, out):
    tokens = mixed.shape[0]
    factor = lax.rsqrt(total[...] / features + 1e-06)
    column = jnp.transpose(jnp.broadcast_to(factor, (HEAD, tokens)))
    scaled = mixed[...] * column * gain[...]
    out[...] = (scaled * jax.nn.sigmoid(gates[...].astype(F32))).astype(BF)


def norm_part(features, total, mixed, gain, gates):
    tokens, width = mixed.shape
    heads = width // HEAD
    spec = pl.BlockSpec((tokens, HEAD), lambda h: (0, h))

    def kernel(*refs):
        _norm_kernel(features, *refs)

    return pl.pallas_call(
        kernel,
        grid=(heads,),
        in_specs=[
            pl.BlockSpec((1, tokens), lambda h: (0, 0)),
            spec,
            pl.BlockSpec((1, HEAD), lambda h: (0, h)),
            spec,
        ],
        out_specs=spec,
        out_shape=jax.ShapeDtypeStruct((tokens, width), BF),
        name="norm_part",
    )(total, mixed, gain, gates)


def shift(array, axis, by):
    n = lax.axis_size(axis)
    return lax.ppermute(array, axis, [(i, (i + by) % n) for i in range(n)])


def on_device(
    queries, keys, values, gates, decay_rate, norm_gain,
    moe_rows, tile_expert, row_weight, w_gate, w_up, w_down,
):
    n_exp, n_z = lax.axis_size("exp"), lax.axis_size("z")
    n_x, n_core = lax.axis_size("x"), lax.axis_size("core")
    n_ctx = n_z * n_x * n_core
    me_e, me_core = lax.axis_index("exp"), lax.axis_index("core")
    tokens, width = queries.shape
    heads = width // HEAD
    model = moe_rows.shape[1]
    tiles = tile_expert.shape[0]

    ids = tile_expert[:, 0]
    order = jnp.arange(tiles)
    earlier = (ids[None, :] == ids[:, None]) & (order[None, :] < order[:, None])
    ranks = jnp.sum(earlier.astype(jnp.int32), axis=1)

    arrived = []
    for k in range(n_exp):
        target = lax.rem(me_e + k, n_exp)
        hit = (ids == target) & (ranks == me_core)
        tile = jnp.sum(jnp.where(hit, order, 0))
        rows = lax.dynamic_slice(moe_rows, (tile * TILE, 0), (TILE, model))
        arrived.append(shift(rows, "exp", k) if k else rows)

    states = local_states(decay_rate, keys, values)
    pieces = states.reshape(n_ctx, width // n_ctx, HEAD)
    pieces = lax.all_to_all(pieces, CTX, 0, 0, tiled=True)
    mine = lax.axis_index(CTX) * (width // n_ctx) // HEAD
    lam = jnp.exp(-decay_rate * tokens)
    pieces = scan_states(lax.dynamic_slice(lam, (mine,), (1,)), pieces)
    prefix = lax.all_to_all(pieces, CTX, 0, 0, tiled=True).reshape(width, HEAD)
    intra = intra_part(decay_rate, queries, keys, values)
    mixed, squares = mix_part(decay_rate, intra, queries, prefix)
    total = lax.psum(squares, "exp")
    attention_out = norm_part(
        float(width * n_exp), total, mixed, norm_gain[None, :], gates
    )

    gate_own = jnp.swapaxes(w_gate[0], 0, 1)
    up_own = jnp.swapaxes(w_up[0], 0, 1)
    gate_other = shift(gate_own, "core", 1)
    up_other = shift(up_own, "core", 1)
    units = gate_own.shape[0]
    chunk = model // n_z
    down_own = jnp.swapaxes(w_down[0].reshape(units, n_z, chunk), 0, 1)
    down_own = lax.all_to_all(down_own, "z", 0, 0, tiled=True)
    down_other = shift(down_own, "core", 1)
    down = jnp.stack([down_own, down_other], axis=1)

    inner = jnp.concatenate([gate_own, gate_other, up_own, up_other], axis=0)
    hidden = []
    for rows in arrived:
        both = lax.dot_general(
            inner, rows, (((1,), (1,)), ((), ())), preferred_element_type=F32
        )
        half = jax.nn.silu(both[: 2 * units]) * both[2 * units :]
        hidden.append(half.astype(BF))
    turned = [hidden[(-m) % n_exp] for m in range(n_exp)]
    twice = jnp.concatenate(turned + turned, axis=1)
    rows_here = n_exp * TILE
    hidden = lax.dynamic_slice(
        twice, (0, (n_exp - me_e) * TILE), (2 * units, rows_here)
    )
    hidden = lax.all_gather(hidden, "z").reshape(n_z, 2, units, rows_here)
    partial = lax.dot_general(
        down.reshape(n_z * 2 * units, chunk),
        hidden.reshape(n_z * 2 * units, rows_here),
        (((0,), (0,)), ((), ())),
        preferred_element_type=F32,
    ).astype(BF)
    columns = chunk // (n_x * n_core)
    parts = partial.reshape(n_x * n_core, columns, n_exp, TILE)
    parts = jnp.swapaxes(parts, 1, 2).reshape(-1, columns, TILE)
    parts = lax.all_to_all(parts, ("x", "core", "exp"), 0, 0, tiled=True)
    parts = parts.reshape(n_x, n_core * n_exp, columns, TILE)
    summed = jnp.sum(parts.astype(F32), axis=0).astype(BF)
    summed = lax.optimization_barrier(summed)
    picked = []
    for t in range(tiles):
        slot = ranks[t] * n_exp + ids[t]
        tile = lax.dynamic_index_in_dim(summed, slot, 0, keepdims=False)
        weight = row_weight[t * TILE : (t + 1) * TILE]
        picked.append((tile.astype(F32) * weight[None, :]).astype(BF))
    moe_out = jnp.swapaxes(jnp.concatenate(picked, axis=1), 0, 1)
    return attention_out, moe_out


def solution(mesh):
    n_core, n_x = 2, 4
    grid = mesh.devices.reshape(-1, n_x, n_core, mesh.devices.shape[1])
    fine = Mesh(grid, ("z", "x", "core", "exp"))
    placed = (
        P(CTX, "exp"),
        P(CTX, "exp"),
        P(CTX, "exp"),
        P(CTX, "exp"),
        P("exp"),
        P("exp"),
        P("exp", None),
        P("exp", None),
        P("exp"),
        P("exp", None, CTX),
        P("exp", None, CTX),
        P("exp", CTX, None),
    )
    return jax.shard_map(
        on_device,
        mesh=fine,
        in_specs=placed,
        out_specs=(P(CTX, "exp"), P("exp", CTX)),
        check_vma=False,
    )
```

```python
import jax
import jax.numpy as jnp
from jax import lax
from jax.experimental import pallas as pl
from jax.experimental.pallas import tpu as pltpu
from jax.sharding import Mesh
from jax.sharding import PartitionSpec as P

BF = jnp.bfloat16
F32 = jnp.float32
CTX = ("z", "x", "core")
HEAD = 128
TILE = 128
GROUP = 4


def _state_kernel(rate, k, v, out):
    tokens = k.shape[0]
    first = pl.program_id(0) * GROUP
    t = lax.broadcasted_iota(jnp.int32, (tokens, HEAD), 0).astype(F32)
    for h in range(GROUP):
        at = slice(h * HEAD, (h + 1) * HEAD)
        decay = jnp.exp(-rate[first + h] * (tokens - t))
        scaled = (k[:, at].astype(F32) * decay).astype(BF)
        out[at, :] = lax.dot_general(
            scaled, v[:, at], (((0,), (0,)), ((), ())), preferred_element_type=F32
        ).astype(BF)


def local_states(rate, keys, values):
    tokens, width = keys.shape
    spec = pl.BlockSpec((tokens, GROUP * HEAD), lambda h: (0, h))
    return pl.pallas_call(
        _state_kernel,
        grid=(width // (GROUP * HEAD),),
        in_specs=[pl.BlockSpec(memory_space=pltpu.SMEM), spec, spec],
        out_specs=pl.BlockSpec((GROUP * HEAD, HEAD), lambda h: (h, 0)),
        out_shape=jax.ShapeDtypeStruct((width, HEAD), BF),
        name="local_states",
    )(rate, keys, values)


def _scan_kernel(decay, states, out):
    lam = decay[0]
    blocks = states.shape[0]
    carry = jnp.zeros(states.shape[1:], F32)
    for b in range(blocks):
        out[b] = carry.astype(BF)
        carry = carry * lam + states[b].astype(F32)


def scan_states(decay, states):
    return pl.pallas_call(
        _scan_kernel,
        in_specs=[
            pl.BlockSpec(memory_space=pltpu.SMEM),
            pl.BlockSpec(memory_space=pltpu.VMEM),
        ],
        out_specs=pl.BlockSpec(memory_space=pltpu.VMEM),
        out_shape=jax.ShapeDtypeStruct(states.shape, BF),
        name="scan_states",
    )(decay, states)


def _intra_kernel(rate, q, k, v, out):
    tokens = q.shape[0]
    first = pl.program_id(0) * GROUP
    i = lax.broadcasted_iota(jnp.int32, (tokens, tokens), 0)
    j = lax.broadcasted_iota(jnp.int32, (tokens, tokens), 1)
    off = (i - j).astype(F32)
    for h in range(GROUP):
        at = slice(h * HEAD, (h + 1) * HEAD)
        r = rate[first + h]
        within = jnp.where(off >= 0.0, jnp.exp(-r * jnp.maximum(off, 0.0)), 0.0)
        scores = lax.dot_general(
            q[:, at], k[:, at], (((1,), (1,)), ((), ())), preferred_element_type=F32
        )
        out[:, at] = jnp.dot(
            (scores * within).astype(BF), v[:, at], preferred_element_type=F32
        )


def intra_part(rate, queries, keys, values):
    tokens, width = keys.shape
    spec = pl.BlockSpec((tokens, GROUP * HEAD), lambda h: (0, h))
    return pl.pallas_call(
        _intra_kernel,
        grid=(width // (GROUP * HEAD),),
        in_specs=[pl.BlockSpec(memory_space=pltpu.SMEM), spec, spec, spec],
        out_specs=spec,
        out_shape=jax.ShapeDtypeStruct((tokens, width), F32),
        name="intra_part",
    )(rate, queries, keys, values)


def _mix_kernel(rate, intra, q, prefix, mixed, squares):
    tokens = q.shape[0]
    step = pl.program_id(0)
    t = lax.broadcasted_iota(jnp.int32, (tokens, HEAD), 0).astype(F32)
    total = jnp.zeros((tokens, HEAD), F32)
    for h in range(GROUP):
        at = slice(h * HEAD, (h + 1) * HEAD)
        r = rate[step * GROUP + h]
        inter = jnp.dot(q[:, at], prefix[at, :], preferred_element_type=F32)
        value = intra[:, at] + inter * jnp.exp(-r * t)
        mixed[:, at] = value
        total += value * value

    @pl.when(step == 0)
    def _():
        squares[...] = jnp.zeros_like(squares)

    squares[...] += jnp.sum(jnp.transpose(total), axis=0, keepdims=True)


def mix_part(rate, intra, queries, prefix):
    tokens, width = queries.shape
    spec = pl.BlockSpec((tokens, GROUP * HEAD), lambda h: (0, h))
    return pl.pallas_call(
        _mix_kernel,
        grid=(width // (GROUP * HEAD),),
        in_specs=[
            pl.BlockSpec(memory_space=pltpu.SMEM),
            spec,
            spec,
            pl.BlockSpec((GROUP * HEAD, HEAD), lambda h: (h, 0)),
        ],
        out_specs=[spec, pl.BlockSpec((1, tokens), lambda h: (0, 0))],
        out_shape=[
            jax.ShapeDtypeStruct((tokens, width), F32),
            jax.ShapeDtypeStruct((1, tokens), F32),
        ],
        name="mix_part",
    )(rate, intra, queries, prefix)


def _norm_kernel(features, total, mixed, gain, gates, out):
    tokens = mixed.shape[0]
    factor = lax.rsqrt(total[...] / features + 1e-06)
    column = jnp.transpose(jnp.broadcast_to(factor, (HEAD, tokens)))
    for h in range(GROUP):
        at = slice(h * HEAD, (h + 1) * HEAD)
        scaled = mixed[:, at] * column * gain[:, at]
        out[:, at] = (scaled * jax.nn.sigmoid(gates[:, at].astype(F32))).astype(BF)


def norm_part(features, total, mixed, gain, gates):
    tokens, width = mixed.shape
    spec = pl.BlockSpec((tokens, GROUP * HEAD), lambda h: (0, h))

    def kernel(*refs):
        _norm_kernel(features, *refs)

    return pl.pallas_call(
        kernel,
        grid=(width // (GROUP * HEAD),),
        in_specs=[
            pl.BlockSpec((1, tokens), lambda h: (0, 0)),
            spec,
            pl.BlockSpec((1, GROUP * HEAD), lambda h: (0, h)),
            spec,
        ],
        out_specs=spec,
        out_shape=jax.ShapeDtypeStruct((tokens, width), BF),
        name="norm_part",
    )(total, mixed, gain, gates)


def _pick_kernel(ids, place, rows, *refs):
    outs, sems = refs[:-1], refs[-1]
    tiles = ids.shape[0]
    n_exp = len(outs)
    me_e, me_core = place[0], place[1]
    copies = []
    for k in range(n_exp):
        target = lax.rem(me_e + k, n_exp)
        tile, rank = jnp.int32(0), jnp.int32(0)
        for t in range(tiles):
            same = ids[t, 0] == target
            tile = jnp.where(same & (rank == me_core), t, tile)
            rank = rank + same.astype(jnp.int32)
        start = pl.multiple_of(tile * TILE, TILE)
        copy = pltpu.make_async_copy(
            rows.at[pl.ds(start, TILE), :], outs[k], sems.at[k]
        )
        copy.start()
        copies.append(copy)
    for copy in copies:
        copy.wait()


def pick_tiles(ids, place, rows, n_exp):
    tile = jax.ShapeDtypeStruct((TILE, rows.shape[1]), rows.dtype)
    return pl.pallas_call(
        _pick_kernel,
        in_specs=[
            pl.BlockSpec(memory_space=pltpu.SMEM),
            pl.BlockSpec(memory_space=pltpu.SMEM),
            pl.BlockSpec(memory_space=pl.ANY),
        ],
        out_specs=[pl.BlockSpec(memory_space=pl.ANY)] * n_exp,
        out_shape=[tile] * n_exp,
        scratch_shapes=[pltpu.SemaphoreType.DMA((n_exp,))],
        name="pick_tiles",
    )(ids, place, rows)


def shift(array, axis, by):
    n = lax.axis_size(axis)
    return lax.ppermute(array, axis, [(i, (i + by) % n) for i in range(n)])


def on_device(
    queries, keys, values, gates, decay_rate, norm_gain,
    moe_rows, tile_expert, row_weight, w_gate, w_up, w_down,
):
    n_exp, n_z = lax.axis_size("exp"), lax.axis_size("z")
    n_x, n_core = lax.axis_size("x"), lax.axis_size("core")
    n_ctx = n_z * n_x * n_core
    me_e, me_core = lax.axis_index("exp"), lax.axis_index("core")
    tokens, width = queries.shape
    heads = width // HEAD
    model = moe_rows.shape[1]
    tiles = tile_expert.shape[0]

    ids = tile_expert[:, 0]
    order = jnp.arange(tiles)
    earlier = (ids[None, :] == ids[:, None]) & (order[None, :] < order[:, None])
    ranks = jnp.sum(earlier.astype(jnp.int32), axis=1)

    place = jnp.stack([me_e, me_core]).astype(jnp.int32)
    picked = pick_tiles(tile_expert, place, moe_rows, n_exp)
    arrived = [shift(rows, "exp", k) if k else rows for k, rows in enumerate(picked)]

    gate_own = jnp.swapaxes(w_gate[0], 0, 1)
    up_own = jnp.swapaxes(w_up[0], 0, 1)
    gate_other = shift(gate_own, "core", 1)
    up_other = shift(up_own, "core", 1)
    units = gate_own.shape[0]
    chunk = model // n_x
    columns = model // n_ctx
    gate_other, up_other, w_down, keys_late = lax.optimization_barrier(
        (gate_other, up_other, w_down, keys)
    )

    states = local_states(decay_rate, keys_late, values)
    pieces = states.reshape(n_ctx, width // n_ctx, HEAD)
    pieces = lax.all_to_all(pieces, CTX, 0, 0, tiled=True)
    mine = lax.axis_index(CTX) * (width // n_ctx) // HEAD
    lam = jnp.exp(-decay_rate * tokens)
    pieces = scan_states(lax.dynamic_slice(lam, (mine,), (1,)), pieces)
    prefix = lax.all_to_all(pieces, CTX, 0, 0, tiled=True).reshape(width, HEAD)
    intra = intra_part(decay_rate, queries, keys, values)
    split = w_down[0].reshape(units, n_z, n_x, n_core * columns)
    split = jnp.transpose(split, (2, 0, 1, 3)).reshape(n_x, units, chunk)
    me_x = lax.axis_index("x")
    down_own = jnp.zeros((n_x, units, chunk), BF)
    for k in range(n_x):
        part = lax.dynamic_index_in_dim(split, lax.rem(me_x + k, n_x), 0)
        part = shift(part, "x", k) if k else part
        source = lax.rem(me_x + n_x - k, n_x)
        down_own = lax.dynamic_update_slice(down_own, part, (source, 0, 0))
    down_other = shift(down_own, "core", 1)
    down = jnp.stack([down_own, down_other], axis=1)

    inner = jnp.concatenate([gate_own, gate_other, up_own, up_other], axis=0)
    arrived[1], down, intra = lax.optimization_barrier((arrived[1], down, intra))
    hidden = []
    for rows in arrived:
        both = lax.dot_general(
            inner, rows, (((1,), (1,)), ((), ())), preferred_element_type=F32
        )
        half = jax.nn.silu(both[: 2 * units]) * both[2 * units :]
        hidden.append(half.astype(BF))
    turned = [hidden[(-m) % n_exp] for m in range(n_exp)]
    twice = jnp.concatenate(turned + turned, axis=1)
    rows_here = n_exp * TILE
    hidden = lax.dynamic_slice(
        twice, (0, (n_exp - me_e) * TILE), (2 * units, rows_here)
    )
    hidden = lax.all_gather(hidden, "x")
    partial = lax.dot_general(
        down.reshape(n_x * 2 * units, chunk),
        hidden.reshape(n_x * 2 * units, rows_here),
        (((0,), (0,)), ((), ())),
        preferred_element_type=F32,
    ).astype(BF)
    parts = partial.reshape(n_z * n_core, columns, n_exp, TILE)
    parts = jnp.swapaxes(parts, 1, 2).reshape(-1, columns, TILE)
    parts, prefix = lax.optimization_barrier((parts, prefix))
    parts = lax.all_to_all(parts, ("z", "core", "exp"), 0, 0, tiled=True)
    mixed, squares = mix_part(decay_rate, intra, queries, prefix)
    total = lax.psum(squares, "exp")
    attention_out = norm_part(
        float(width * n_exp), total, mixed, norm_gain[None, :], gates
    )
    parts = parts.reshape(n_z, n_core * n_exp, columns, TILE)
    summed = jnp.sum(parts.astype(F32), axis=0).astype(BF)
    summed = lax.optimization_barrier(summed)
    picked = []
    for t in range(tiles):
        slot = ranks[t] * n_exp + ids[t]
        tile = lax.dynamic_index_in_dim(summed, slot, 0, keepdims=False)
        weight = row_weight[t * TILE : (t + 1) * TILE]
        picked.append((tile.astype(F32) * weight[None, :]).astype(BF))
    moe_out = jnp.swapaxes(jnp.concatenate(picked, axis=1), 0, 1)
    return attention_out, moe_out


def solution(mesh):
    n_core, n_x = 2, 4
    grid = mesh.devices.reshape(-1, n_x, n_core, mesh.devices.shape[1])
    fine = Mesh(grid, ("z", "x", "core", "exp"))
    placed = (
        P(CTX, "exp"),
        P(CTX, "exp"),
        P(CTX, "exp"),
        P(CTX, "exp"),
        P("exp"),
        P("exp"),
        P("exp", None),
        P("exp", None),
        P("exp"),
        P("exp", None, CTX),
        P("exp", None, CTX),
        P("exp", CTX, None),
    )
    return jax.shard_map(
        on_device,
        mesh=fine,
        in_specs=placed,
        out_specs=(P(CTX, "exp"), P("exp", CTX)),
        check_vma=False,
    )
```

```python
import jax
import jax.numpy as jnp
from jax import lax
from jax.experimental import pallas as pl
from jax.experimental.pallas import tpu as pltpu
from jax.sharding import Mesh
from jax.sharding import PartitionSpec as P

BF = jnp.bfloat16
F32 = jnp.float32
CTX = ("z", "x", "core")
HEAD = 128
TILE = 128
GROUP = 4


def _state_kernel(rate, k, v, out):
    tokens = k.shape[0]
    first = pl.program_id(0) * GROUP
    t = lax.broadcasted_iota(jnp.int32, (tokens, HEAD), 0).astype(F32)
    for h in range(GROUP):
        at = slice(h * HEAD, (h + 1) * HEAD)
        decay = jnp.exp(-rate[first + h] * (tokens - t))
        scaled = (k[:, at].astype(F32) * decay).astype(BF)
        out[at, :] = lax.dot_general(
            scaled, v[:, at], (((0,), (0,)), ((), ())), preferred_element_type=F32
        ).astype(BF)


def local_states(rate, keys, values):
    tokens, width = keys.shape
    spec = pl.BlockSpec((tokens, GROUP * HEAD), lambda h: (0, h))
    return pl.pallas_call(
        _state_kernel,
        grid=(width // (GROUP * HEAD),),
        in_specs=[pl.BlockSpec(memory_space=pltpu.SMEM), spec, spec],
        out_specs=pl.BlockSpec((GROUP * HEAD, HEAD), lambda h: (h, 0)),
        out_shape=jax.ShapeDtypeStruct((width, HEAD), BF),
        name="local_states",
    )(rate, keys, values)


def _scan_kernel(decay, states, out):
    lam = decay[0]
    blocks = states.shape[0]
    carry = jnp.zeros(states.shape[1:], F32)
    for b in range(blocks):
        out[b] = carry.astype(BF)
        carry = carry * lam + states[b].astype(F32)


def scan_states(decay, states):
    return pl.pallas_call(
        _scan_kernel,
        in_specs=[
            pl.BlockSpec(memory_space=pltpu.SMEM),
            pl.BlockSpec(memory_space=pltpu.VMEM),
        ],
        out_specs=pl.BlockSpec(memory_space=pltpu.VMEM),
        out_shape=jax.ShapeDtypeStruct(states.shape, BF),
        name="scan_states",
    )(decay, states)


def _intra_kernel(rate, q, k, v, out):
    tokens = q.shape[0]
    first = pl.program_id(0) * GROUP
    i = lax.broadcasted_iota(jnp.int32, (tokens, tokens), 0)
    j = lax.broadcasted_iota(jnp.int32, (tokens, tokens), 1)
    off = (i - j).astype(F32)
    for h in range(GROUP):
        at = slice(h * HEAD, (h + 1) * HEAD)
        r = rate[first + h]
        within = jnp.where(off >= 0.0, jnp.exp(-r * jnp.maximum(off, 0.0)), 0.0)
        scores = lax.dot_general(
            q[:, at], k[:, at], (((1,), (1,)), ((), ())), preferred_element_type=F32
        )
        out[:, at] = jnp.dot(
            (scores * within).astype(BF), v[:, at], preferred_element_type=F32
        )


def intra_part(rate, queries, keys, values):
    tokens, width = keys.shape
    spec = pl.BlockSpec((tokens, GROUP * HEAD), lambda h: (0, h))
    return pl.pallas_call(
        _intra_kernel,
        grid=(width // (GROUP * HEAD),),
        in_specs=[pl.BlockSpec(memory_space=pltpu.SMEM), spec, spec, spec],
        out_specs=spec,
        out_shape=jax.ShapeDtypeStruct((tokens, width), F32),
        name="intra_part",
    )(rate, queries, keys, values)


def _mix_kernel(rate, intra, q, prefix, mixed, squares):
    tokens = q.shape[0]
    step = pl.program_id(0)
    t = lax.broadcasted_iota(jnp.int32, (tokens, HEAD), 0).astype(F32)
    total = jnp.zeros((tokens, HEAD), F32)
    for h in range(GROUP):
        at = slice(h * HEAD, (h + 1) * HEAD)
        r = rate[step * GROUP + h]
        inter = jnp.dot(q[:, at], prefix[at, :], preferred_element_type=F32)
        value = intra[:, at] + inter * jnp.exp(-r * t)
        mixed[:, at] = value
        total += value * value

    @pl.when(step == 0)
    def _():
        squares[...] = jnp.zeros_like(squares)

    squares[...] += jnp.sum(jnp.transpose(total), axis=0, keepdims=True)


def mix_part(rate, intra, queries, prefix):
    tokens, width = queries.shape
    spec = pl.BlockSpec((tokens, GROUP * HEAD), lambda h: (0, h))
    return pl.pallas_call(
        _mix_kernel,
        grid=(width // (GROUP * HEAD),),
        in_specs=[
            pl.BlockSpec(memory_space=pltpu.SMEM),
            spec,
            spec,
            pl.BlockSpec((GROUP * HEAD, HEAD), lambda h: (h, 0)),
        ],
        out_specs=[spec, pl.BlockSpec((1, tokens), lambda h: (0, 0))],
        out_shape=[
            jax.ShapeDtypeStruct((tokens, width), F32),
            jax.ShapeDtypeStruct((1, tokens), F32),
        ],
        name="mix_part",
    )(rate, intra, queries, prefix)


def _norm_kernel(features, total, mixed, gain, gates, out):
    tokens = mixed.shape[0]
    factor = lax.rsqrt(total[...] / features + 1e-06)
    column = jnp.transpose(jnp.broadcast_to(factor, (HEAD, tokens)))
    for h in range(GROUP):
        at = slice(h * HEAD, (h + 1) * HEAD)
        scaled = mixed[:, at] * column * gain[:, at]
        out[:, at] = (scaled * jax.nn.sigmoid(gates[:, at].astype(F32))).astype(BF)


def norm_part(features, total, mixed, gain, gates):
    tokens, width = mixed.shape
    spec = pl.BlockSpec((tokens, GROUP * HEAD), lambda h: (0, h))

    def kernel(*refs):
        _norm_kernel(features, *refs)

    return pl.pallas_call(
        kernel,
        grid=(width // (GROUP * HEAD),),
        in_specs=[
            pl.BlockSpec((1, tokens), lambda h: (0, 0)),
            spec,
            pl.BlockSpec((1, GROUP * HEAD), lambda h: (0, h)),
            spec,
        ],
        out_specs=spec,
        out_shape=jax.ShapeDtypeStruct((tokens, width), BF),
        name="norm_part",
    )(total, mixed, gain, gates)


def _pick_kernel(ids, place, rows, *refs):
    n_exp = place[2]
    outs, held, into, out_of = refs[:-3], refs[-3], refs[-2], refs[-1]
    tiles = ids.shape[0]
    loads = []
    for k in range(len(outs)):
        target = lax.rem(place[0] + k + 1, n_exp)
        tile, rank = jnp.int32(0), jnp.int32(0)
        for t in range(tiles):
            same = ids[t, 0] == target
            tile = jnp.where(same & (rank == place[1]), t, tile)
            rank = rank + same.astype(jnp.int32)
        start = pl.multiple_of(tile * TILE, TILE)
        load = pltpu.make_async_copy(
            rows.at[pl.ds(start, TILE), :], held.at[k], into.at[k]
        )
        load.start()
        loads.append(load)
    stores = []
    for k, load in enumerate(loads):
        load.wait()
        store = pltpu.make_async_copy(held.at[k], outs[k], out_of.at[k])
        store.start()
        stores.append(store)
    for store in stores:
        store.wait()


def pick_tiles(ids, place, rows, count):
    tile = jax.ShapeDtypeStruct((TILE, rows.shape[1]), rows.dtype)
    return pl.pallas_call(
        _pick_kernel,
        in_specs=[
            pl.BlockSpec(memory_space=pltpu.SMEM),
            pl.BlockSpec(memory_space=pltpu.SMEM),
            pl.BlockSpec(memory_space=pl.ANY),
        ],
        out_specs=[pl.BlockSpec(memory_space=pl.ANY)] * count,
        out_shape=[tile] * count,
        scratch_shapes=[
            pltpu.VMEM((count, TILE, rows.shape[1]), rows.dtype),
            pltpu.SemaphoreType.DMA((count,)),
            pltpu.SemaphoreType.DMA((count,)),
        ],
        name="pick_tiles",
    )(ids, place, rows)


def shift(array, axis, by):
    n = lax.axis_size(axis)
    return lax.ppermute(array, axis, [(i, (i + by) % n) for i in range(n)])


def on_device(
    queries, keys, values, gates, decay_rate, norm_gain,
    moe_rows, tile_expert, row_weight, w_gate, w_up, w_down,
):
    n_exp, n_z = lax.axis_size("exp"), lax.axis_size("z")
    n_x, n_core = lax.axis_size("x"), lax.axis_size("core")
    n_ctx = n_z * n_x * n_core
    me_e, me_core = lax.axis_index("exp"), lax.axis_index("core")
    tokens, width = queries.shape
    heads = width // HEAD
    model = moe_rows.shape[1]
    tiles = tile_expert.shape[0]

    ids = tile_expert[:, 0]
    order = jnp.arange(tiles)
    earlier = (ids[None, :] == ids[:, None]) & (order[None, :] < order[:, None])
    ranks = jnp.sum(earlier.astype(jnp.int32), axis=1)

    place = jnp.stack([me_e, me_core, n_exp]).astype(jnp.int32)
    picked = pick_tiles(tile_expert, place, moe_rows, n_exp)
    arrived = [picked[-1]]
    arrived += [shift(picked[k - 1], "exp", k) for k in range(1, n_exp)]

    gate_own = jnp.swapaxes(w_gate[0], 0, 1)
    up_own = jnp.swapaxes(w_up[0], 0, 1)
    gate_other = shift(gate_own, "core", 1)
    up_other = shift(up_own, "core", 1)
    units = gate_own.shape[0]
    chunk = model // n_x
    columns = model // n_ctx
    gate_other, up_other, w_down, keys_late = lax.optimization_barrier(
        (gate_other, up_other, w_down, keys)
    )

    states = local_states(decay_rate, keys_late, values)
    pieces = states.reshape(n_ctx, width // n_ctx, HEAD)
    pieces = lax.all_to_all(pieces, CTX, 0, 0, tiled=True)
    mine = lax.axis_index(CTX) * (width // n_ctx) // HEAD
    lam = jnp.exp(-decay_rate * tokens)
    pieces = scan_states(lax.dynamic_slice(lam, (mine,), (1,)), pieces)
    arrived[2], pieces = lax.optimization_barrier((arrived[2], pieces))
    prefix = lax.all_to_all(pieces, CTX, 0, 0, tiled=True).reshape(width, HEAD)
    intra = intra_part(decay_rate, queries, keys, values)
    split = w_down[0].reshape(units, n_z, n_x, n_core * columns)
    split = jnp.transpose(split, (2, 0, 1, 3)).reshape(n_x, units, chunk)
    me_x = lax.axis_index("x")
    down_own = jnp.zeros((n_x, units, chunk), BF)
    for k in range(n_x):
        part = lax.dynamic_index_in_dim(split, lax.rem(me_x + k, n_x), 0)
        part = shift(part, "x", k) if k else part
        source = lax.rem(me_x + n_x - k, n_x)
        down_own = lax.dynamic_update_slice(down_own, part, (source, 0, 0))
    down_other = shift(down_own, "core", 1)
    down = jnp.stack([down_own, down_other], axis=1)

    inner = jnp.concatenate([gate_own, gate_other, up_own, up_other], axis=0)
    arrived[1], down, intra = lax.optimization_barrier((arrived[1], down, intra))
    down = down.reshape(n_x * 2 * units, chunk)
    parts = jnp.zeros((n_z * n_core, n_exp, columns, TILE), BF)
    for pair in ((0, 1), (3, 2)):
        hidden = []
        for k in pair:
            both = lax.dot_general(
                inner, arrived[k], (((1,), (1,)), ((), ())), preferred_element_type=F32
            )
            half = jax.nn.silu(both[: 2 * units]) * both[2 * units :]
            hidden.append(half.astype(BF))
        hidden = lax.all_gather(jnp.concatenate(hidden, axis=1), "x")
        partial = lax.dot_general(
            down,
            hidden.reshape(n_x * 2 * units, len(pair) * TILE),
            (((0,), (0,)), ((), ())),
            preferred_element_type=F32,
        ).astype(BF)
        partial = partial.reshape(n_z * n_core, 1, columns, len(pair) * TILE)
        for i, k in enumerate(pair):
            source = lax.rem(me_e + n_exp - k, n_exp)
            parts = lax.dynamic_update_slice(
                parts, partial[..., i * TILE : (i + 1) * TILE], (0, source, 0, 0)
            )
    parts = parts.reshape(-1, columns, TILE)
    parts, prefix = lax.optimization_barrier((parts, prefix))
    parts = lax.all_to_all(parts, ("z", "core", "exp"), 0, 0, tiled=True)
    mixed, squares = mix_part(decay_rate, intra, queries, prefix)
    total = lax.psum(squares, "exp")
    attention_out = norm_part(
        float(width * n_exp), total, mixed, norm_gain[None, :], gates
    )
    parts = parts.reshape(n_z, n_core * n_exp, columns, TILE)
    summed = jnp.sum(parts.astype(F32), axis=0).astype(BF)
    summed = lax.optimization_barrier(summed)
    picked = []
    for t in range(tiles):
        slot = ranks[t] * n_exp + ids[t]
        tile = lax.dynamic_index_in_dim(summed, slot, 0, keepdims=False)
        weight = row_weight[t * TILE : (t + 1) * TILE]
        picked.append((tile.astype(F32) * weight[None, :]).astype(BF))
    moe_out = jnp.swapaxes(jnp.concatenate(picked, axis=1), 0, 1)
    return attention_out, moe_out


def solution(mesh):
    n_core, n_x = 2, 4
    grid = mesh.devices.reshape(-1, n_x, n_core, mesh.devices.shape[1])
    fine = Mesh(grid, ("z", "x", "core", "exp"))
    placed = (
        P(CTX, "exp"),
        P(CTX, "exp"),
        P(CTX, "exp"),
        P(CTX, "exp"),
        P("exp"),
        P("exp"),
        P("exp", None),
        P("exp", None),
        P("exp"),
        P("exp", None, CTX),
        P("exp", None, CTX),
        P("exp", CTX, None),
    )
    return jax.shard_map(
        on_device,
        mesh=fine,
        in_specs=placed,
        out_specs=(P(CTX, "exp"), P("exp", CTX)),
        check_vma=False,
    )
```

```python
import functools

import jax
import jax.numpy as jnp
from jax import lax
from jax.experimental import pallas as pl
from jax.experimental.pallas import tpu as pltpu
from jax.sharding import Mesh
from jax.sharding import PartitionSpec as P

BF = jnp.bfloat16
F32 = jnp.float32
CTX = ("z", "x", "core")
HEAD = 128
TILE = 128
GROUP = 4
LAST = 1


def _state_kernel(rate, k, v, out):
    tokens = k.shape[0]
    first = pl.program_id(0) * GROUP
    t = lax.broadcasted_iota(jnp.int32, (tokens, HEAD), 0).astype(F32)
    for h in range(GROUP):
        at = slice(h * HEAD, (h + 1) * HEAD)
        decay = jnp.exp(-rate[first + h] * (tokens - t))
        scaled = (k[:, at].astype(F32) * decay).astype(BF)
        out[at, :] = lax.dot_general(
            scaled, v[:, at], (((0,), (0,)), ((), ())), preferred_element_type=F32
        ).astype(BF)


def local_states(rate, keys, values):
    tokens, width = keys.shape
    spec = pl.BlockSpec((tokens, GROUP * HEAD), lambda h: (0, h))
    return pl.pallas_call(
        _state_kernel,
        grid=(width // (GROUP * HEAD),),
        in_specs=[pl.BlockSpec(memory_space=pltpu.SMEM), spec, spec],
        out_specs=pl.BlockSpec((GROUP * HEAD, HEAD), lambda h: (h, 0)),
        out_shape=jax.ShapeDtypeStruct((width, HEAD), BF),
        name="local_states",
    )(rate, keys, values)


def _scan_kernel(tokens, heads, rate, states, out):
    blocks, rows, width = states.shape
    mine = lax.axis_index(CTX) * heads // blocks
    lam = jnp.exp(jnp.full((rows, width), -rate[mine] * tokens, F32))
    carry = jnp.zeros((rows, width), F32)
    for b in range(blocks):
        out[b] = carry.astype(BF)
        carry = carry * lam + states[b].astype(F32)


def scan_states(tokens, rate, states):
    return pl.pallas_call(
        functools.partial(_scan_kernel, tokens, rate.shape[0]),
        in_specs=[
            pl.BlockSpec(memory_space=pltpu.SMEM),
            pl.BlockSpec(memory_space=pltpu.VMEM),
        ],
        out_specs=pl.BlockSpec(memory_space=pltpu.VMEM),
        out_shape=jax.ShapeDtypeStruct(states.shape, BF),
        name="scan_states",
    )(rate, states)


def _intra_kernel(rate, q, k, v, out):
    tokens = q.shape[0]
    first = pl.program_id(0) * GROUP
    i = lax.broadcasted_iota(jnp.int32, (tokens, tokens), 0)
    j = lax.broadcasted_iota(jnp.int32, (tokens, tokens), 1)
    off = (i - j).astype(F32)
    for h in range(GROUP):
        at = slice(h * HEAD, (h + 1) * HEAD)
        r = rate[first + h]
        within = jnp.where(off >= 0.0, jnp.exp(-r * jnp.maximum(off, 0.0)), 0.0)
        scores = lax.dot_general(
            q[:, at], k[:, at], (((1,), (1,)), ((), ())), preferred_element_type=F32
        )
        out[:, at] = jnp.dot(
            (scores * within).astype(BF), v[:, at], preferred_element_type=F32
        )


def intra_part(rate, queries, keys, values):
    tokens, width = keys.shape
    spec = pl.BlockSpec((tokens, GROUP * HEAD), lambda h: (0, h))
    return pl.pallas_call(
        _intra_kernel,
        grid=(width // (GROUP * HEAD),),
        in_specs=[pl.BlockSpec(memory_space=pltpu.SMEM), spec, spec, spec],
        out_specs=spec,
        out_shape=jax.ShapeDtypeStruct((tokens, width), F32),
        name="intra_part",
    )(rate, queries, keys, values)


def _mix_kernel(rate, intra, q, prefix, mixed, squares):
    tokens = q.shape[0]
    step = pl.program_id(0)
    t = lax.broadcasted_iota(jnp.int32, (tokens, HEAD), 0).astype(F32)
    total = jnp.zeros((tokens, HEAD), F32)
    for h in range(GROUP):
        at = slice(h * HEAD, (h + 1) * HEAD)
        r = rate[step * GROUP + h]
        inter = jnp.dot(q[:, at], prefix[at, :], preferred_element_type=F32)
        value = intra[:, at] + inter * jnp.exp(-r * t)
        mixed[:, at] = value
        total += value * value

    @pl.when(step == 0)
    def _():
        squares[...] = jnp.zeros_like(squares)

    squares[...] += jnp.sum(jnp.transpose(total), axis=0, keepdims=True)


def mix_part(rate, intra, queries, prefix):
    tokens, width = queries.shape
    spec = pl.BlockSpec((tokens, GROUP * HEAD), lambda h: (0, h))
    return pl.pallas_call(
        _mix_kernel,
        grid=(width // (GROUP * HEAD),),
        in_specs=[
            pl.BlockSpec(memory_space=pltpu.SMEM),
            spec,
            spec,
            pl.BlockSpec((GROUP * HEAD, HEAD), lambda h: (h, 0)),
        ],
        out_specs=[spec, pl.BlockSpec((1, tokens), lambda h: (0, 0))],
        out_shape=[
            jax.ShapeDtypeStruct((tokens, width), F32),
            jax.ShapeDtypeStruct((1, tokens), F32),
        ],
        name="mix_part",
    )(rate, intra, queries, prefix)


def _norm_kernel(features, total, mixed, gain, gates, out):
    tokens = mixed.shape[0]
    factor = lax.rsqrt(total[...] / features + 1e-06)
    column = jnp.transpose(jnp.broadcast_to(factor, (HEAD, tokens)))
    for h in range(GROUP):
        at = slice(h * HEAD, (h + 1) * HEAD)
        scaled = mixed[:, at] * column * gain[:, at]
        out[:, at] = (scaled * jax.nn.sigmoid(gates[:, at].astype(F32))).astype(BF)


def norm_part(features, total, mixed, gain, gates):
    tokens, width = mixed.shape
    spec = pl.BlockSpec((tokens, GROUP * HEAD), lambda h: (0, h))

    def kernel(*refs):
        _norm_kernel(features, *refs)

    return pl.pallas_call(
        kernel,
        grid=(width // (GROUP * HEAD),),
        in_specs=[
            pl.BlockSpec((1, tokens), lambda h: (0, 0)),
            spec,
            pl.BlockSpec((1, GROUP * HEAD), lambda h: (0, h)),
            spec,
        ],
        out_specs=spec,
        out_shape=jax.ShapeDtypeStruct((tokens, width), BF),
        name="norm_part",
    )(total, mixed, gain, gates)


def _pick_kernel(ids, rows, *refs):
    outs, held, into, out_of = refs[:-3], refs[-3], refs[-2], refs[-1]
    n_exp, me_e, me_core = lax.axis_size("exp"), lax.axis_index("exp"), lax.axis_index("core")
    tiles, half = ids.shape[0], TILE // 2
    loads = []
    for k in range(len(outs)):
        target = lax.rem(me_e + k + 1, n_exp)
        seen = jnp.int32(0)
        tile = [jnp.int32(0), jnp.int32(0)]
        for t in range(tiles):
            same = ids[t] == target
            for rank in range(2):
                tile[rank] = jnp.where(same & (seen == rank), t, tile[rank])
            seen = seen + same.astype(jnp.int32)
        for rank in range(2):
            start = pl.multiple_of(tile[rank] * TILE + me_core * half, half)
            load = pltpu.make_async_copy(
                rows.at[pl.ds(start, half), :],
                held.at[k, pl.ds(rank * half, half), :],
                into.at[k, rank],
            )
            load.start()
            loads.append(load)
    stores = []
    for k in range(len(outs)):
        loads[2 * k].wait()
        loads[2 * k + 1].wait()
        store = pltpu.make_async_copy(held.at[k], outs[k], out_of.at[k])
        store.start()
        stores.append(store)
    for store in stores:
        store.wait()


def pick_tiles(ids, rows, count):
    tile = jax.ShapeDtypeStruct((TILE, rows.shape[1]), rows.dtype)
    return pl.pallas_call(
        _pick_kernel,
        in_specs=[
            pl.BlockSpec(memory_space=pltpu.SMEM),
            pl.BlockSpec(memory_space=pl.ANY),
        ],
        out_specs=[pl.BlockSpec(memory_space=pl.ANY)] * count,
        out_shape=[tile] * count,
        scratch_shapes=[
            pltpu.VMEM((count, TILE, rows.shape[1]), rows.dtype),
            pltpu.SemaphoreType.DMA((count, 2)),
            pltpu.SemaphoreType.DMA((count,)),
        ],
        name="pick_tiles",
    )(ids, rows)


def _hidden_kernel(count, *refs):
    rows, weights = refs[:count], refs[count : count + 4]
    held, out = refs[-1], refs[-2]
    gate_own, gate_other, up_own, up_other = weights
    units = gate_own.shape[0]
    for i in range(count):
        held[i * TILE : (i + 1) * TILE, :] = rows[i][...]
    x = held[...]
    for i, (gate, up) in enumerate(((gate_own, up_own), (gate_other, up_other))):
        dims = (((1,), (1,)), ((), ()))
        g = lax.dot_general(gate[...], x, dims, preferred_element_type=F32)
        u = lax.dot_general(up[...], x, dims, preferred_element_type=F32)
        out[i * units : (i + 1) * units, :] = (jax.nn.silu(g) * u).astype(BF)


def hidden_part(rows, weights):
    count, units, model = len(rows), weights[0].shape[0], weights[0].shape[1]
    vmem = pl.BlockSpec(memory_space=pltpu.VMEM)
    return pl.pallas_call(
        functools.partial(_hidden_kernel, count),
        in_specs=[vmem] * (count + 4),
        out_specs=vmem,
        out_shape=jax.ShapeDtypeStruct((2 * units, count * TILE), BF),
        scratch_shapes=[pltpu.VMEM((count * TILE, model), BF)],
        compiler_params=pltpu.CompilerParams(vmem_limit_bytes=40 << 20),
        name="hidden_part",
    )(*rows, *weights)


def _down_kernel(groups, own, other, hidden, out):
    n_exp, me_e = lax.axis_size("exp"), lax.axis_index("exp")
    n_x = len(own)
    units = own[0].shape[0]
    blocks, columns = out.shape[0], out.shape[2]
    for slots, held in zip(groups, hidden):
        total = None
        for k in range(n_x):
            for i, part in enumerate((own[k], other[k])):
                h = held[k][i * units : (i + 1) * units, :]
                term = lax.dot_general(
                    part[...], h, (((0,), (0,)), ((), ())), preferred_element_type=F32
                )
                total = term if total is None else total + term
        total = total.astype(BF)
        for i, slot in enumerate(slots):
            home = lax.rem(me_e + n_exp - slot, n_exp)
            block = total[:, i * TILE : (i + 1) * TILE]
            out[:, home] = block.reshape(blocks, columns, TILE)


def down_part(groups, own, other, hidden, blocks, columns):
    n_x = len(own)
    n_slots = sum(len(slots) for slots in groups)
    vmem = pl.BlockSpec(memory_space=pltpu.VMEM)

    def kernel(*refs):
        held = [
            refs[n_x * (2 + g) : n_x * (3 + g)] for g in range(len(groups))
        ]
        _down_kernel(groups, refs[:n_x], refs[n_x : 2 * n_x], held, refs[-1])

    flat = [piece for held in hidden for piece in held]
    return pl.pallas_call(
        kernel,
        in_specs=[vmem] * (2 * n_x + len(flat)),
        out_specs=vmem,
        out_shape=jax.ShapeDtypeStruct((blocks, n_slots, columns, TILE), BF),
        compiler_params=pltpu.CompilerParams(vmem_limit_bytes=40 << 20),
        name="down_part",
    )(*own, *other, *flat)


def _finish_kernel(ids, parts, weight, out):
    n_z, n_core, n_exp, columns, _ = parts.shape
    tiles, half = ids.shape[0], TILE // 2
    low = lax.broadcasted_iota(jnp.int32, (columns, TILE), 1) < half
    for t in range(tiles):
        rank = jnp.int32(0)
        for earlier in range(t):
            rank = rank + (ids[earlier] == ids[t]).astype(jnp.int32)
        sums = []
        for core in range(n_core):
            total = jnp.zeros((columns, TILE), F32)
            for z in range(n_z):
                total = total + parts[z, core, ids[t]].astype(F32)
            sums.append(total.astype(BF).astype(F32))
        first, second = sums
        zero = jnp.where(low, first, pltpu.roll(second, half, 1))
        one = jnp.where(low, pltpu.roll(first, half, 1), second)
        rows = jnp.where(rank == 0, zero, one)
        at = slice(t * TILE, (t + 1) * TILE)
        out[:, at] = (rows * weight[:, at]).astype(BF)


def finish_part(ids, parts, weight):
    columns = parts.shape[3]
    vmem = pl.BlockSpec(memory_space=pltpu.VMEM)
    return pl.pallas_call(
        _finish_kernel,
        in_specs=[pl.BlockSpec(memory_space=pltpu.SMEM), vmem, vmem],
        out_specs=vmem,
        out_shape=jax.ShapeDtypeStruct((columns, weight.shape[1]), BF),
        name="finish_part",
    )(ids, parts, weight)


def shift(array, axis, by):
    n = lax.axis_size(axis)
    return lax.ppermute(array, axis, [(i, (i + by) % n) for i in range(n)])


def on_device(
    queries, keys, values, gates, decay_rate, norm_gain,
    moe_rows, tile_expert, row_weight, w_gate, w_up, w_down,
):
    n_exp, n_z = lax.axis_size("exp"), lax.axis_size("z")
    n_x, n_core = lax.axis_size("x"), lax.axis_size("core")
    n_ctx = n_z * n_x * n_core
    tokens, width = queries.shape
    model = moe_rows.shape[1]
    ids = tile_expert[:, 0]
    columns = model // n_ctx
    chunk = model // n_x

    gate_own = jnp.swapaxes(w_gate[0], 0, 1)
    up_own = jnp.swapaxes(w_up[0], 0, 1)
    gate_other = shift(gate_own, "core", 1)
    up_other = shift(up_own, "core", 1)
    units = gate_own.shape[0]

    picked = pick_tiles(ids, moe_rows, n_exp)
    arrived = [picked[-1]]
    arrived += [shift(picked[k - 1], "exp", k) for k in range(1, n_exp)]
    gate_other, up_other, w_down, keys_late = lax.optimization_barrier(
        (gate_other, up_other, w_down, keys)
    )

    states = local_states(decay_rate, keys_late, values)
    pieces = states.reshape(n_ctx, width // n_ctx, HEAD)
    pieces = lax.all_to_all(pieces, CTX, 0, 0, tiled=True)
    pieces = scan_states(float(tokens), decay_rate, pieces)
    arrived[LAST], pieces = lax.optimization_barrier((arrived[LAST], pieces))
    prefix = lax.all_to_all(pieces, CTX, 0, 0, tiled=True).reshape(width, HEAD)
    intra = intra_part(decay_rate, queries, keys, values)

    split = w_down[0].reshape(units, n_z, n_x, n_core * columns)
    split = jnp.transpose(split, (2, 0, 1, 3)).reshape(n_x, units, chunk)
    me_x = lax.axis_index("x")
    down_own, down_other = [], []
    for k in range(n_x):
        part = lax.dynamic_index_in_dim(
            split, lax.rem(me_x + k, n_x), 0, keepdims=False
        )
        part = shift(part, "x", k) if k else part
        down_own.append(part)
        down_other.append(shift(part, "core", 1))
    arrived[LAST], intra, *down_other = lax.optimization_barrier(
        (arrived[LAST], intra, *down_other)
    )

    weights = (gate_own, gate_other, up_own, up_other)
    early = [k for k in range(n_exp) if k != LAST]
    groups = [early, [LAST]]
    hidden = []
    for slots in groups:
        mine = hidden_part([arrived[k] for k in slots], weights)
        hidden.append([mine] + [shift(mine, "x", k) for k in range(1, n_x)])
    hidden[-1][0], prefix = lax.optimization_barrier((hidden[-1][0], prefix))
    parts = down_part(groups, down_own, down_other, hidden, n_z * n_core, columns)
    parts = parts.reshape(-1, columns, TILE)
    parts = lax.all_to_all(parts, ("z", "core", "exp"), 0, 0, tiled=True)
    parts = parts.reshape(n_z, n_core, n_exp, columns, TILE)

    mixed, squares = mix_part(decay_rate, intra, queries, prefix)
    total = lax.psum(squares, "exp")
    attention_out = norm_part(
        float(width * n_exp), total, mixed, norm_gain[None, :], gates
    )
    moe_out = jnp.swapaxes(finish_part(ids, parts, row_weight[None, :]), 0, 1)
    return attention_out, moe_out


def solution(mesh):
    n_core, n_x = 2, 4
    grid = mesh.devices.reshape(-1, n_x, n_core, mesh.devices.shape[1])
    fine = Mesh(grid, ("z", "x", "core", "exp"))
    placed = (
        P(CTX, "exp"),
        P(CTX, "exp"),
        P(CTX, "exp"),
        P(CTX, "exp"),
        P("exp"),
        P("exp"),
        P("exp", None),
        P("exp", None),
        P("exp"),
        P("exp", None, CTX),
        P("exp", None, CTX),
        P("exp", CTX, None),
    )
    return jax.shard_map(
        on_device,
        mesh=fine,
        in_specs=placed,
        out_specs=(P(CTX, "exp"), P("exp", CTX)),
        check_vma=False,
    )
```

```python
import functools

import jax
import jax.numpy as jnp
from jax import lax
from jax.experimental import pallas as pl
from jax.experimental.pallas import tpu as pltpu
from jax.sharding import Mesh
from jax.sharding import PartitionSpec as P

BF = jnp.bfloat16
F32 = jnp.float32
CTX = ("z", "x", "core")
HEAD = 128
TILE = 128
GROUP = 4
LAST = 1


def _state_kernel(rate, k, v, out):
    tokens = k.shape[0]
    first = pl.program_id(0) * GROUP
    t = lax.broadcasted_iota(jnp.int32, (tokens, HEAD), 0).astype(F32)
    for h in range(GROUP):
        at = slice(h * HEAD, (h + 1) * HEAD)
        decay = jnp.exp(-rate[first + h] * (tokens - t))
        scaled = (k[:, at].astype(F32) * decay).astype(BF)
        out[at, :] = lax.dot_general(
            scaled, v[:, at], (((0,), (0,)), ((), ())), preferred_element_type=F32
        ).astype(BF)


def local_states(rate, keys, values):
    tokens, width = keys.shape
    spec = pl.BlockSpec((tokens, GROUP * HEAD), lambda h: (0, h))
    return pl.pallas_call(
        _state_kernel,
        grid=(width // (GROUP * HEAD),),
        in_specs=[pl.BlockSpec(memory_space=pltpu.SMEM), spec, spec],
        out_specs=pl.BlockSpec((GROUP * HEAD, HEAD), lambda h: (h, 0)),
        out_shape=jax.ShapeDtypeStruct((width, HEAD), BF),
        compiler_params=pltpu.CompilerParams(vmem_limit_bytes=8 << 20),
        name="local_states",
    )(rate, keys, values)


def _scan_kernel(tokens, heads, rate, states, out):
    blocks, rows, width = states.shape
    mine = lax.axis_index(CTX) * heads // blocks
    lam = jnp.exp(jnp.full((rows, width), -rate[mine] * tokens, F32))
    carry = jnp.zeros((rows, width), F32)
    for b in range(blocks):
        out[b] = carry.astype(BF)
        carry = carry * lam + states[b].astype(F32)


def scan_states(tokens, rate, states):
    return pl.pallas_call(
        functools.partial(_scan_kernel, tokens, rate.shape[0]),
        in_specs=[
            pl.BlockSpec(memory_space=pltpu.SMEM),
            pl.BlockSpec(memory_space=pltpu.VMEM),
        ],
        out_specs=pl.BlockSpec(memory_space=pltpu.VMEM),
        out_shape=jax.ShapeDtypeStruct(states.shape, BF),
        compiler_params=pltpu.CompilerParams(vmem_limit_bytes=6 << 20),
        name="scan_states",
    )(rate, states)


def _intra_kernel(rate, q, k, v, out):
    tokens = q.shape[0]
    first = pl.program_id(0) * GROUP
    i = lax.broadcasted_iota(jnp.int32, (tokens, tokens), 0)
    j = lax.broadcasted_iota(jnp.int32, (tokens, tokens), 1)
    off = (i - j).astype(F32)
    for h in range(GROUP):
        at = slice(h * HEAD, (h + 1) * HEAD)
        r = rate[first + h]
        within = jnp.where(off >= 0.0, jnp.exp(-r * jnp.maximum(off, 0.0)), 0.0)
        scores = lax.dot_general(
            q[:, at], k[:, at], (((1,), (1,)), ((), ())), preferred_element_type=F32
        )
        out[:, at] = jnp.dot(
            (scores * within).astype(BF), v[:, at], preferred_element_type=F32
        )


def intra_part(rate, queries, keys, values):
    tokens, width = keys.shape
    spec = pl.BlockSpec((tokens, GROUP * HEAD), lambda h: (0, h))
    return pl.pallas_call(
        _intra_kernel,
        grid=(width // (GROUP * HEAD),),
        in_specs=[pl.BlockSpec(memory_space=pltpu.SMEM), spec, spec, spec],
        out_specs=spec,
        out_shape=jax.ShapeDtypeStruct((tokens, width), F32),
        compiler_params=pltpu.CompilerParams(vmem_limit_bytes=14 << 20),
        name="intra_part",
    )(rate, queries, keys, values)


def _mix_kernel(rate, intra, q, prefix, mixed, squares):
    tokens = q.shape[0]
    step = pl.program_id(0)
    t = lax.broadcasted_iota(jnp.int32, (tokens, HEAD), 0).astype(F32)
    total = jnp.zeros((tokens, HEAD), F32)
    for h in range(GROUP):
        at = slice(h * HEAD, (h + 1) * HEAD)
        r = rate[step * GROUP + h]
        inter = jnp.dot(q[:, at], prefix[at, :], preferred_element_type=F32)
        value = intra[:, at] + inter * jnp.exp(-r * t)
        mixed[:, at] = value
        total += value * value

    @pl.when(step == 0)
    def _():
        squares[...] = jnp.zeros_like(squares)

    squares[...] += jnp.sum(jnp.transpose(total), axis=0, keepdims=True)


def mix_part(rate, intra, queries, prefix):
    tokens, width = queries.shape
    spec = pl.BlockSpec((tokens, GROUP * HEAD), lambda h: (0, h))
    return pl.pallas_call(
        _mix_kernel,
        grid=(width // (GROUP * HEAD),),
        in_specs=[
            pl.BlockSpec(memory_space=pltpu.SMEM),
            spec,
            spec,
            pl.BlockSpec((GROUP * HEAD, HEAD), lambda h: (h, 0)),
        ],
        out_specs=[spec, pl.BlockSpec((1, tokens), lambda h: (0, 0))],
        out_shape=[
            jax.ShapeDtypeStruct((tokens, width), F32),
            jax.ShapeDtypeStruct((1, tokens), F32),
        ],
        compiler_params=pltpu.CompilerParams(vmem_limit_bytes=14 << 20),
        name="mix_part",
    )(rate, intra, queries, prefix)


def _norm_kernel(features, *refs):
    *squares, mixed, gain, gates, out = refs
    tokens = mixed.shape[0]
    total = sum((part[...] for part in squares[1:]), squares[0][...])
    factor = lax.rsqrt(total / features + 1e-06)
    column = jnp.transpose(jnp.broadcast_to(factor, (HEAD, tokens)))
    for h in range(GROUP):
        at = slice(h * HEAD, (h + 1) * HEAD)
        scaled = mixed[:, at] * column * gain[:, at]
        out[:, at] = (scaled * jax.nn.sigmoid(gates[:, at].astype(F32))).astype(BF)


def norm_part(features, squares, mixed, gain, gates):
    tokens, width = mixed.shape
    spec = pl.BlockSpec((tokens, GROUP * HEAD), lambda h: (0, h))
    row = pl.BlockSpec((1, tokens), lambda h: (0, 0))
    return pl.pallas_call(
        functools.partial(_norm_kernel, features),
        grid=(width // (GROUP * HEAD),),
        in_specs=[row] * len(squares)
        + [spec, pl.BlockSpec((1, GROUP * HEAD), lambda h: (0, h)), spec],
        out_specs=spec,
        out_shape=jax.ShapeDtypeStruct((tokens, width), BF),
        compiler_params=pltpu.CompilerParams(vmem_limit_bytes=14 << 20),
        name="norm_part",
    )(*squares, mixed, gain, gates)


def _pick_kernel(ids, rows, *refs):
    outs, held, into, out_of = refs[:-3], refs[-3], refs[-2], refs[-1]
    n_exp, me_e, me_core = lax.axis_size("exp"), lax.axis_index("exp"), lax.axis_index("core")
    tiles, half = ids.shape[0], TILE // 2
    loads = []
    for k in range(len(outs)):
        target = lax.rem(me_e + k + 1, n_exp)
        seen = jnp.int32(0)
        tile = [jnp.int32(0), jnp.int32(0)]
        for t in range(tiles):
            same = ids[t] == target
            for rank in range(2):
                tile[rank] = jnp.where(same & (seen == rank), t, tile[rank])
            seen = seen + same.astype(jnp.int32)
        for rank in range(2):
            start = pl.multiple_of(tile[rank] * TILE + me_core * half, half)
            load = pltpu.make_async_copy(
                rows.at[pl.ds(start, half), :],
                held.at[k, pl.ds(rank * half, half), :],
                into.at[k, rank],
            )
            load.start()
            loads.append(load)
    stores = []
    for k in range(len(outs)):
        loads[2 * k].wait()
        loads[2 * k + 1].wait()
        store = pltpu.make_async_copy(held.at[k], outs[k], out_of.at[k])
        store.start()
        stores.append(store)
    for store in stores:
        store.wait()


def pick_tiles(ids, rows, count):
    tile = jax.ShapeDtypeStruct((TILE, rows.shape[1]), rows.dtype)
    return pl.pallas_call(
        _pick_kernel,
        in_specs=[
            pl.BlockSpec(memory_space=pltpu.SMEM),
            pl.BlockSpec(memory_space=pl.ANY),
        ],
        out_specs=[pl.BlockSpec(memory_space=pl.ANY)] * count,
        out_shape=[tile] * count,
        scratch_shapes=[
            pltpu.VMEM((count, TILE, rows.shape[1]), rows.dtype),
            pltpu.SemaphoreType.DMA((count, 2)),
            pltpu.SemaphoreType.DMA((count,)),
        ],
        compiler_params=pltpu.CompilerParams(vmem_limit_bytes=8 << 20),
        name="pick_tiles",
    )(ids, rows)


def _hidden_kernel(count, *refs):
    rows, weights = refs[:count], refs[count : count + 4]
    held, out = refs[-1], refs[-2]
    gate_own, gate_other, up_own, up_other = weights
    units = gate_own.shape[0]
    for i in range(count):
        held[i * TILE : (i + 1) * TILE, :] = rows[i][...]
    x = held[...]
    for i, (gate, up) in enumerate(((gate_own, up_own), (gate_other, up_other))):
        dims = (((1,), (1,)), ((), ()))
        g = lax.dot_general(gate[...], x, dims, preferred_element_type=F32)
        u = lax.dot_general(up[...], x, dims, preferred_element_type=F32)
        out[i * units : (i + 1) * units, :] = (jax.nn.silu(g) * u).astype(BF)


def hidden_part(rows, weights):
    count, units, model = len(rows), weights[0].shape[0], weights[0].shape[1]
    vmem = pl.BlockSpec(memory_space=pltpu.VMEM)
    return pl.pallas_call(
        functools.partial(_hidden_kernel, count),
        in_specs=[vmem] * (count + 4),
        out_specs=vmem,
        out_shape=jax.ShapeDtypeStruct((2 * units, count * TILE), BF),
        scratch_shapes=[pltpu.VMEM((count * TILE, model), BF)],
        compiler_params=pltpu.CompilerParams(vmem_limit_bytes=24 << 20),
        name="hidden_part",
    )(*rows, *weights)


def _down_kernel(own, other, hidden, out):
    n_x = len(own)
    units = own[0].shape[0]
    blocks, slots, columns = out.shape[:3]
    wide = 2 * TILE
    for j in range(slots // 2):
        total = None
        for k in range(n_x):
            for i, part in enumerate((own[k], other[k])):
                h = hidden[k][i * units : (i + 1) * units, j * wide : (j + 1) * wide]
                term = lax.dot_general(
                    part[...], h, (((0,), (0,)), ((), ())), preferred_element_type=F32
                )
                total = term if total is None else total + term
        total = total.astype(BF)
        for i in range(2):
            block = total[:, i * TILE : (i + 1) * TILE]
            out[:, 2 * j + i] = block.reshape(blocks, columns, TILE)


def down_part(own, other, hidden, blocks, columns):
    n_x, slots = len(own), hidden[0].shape[1] // TILE
    vmem = pl.BlockSpec(memory_space=pltpu.VMEM)

    def kernel(*refs):
        _down_kernel(
            refs[:n_x], refs[n_x : 2 * n_x], refs[2 * n_x : 3 * n_x], refs[-1]
        )

    return pl.pallas_call(
        kernel,
        in_specs=[vmem] * (3 * n_x),
        out_specs=vmem,
        out_shape=jax.ShapeDtypeStruct((blocks, slots, columns, TILE), BF),
        compiler_params=pltpu.CompilerParams(vmem_limit_bytes=24 << 20),
        name="down_part",
    )(*own, *other, *hidden)


def _sum_kernel(parts, *outs):
    n_z, n_core = parts.shape[:2]
    for k, out in enumerate(outs):
        for core in range(n_core):
            total = parts[0, core, k].astype(F32)
            for z in range(1, n_z):
                total = total + parts[z, core, k].astype(F32)
            out[core] = total.astype(BF)


def sum_part(parts):
    _, n_core, slots, columns, _ = parts.shape
    vmem = pl.BlockSpec(memory_space=pltpu.VMEM)
    block = jax.ShapeDtypeStruct((n_core, columns, TILE), BF)
    return pl.pallas_call(
        _sum_kernel,
        in_specs=[vmem],
        out_specs=[vmem] * slots,
        out_shape=[block] * slots,
        compiler_params=pltpu.CompilerParams(vmem_limit_bytes=8 << 20),
        name="sum_part",
    )(parts)


def _finish_kernel(ids, *refs):
    *parts, weight, out = refs
    n_exp, me_e = lax.axis_size("exp"), lax.axis_index("exp")
    columns = out.shape[0]
    tiles, half = ids.shape[0], TILE // 2
    low = lax.broadcasted_iota(jnp.int32, (columns, TILE), 1) < half
    for t in range(tiles):
        rank = jnp.int32(0)
        for earlier in range(t):
            rank = rank + (ids[earlier] == ids[t]).astype(jnp.int32)
        slot = lax.rem(ids[t] + n_exp - me_e, n_exp)
        halves = []
        for core in range(2):
            found = parts[0][core].astype(F32)
            for k in range(1, n_exp):
                found = jnp.where(slot == k, parts[k][core].astype(F32), found)
            halves.append(found)
        first, second = halves
        zero = jnp.where(low, first, pltpu.roll(second, half, 1))
        one = jnp.where(low, pltpu.roll(first, half, 1), second)
        rows = jnp.where(rank == 0, zero, one)
        at = slice(t * TILE, (t + 1) * TILE)
        out[:, at] = (rows * weight[:, at]).astype(BF)


def finish_part(ids, parts, weight):
    columns = parts[0].shape[1]
    vmem = pl.BlockSpec(memory_space=pltpu.VMEM)
    return pl.pallas_call(
        _finish_kernel,
        in_specs=[pl.BlockSpec(memory_space=pltpu.SMEM)] + [vmem] * (len(parts) + 1),
        out_specs=vmem,
        out_shape=jax.ShapeDtypeStruct((columns, weight.shape[1]), BF),
        compiler_params=pltpu.CompilerParams(vmem_limit_bytes=6 << 20),
        name="finish_part",
    )(ids, *parts, weight)


def shift(array, axis, by):
    n = lax.axis_size(axis)
    return lax.ppermute(array, axis, [(i, (i + by) % n) for i in range(n)])


def on_device(
    queries, keys, values, gates, decay_rate, norm_gain,
    moe_rows, tile_expert, row_weight, w_gate, w_up, w_down,
):
    n_exp, n_z = lax.axis_size("exp"), lax.axis_size("z")
    n_x, n_core = lax.axis_size("x"), lax.axis_size("core")
    n_ctx = n_z * n_x * n_core
    tokens, width = queries.shape
    model = moe_rows.shape[1]
    ids = tile_expert[:, 0]
    columns = model // n_ctx
    chunk = model // n_x

    gate_own = jnp.swapaxes(w_gate[0], 0, 1)
    up_own = jnp.swapaxes(w_up[0], 0, 1)
    gate_other = shift(gate_own, "core", 1)
    up_other = shift(up_own, "core", 1)
    units = gate_own.shape[0]

    picked = pick_tiles(ids, moe_rows, n_exp)
    arrived = [picked[-1]]
    arrived += [shift(picked[k - 1], "exp", k) for k in range(1, n_exp)]
    gate_other, up_other, w_down, keys_late = lax.optimization_barrier(
        (gate_other, up_other, w_down, keys)
    )

    states = local_states(decay_rate, keys_late, values)
    pieces = states.reshape(n_ctx, width // n_ctx, HEAD)
    pieces = lax.all_to_all(pieces, CTX, 0, 0, tiled=True)
    pieces = scan_states(float(tokens), decay_rate, pieces)
    arrived[LAST], pieces = lax.optimization_barrier((arrived[LAST], pieces))
    prefix = lax.all_to_all(pieces, CTX, 0, 0, tiled=True).reshape(width, HEAD)
    intra = intra_part(decay_rate, queries, keys, values)

    me_x = lax.axis_index("x")
    down_own, down_other = [], []
    for k in range(n_x):
        start = lax.rem(me_x + k, n_x) * chunk
        part = lax.dynamic_slice(w_down[0], (0, start), (units, chunk))
        part = shift(part, "x", k) if k else part
        down_own.append(part)
        down_other.append(shift(part, "core", 1))
    arrived[LAST], intra, *down_other = lax.optimization_barrier(
        (arrived[LAST], intra, *down_other)
    )

    weights = (gate_own, gate_other, up_own, up_other)
    hidden = hidden_part(arrived, weights)
    hidden = [hidden] + [shift(hidden, "x", k) for k in range(1, n_x)]
    parts = down_part(down_own, down_other, hidden, n_z * n_core, columns)
    parts, prefix = lax.optimization_barrier((parts, prefix))
    parts = lax.all_to_all(parts, ("z", "core"), 0, 0, tiled=True)

    mixed, squares = mix_part(decay_rate, intra, queries, prefix)
    squares = [squares] + [shift(squares, "exp", k) for k in range(1, n_exp)]
    parts, *squares = lax.optimization_barrier((parts, *squares))
    attention_out = norm_part(
        float(width * n_exp), squares, mixed, norm_gain[None, :], gates
    )

    parts = sum_part(parts.reshape(n_z, n_core, n_exp, columns, TILE))
    homes = []
    for k in range(n_exp):
        pairs = []
        for z in range(n_z):
            for x in range(n_x):
                chip = x * n_z + z
                for e in range(n_exp):
                    home = chip * n_exp + (e + n_exp - k) % n_exp
                    pairs.append(((z * n_x + x) * n_exp + e, home))
        homes.append(lax.ppermute(parts[k], ("z", "x", "exp"), pairs))
    moe_out = jnp.swapaxes(finish_part(ids, homes, row_weight[None, :]), 0, 1)
    return attention_out, moe_out


def solution(mesh):
    n_core, n_x = 2, 4
    grid = mesh.devices.reshape(-1, n_x, n_core, mesh.devices.shape[1])
    fine = Mesh(grid, ("z", "x", "core", "exp"))
    placed = (
        P(CTX, "exp"),
        P(CTX, "exp"),
        P(CTX, "exp"),
        P(CTX, "exp"),
        P("exp"),
        P("exp"),
        P("exp", None),
        P("exp", None),
        P("exp"),
        P("exp", None, CTX),
        P("exp", None, CTX),
        P("exp", CTX, None),
    )
    return jax.shard_map(
        on_device,
        mesh=fine,
        in_specs=placed,
        out_specs=(P(CTX, "exp"), P("exp", CTX)),
        check_vma=False,
    )
```

```python
import functools

import jax
import jax.numpy as jnp
from jax import lax
from jax.experimental import pallas as pl
from jax.experimental.pallas import tpu as pltpu
from jax.sharding import Mesh
from jax.sharding import PartitionSpec as P

BF = jnp.bfloat16
F32 = jnp.float32
CTX = ("z", "x", "core")
HEAD = 128
TILE = 128
GROUP = 4
LAST = 1


def _state_kernel(rate, k, v, out):
    tokens = k.shape[0]
    first = pl.program_id(0) * GROUP
    t = lax.broadcasted_iota(jnp.int32, (tokens, HEAD), 0).astype(F32)
    for h in range(GROUP):
        at = slice(h * HEAD, (h + 1) * HEAD)
        decay = jnp.exp(-rate[first + h] * (tokens - t))
        scaled = (k[:, at].astype(F32) * decay).astype(BF)
        out[at, :] = lax.dot_general(
            scaled, v[:, at], (((0,), (0,)), ((), ())), preferred_element_type=F32
        ).astype(BF)


def local_states(rate, keys, values):
    tokens, width = keys.shape
    spec = pl.BlockSpec((tokens, GROUP * HEAD), lambda h: (0, h))
    return pl.pallas_call(
        _state_kernel,
        grid=(width // (GROUP * HEAD),),
        in_specs=[pl.BlockSpec(memory_space=pltpu.SMEM), spec, spec],
        out_specs=pl.BlockSpec((GROUP * HEAD, HEAD), lambda h: (h, 0)),
        out_shape=jax.ShapeDtypeStruct((width, HEAD), BF),
        compiler_params=pltpu.CompilerParams(vmem_limit_bytes=8 << 20),
        name="local_states",
    )(rate, keys, values)


def _scan_kernel(tokens, heads, rate, states, out):
    blocks, rows, width = states.shape
    mine = lax.axis_index(CTX) * heads // blocks
    lam = jnp.exp(jnp.full((rows, width), -rate[mine] * tokens, F32))
    carry = jnp.zeros((rows, width), F32)
    for b in range(blocks):
        out[b] = carry.astype(BF)
        carry = carry * lam + states[b].astype(F32)


def scan_states(tokens, rate, states):
    return pl.pallas_call(
        functools.partial(_scan_kernel, tokens, rate.shape[0]),
        in_specs=[
            pl.BlockSpec(memory_space=pltpu.SMEM),
            pl.BlockSpec(memory_space=pltpu.VMEM),
        ],
        out_specs=pl.BlockSpec(memory_space=pltpu.VMEM),
        out_shape=jax.ShapeDtypeStruct(states.shape, BF),
        compiler_params=pltpu.CompilerParams(vmem_limit_bytes=6 << 20),
        name="scan_states",
    )(rate, states)


def _intra_kernel(rate, q, k, v, out):
    tokens = q.shape[0]
    first = pl.program_id(0) * GROUP
    i = lax.broadcasted_iota(jnp.int32, (tokens, tokens), 0)
    j = lax.broadcasted_iota(jnp.int32, (tokens, tokens), 1)
    off = (i - j).astype(F32)
    for h in range(GROUP):
        at = slice(h * HEAD, (h + 1) * HEAD)
        r = rate[first + h]
        within = jnp.where(off >= 0.0, jnp.exp(-r * jnp.maximum(off, 0.0)), 0.0)
        scores = lax.dot_general(
            q[:, at], k[:, at], (((1,), (1,)), ((), ())), preferred_element_type=F32
        )
        out[:, at] = jnp.dot(
            (scores * within).astype(BF), v[:, at], preferred_element_type=F32
        )


def intra_part(rate, queries, keys, values):
    tokens, width = keys.shape
    spec = pl.BlockSpec((tokens, GROUP * HEAD), lambda h: (0, h))
    return pl.pallas_call(
        _intra_kernel,
        grid=(width // (GROUP * HEAD),),
        in_specs=[pl.BlockSpec(memory_space=pltpu.SMEM), spec, spec, spec],
        out_specs=spec,
        out_shape=jax.ShapeDtypeStruct((tokens, width), F32),
        compiler_params=pltpu.CompilerParams(vmem_limit_bytes=14 << 20),
        name="intra_part",
    )(rate, queries, keys, values)


def _mix_kernel(rate, intra, q, prefix, mixed, squares):
    tokens = q.shape[0]
    step = pl.program_id(0)
    t = lax.broadcasted_iota(jnp.int32, (tokens, HEAD), 0).astype(F32)
    total = jnp.zeros((tokens, HEAD), F32)
    for h in range(GROUP):
        at = slice(h * HEAD, (h + 1) * HEAD)
        r = rate[step * GROUP + h]
        inter = jnp.dot(q[:, at], prefix[at, :], preferred_element_type=F32)
        value = intra[:, at] + inter * jnp.exp(-r * t)
        mixed[:, at] = value
        total += value * value

    @pl.when(step == 0)
    def _():
        squares[...] = jnp.zeros_like(squares)

    squares[...] += jnp.sum(jnp.transpose(total), axis=0, keepdims=True)


def mix_part(rate, intra, queries, prefix):
    tokens, width = queries.shape
    spec = pl.BlockSpec((tokens, GROUP * HEAD), lambda h: (0, h))
    return pl.pallas_call(
        _mix_kernel,
        grid=(width // (GROUP * HEAD),),
        in_specs=[
            pl.BlockSpec(memory_space=pltpu.SMEM),
            spec,
            spec,
            pl.BlockSpec((GROUP * HEAD, HEAD), lambda h: (h, 0)),
        ],
        out_specs=[spec, pl.BlockSpec((1, tokens), lambda h: (0, 0))],
        out_shape=[
            jax.ShapeDtypeStruct((tokens, width), F32),
            jax.ShapeDtypeStruct((1, tokens), F32),
        ],
        compiler_params=pltpu.CompilerParams(vmem_limit_bytes=14 << 20),
        name="mix_part",
    )(rate, intra, queries, prefix)


def _norm_kernel(features, *refs):
    *squares, mixed, gain, gates, out = refs
    tokens = mixed.shape[0]
    total = sum((part[...] for part in squares[1:]), squares[0][...])
    factor = lax.rsqrt(total / features + 1e-06)
    column = jnp.transpose(jnp.broadcast_to(factor, (HEAD, tokens)))
    for h in range(GROUP):
        at = slice(h * HEAD, (h + 1) * HEAD)
        scaled = mixed[:, at] * column * gain[:, at]
        out[:, at] = (scaled * jax.nn.sigmoid(gates[:, at].astype(F32))).astype(BF)


def norm_part(features, squares, mixed, gain, gates):
    tokens, width = mixed.shape
    spec = pl.BlockSpec((tokens, GROUP * HEAD), lambda h: (0, h))
    row = pl.BlockSpec((1, tokens), lambda h: (0, 0))
    return pl.pallas_call(
        functools.partial(_norm_kernel, features),
        grid=(width // (GROUP * HEAD),),
        in_specs=[row] * len(squares)
        + [spec, pl.BlockSpec((1, GROUP * HEAD), lambda h: (0, h)), spec],
        out_specs=spec,
        out_shape=jax.ShapeDtypeStruct((tokens, width), BF),
        compiler_params=pltpu.CompilerParams(vmem_limit_bytes=14 << 20),
        name="norm_part",
    )(*squares, mixed, gain, gates)


def _pick_kernel(ids, rows, *refs):
    outs, held, into, out_of = refs[:-3], refs[-3], refs[-2], refs[-1]
    n_exp, me_e, me_core = lax.axis_size("exp"), lax.axis_index("exp"), lax.axis_index("core")
    tiles, half = ids.shape[0], TILE // 2
    loads = []
    for k in range(len(outs)):
        target = lax.rem(me_e + k + 1, n_exp)
        seen = jnp.int32(0)
        tile = [jnp.int32(0), jnp.int32(0)]
        for t in range(tiles):
            same = ids[t] == target
            for rank in range(2):
                tile[rank] = jnp.where(same & (seen == rank), t, tile[rank])
            seen = seen + same.astype(jnp.int32)
        for rank in range(2):
            start = pl.multiple_of(tile[rank] * TILE + me_core * half, half)
            load = pltpu.make_async_copy(
                rows.at[pl.ds(start, half), :],
                held.at[k, pl.ds(rank * half, half), :],
                into.at[k, rank],
            )
            load.start()
            loads.append(load)
    stores = []
    for k in range(len(outs)):
        loads[2 * k].wait()
        loads[2 * k + 1].wait()
        store = pltpu.make_async_copy(held.at[k], outs[k], out_of.at[k])
        store.start()
        stores.append(store)
    for store in stores:
        store.wait()


def pick_tiles(ids, rows, count):
    tile = jax.ShapeDtypeStruct((TILE, rows.shape[1]), rows.dtype)
    return pl.pallas_call(
        _pick_kernel,
        in_specs=[
            pl.BlockSpec(memory_space=pltpu.SMEM),
            pl.BlockSpec(memory_space=pl.ANY),
        ],
        out_specs=[pl.BlockSpec(memory_space=pl.ANY)] * count,
        out_shape=[tile] * count,
        scratch_shapes=[
            pltpu.VMEM((count, TILE, rows.shape[1]), rows.dtype),
            pltpu.SemaphoreType.DMA((count, 2)),
            pltpu.SemaphoreType.DMA((count,)),
        ],
        compiler_params=pltpu.CompilerParams(vmem_limit_bytes=8 << 20),
        name="pick_tiles",
    )(ids, rows)


def _hidden_kernel(count, *refs):
    rows, weights = refs[:count], refs[count : count + 4]
    held, out = refs[-1], refs[-2]
    gate_own, gate_other, up_own, up_other = weights
    units = gate_own.shape[0]
    for i in range(count):
        held[i * TILE : (i + 1) * TILE, :] = rows[i][...]
    x = held[...]
    for i, (gate, up) in enumerate(((gate_own, up_own), (gate_other, up_other))):
        dims = (((1,), (1,)), ((), ()))
        g = lax.dot_general(gate[...], x, dims, preferred_element_type=F32)
        u = lax.dot_general(up[...], x, dims, preferred_element_type=F32)
        out[i * units : (i + 1) * units, :] = (jax.nn.silu(g) * u).astype(BF)


def hidden_part(rows, weights):
    count, units, model = len(rows), weights[0].shape[0], weights[0].shape[1]
    vmem = pl.BlockSpec(memory_space=pltpu.VMEM)
    return pl.pallas_call(
        functools.partial(_hidden_kernel, count),
        in_specs=[vmem] * (count + 4),
        out_specs=vmem,
        out_shape=jax.ShapeDtypeStruct((2 * units, count * TILE), BF),
        scratch_shapes=[pltpu.VMEM((count * TILE, model), BF)],
        compiler_params=pltpu.CompilerParams(vmem_limit_bytes=24 << 20),
        name="hidden_part",
    )(*rows, *weights)


def _down_kernel(own, other, hidden, out):
    n_x = len(own)
    units = own[0].shape[0]
    blocks, slots, columns = out.shape[:3]
    me_e, wide = lax.axis_index("exp"), 2 * TILE
    for j in range(slots // 2):
        total = None
        for k in range(n_x):
            for i, part in enumerate((own[k], other[k])):
                h = hidden[k][i * units : (i + 1) * units, j * wide : (j + 1) * wide]
                term = lax.dot_general(
                    part[...], h, (((0,), (0,)), ((), ())), preferred_element_type=F32
                )
                total = term if total is None else total + term
        total = total.astype(BF)
        for i in range(2):
            block = total[:, i * TILE : (i + 1) * TILE]
            home = lax.rem(me_e + slots - (2 * j + i), slots)
            out[:, home] = block.reshape(blocks, columns, TILE)


def down_part(own, other, hidden, blocks, columns):
    n_x, slots = len(own), hidden[0].shape[1] // TILE
    vmem = pl.BlockSpec(memory_space=pltpu.VMEM)

    def kernel(*refs):
        _down_kernel(
            refs[:n_x], refs[n_x : 2 * n_x], refs[2 * n_x : 3 * n_x], refs[-1]
        )

    return pl.pallas_call(
        kernel,
        in_specs=[vmem] * (3 * n_x),
        out_specs=vmem,
        out_shape=jax.ShapeDtypeStruct((blocks, slots, columns, TILE), BF),
        compiler_params=pltpu.CompilerParams(vmem_limit_bytes=24 << 20),
        name="down_part",
    )(*own, *other, *hidden)


def _finish_kernel(ids, parts, weight, out):
    n_z, n_core, n_exp, columns, _ = parts.shape
    tiles, half = ids.shape[0], TILE // 2
    low = lax.broadcasted_iota(jnp.int32, (columns, TILE), 1) < half
    for t in range(tiles):
        rank = jnp.int32(0)
        for earlier in range(t):
            rank = rank + (ids[earlier] == ids[t]).astype(jnp.int32)
        sums = []
        for core in range(n_core):
            total = jnp.zeros((columns, TILE), F32)
            for z in range(n_z):
                total = total + parts[z, core, ids[t]].astype(F32)
            sums.append(total.astype(BF).astype(F32))
        first, second = sums
        zero = jnp.where(low, first, pltpu.roll(second, half, 1))
        one = jnp.where(low, pltpu.roll(first, half, 1), second)
        rows = jnp.where(rank == 0, zero, one)
        at = slice(t * TILE, (t + 1) * TILE)
        out[:, at] = (rows * weight[:, at]).astype(BF)


def finish_part(ids, parts, weight):
    columns = parts.shape[3]
    vmem = pl.BlockSpec(memory_space=pltpu.VMEM)
    return pl.pallas_call(
        _finish_kernel,
        in_specs=[pl.BlockSpec(memory_space=pltpu.SMEM), vmem, vmem],
        out_specs=vmem,
        out_shape=jax.ShapeDtypeStruct((columns, weight.shape[1]), BF),
        compiler_params=pltpu.CompilerParams(vmem_limit_bytes=8 << 20),
        name="finish_part",
    )(ids, parts, weight)


def shift(array, axis, by):
    n = lax.axis_size(axis)
    return lax.ppermute(array, axis, [(i, (i + by) % n) for i in range(n)])


def on_device(
    queries, keys, values, gates, decay_rate, norm_gain,
    moe_rows, tile_expert, row_weight, w_gate, w_up, w_down,
):
    n_exp, n_z = lax.axis_size("exp"), lax.axis_size("z")
    n_x, n_core = lax.axis_size("x"), lax.axis_size("core")
    n_ctx = n_z * n_x * n_core
    tokens, width = queries.shape
    model = moe_rows.shape[1]
    ids = tile_expert[:, 0]
    columns = model // n_ctx
    chunk = model // n_x

    gate_own = jnp.swapaxes(w_gate[0], 0, 1)
    up_own = jnp.swapaxes(w_up[0], 0, 1)
    gate_other = shift(gate_own, "core", 1)
    up_other = shift(up_own, "core", 1)
    units = gate_own.shape[0]

    picked = pick_tiles(ids, moe_rows, n_exp)
    *picked, keys_late = lax.optimization_barrier((*picked, keys))
    arrived = [picked[-1]]
    arrived += [shift(picked[k - 1], "exp", k) for k in range(1, n_exp)]
    gate_other, up_other, keys_late = lax.optimization_barrier(
        (gate_other, up_other, keys_late)
    )

    states = local_states(decay_rate, keys_late, values)
    states, w_down = lax.optimization_barrier((states, w_down))
    pieces = states.reshape(n_ctx, width // n_ctx, HEAD)
    pieces = lax.all_to_all(pieces, CTX, 0, 0, tiled=True)
    pieces = scan_states(float(tokens), decay_rate, pieces)
    split = w_down[0].reshape(units, n_z, n_x, n_core * columns)
    split = jnp.transpose(split, (2, 0, 1, 3)).reshape(n_x, units, chunk)
    me_x = lax.axis_index("x")
    chunks = [
        lax.dynamic_index_in_dim(split, lax.rem(me_x + k, n_x), 0, keepdims=False)
        for k in range(n_x)
    ]
    down_own, down_other = [chunks[0]] + [None] * (n_x - 1), [None] * n_x
    lanes = (
        (("x", 1), ("x", 3), ("core", 1), ("core", 3)),
        (("x", 2), ("core", 0), ("core", 2)),
    )
    for lane in lanes:
        last = None
        for axis, k in lane:
            part = chunks[k] if axis == "x" else down_own[k]
            if last is not None and last is not part:
                part, last = lax.optimization_barrier((part, last))
            last = shift(part, axis, k if axis == "x" else 1)
            if axis == "x":
                down_own[k] = last
            else:
                down_other[k] = last
    arrived[LAST], pieces = lax.optimization_barrier((arrived[LAST], pieces))

    weights = (gate_own, gate_other, up_own, up_other)
    hidden = hidden_part(arrived, weights)
    hidden, queries = lax.optimization_barrier((hidden, queries))
    hidden = [hidden] + [shift(hidden, "x", k) for k in range(1, n_x)]
    intra = intra_part(decay_rate, queries, keys, values)
    hidden[1], intra = lax.optimization_barrier((hidden[1], intra))
    prefix = lax.all_to_all(pieces, CTX, 0, 0, tiled=True).reshape(width, HEAD)
    parts = down_part(down_own, down_other, hidden, n_z * n_core, columns)
    parts, prefix = lax.optimization_barrier((parts, prefix))
    parts = parts.reshape(-1, columns, TILE)
    parts = lax.all_to_all(parts, ("z", "core", "exp"), 0, 0, tiled=True)
    parts = parts.reshape(n_z, n_core, n_exp, columns, TILE)

    mixed, squares = mix_part(decay_rate, intra, queries, prefix)
    squares = [lax.psum(squares, "exp")]
    attention_out = norm_part(
        float(width * n_exp), squares, mixed, norm_gain[None, :], gates
    )
    moe_out = jnp.swapaxes(finish_part(ids, parts, row_weight[None, :]), 0, 1)
    return attention_out, moe_out


def solution(mesh):
    n_core, n_x = 2, 4
    grid = mesh.devices.reshape(-1, n_x, n_core, mesh.devices.shape[1])
    fine = Mesh(grid, ("z", "x", "core", "exp"))
    placed = (
        P(CTX, "exp"),
        P(CTX, "exp"),
        P(CTX, "exp"),
        P(CTX, "exp"),
        P("exp"),
        P("exp"),
        P("exp", None),
        P("exp", None),
        P("exp"),
        P("exp", None, CTX),
        P("exp", None, CTX),
        P("exp", CTX, None),
    )
    return jax.shard_map(
        on_device,
        mesh=fine,
        in_specs=placed,
        out_specs=(P(CTX, "exp"), P("exp", CTX)),
        check_vma=False,
    )
```

```python
import functools

import jax
import jax.numpy as jnp
from jax import lax
from jax.experimental import pallas as pl
from jax.experimental.pallas import tpu as pltpu
from jax.sharding import Mesh
from jax.sharding import PartitionSpec as P

BF = jnp.bfloat16
F32 = jnp.float32
CTX = ("z", "x", "core")
HEAD = 128
TILE = 128
GROUP = 4
LAST = 1


def _state_kernel(rate, k, v, out):
    tokens = k.shape[0]
    first = pl.program_id(0) * GROUP
    t = lax.broadcasted_iota(jnp.int32, (tokens, HEAD), 0).astype(F32)
    for h in range(GROUP):
        at = slice(h * HEAD, (h + 1) * HEAD)
        decay = jnp.exp(-rate[first + h] * (tokens - t))
        scaled = (k[:, at].astype(F32) * decay).astype(BF)
        out[at, :] = lax.dot_general(
            scaled, v[:, at], (((0,), (0,)), ((), ())), preferred_element_type=F32
        ).astype(BF)


def local_states(rate, keys, values):
    tokens, width = keys.shape
    spec = pl.BlockSpec((tokens, GROUP * HEAD), lambda h: (0, h))
    return pl.pallas_call(
        _state_kernel,
        grid=(width // (GROUP * HEAD),),
        in_specs=[pl.BlockSpec(memory_space=pltpu.SMEM), spec, spec],
        out_specs=pl.BlockSpec((GROUP * HEAD, HEAD), lambda h: (h, 0)),
        out_shape=jax.ShapeDtypeStruct((width, HEAD), BF),
        compiler_params=pltpu.CompilerParams(vmem_limit_bytes=8 << 20),
        name="local_states",
    )(rate, keys, values)


def _scan_kernel(tokens, heads, rate, states, out):
    blocks, rows, width = states.shape
    mine = lax.axis_index(CTX) * heads // blocks
    lam = jnp.exp(jnp.full((rows, width), -rate[mine] * tokens, F32))
    carry = jnp.zeros((rows, width), F32)
    for b in range(blocks):
        out[b] = carry.astype(BF)
        carry = carry * lam + states[b].astype(F32)


def scan_states(tokens, rate, states):
    return pl.pallas_call(
        functools.partial(_scan_kernel, tokens, rate.shape[0]),
        in_specs=[
            pl.BlockSpec(memory_space=pltpu.SMEM),
            pl.BlockSpec(memory_space=pltpu.VMEM),
        ],
        out_specs=pl.BlockSpec(memory_space=pltpu.VMEM),
        out_shape=jax.ShapeDtypeStruct(states.shape, BF),
        compiler_params=pltpu.CompilerParams(vmem_limit_bytes=6 << 20),
        name="scan_states",
    )(rate, states)


def _intra_kernel(rate, q, k, v, out):
    tokens = q.shape[0]
    first = pl.program_id(0) * GROUP
    i = lax.broadcasted_iota(jnp.int32, (tokens, tokens), 0)
    j = lax.broadcasted_iota(jnp.int32, (tokens, tokens), 1)
    off = (i - j).astype(F32)
    for h in range(GROUP):
        at = slice(h * HEAD, (h + 1) * HEAD)
        r = rate[first + h]
        within = jnp.where(off >= 0.0, jnp.exp(-r * jnp.maximum(off, 0.0)), 0.0)
        scores = lax.dot_general(
            q[:, at], k[:, at], (((1,), (1,)), ((), ())), preferred_element_type=F32
        )
        out[:, at] = jnp.dot(
            (scores * within).astype(BF), v[:, at], preferred_element_type=F32
        )


def intra_part(rate, queries, keys, values):
    tokens, width = keys.shape
    spec = pl.BlockSpec((tokens, GROUP * HEAD), lambda h: (0, h))
    return pl.pallas_call(
        _intra_kernel,
        grid=(width // (GROUP * HEAD),),
        in_specs=[pl.BlockSpec(memory_space=pltpu.SMEM), spec, spec, spec],
        out_specs=spec,
        out_shape=jax.ShapeDtypeStruct((tokens, width), F32),
        compiler_params=pltpu.CompilerParams(vmem_limit_bytes=14 << 20),
        name="intra_part",
    )(rate, queries, keys, values)


def _mix_kernel(rate, intra, q, prefix, mixed, squares):
    tokens = q.shape[0]
    step = pl.program_id(0)
    t = lax.broadcasted_iota(jnp.int32, (tokens, HEAD), 0).astype(F32)
    total = jnp.zeros((tokens, HEAD), F32)
    for h in range(GROUP):
        at = slice(h * HEAD, (h + 1) * HEAD)
        r = rate[step * GROUP + h]
        inter = jnp.dot(q[:, at], prefix[at, :], preferred_element_type=F32)
        value = intra[:, at] + inter * jnp.exp(-r * t)
        mixed[:, at] = value
        total += value * value

    @pl.when(step == 0)
    def _():
        squares[...] = jnp.zeros_like(squares)

    squares[...] += jnp.sum(jnp.transpose(total), axis=0, keepdims=True)


def mix_part(rate, intra, queries, prefix):
    tokens, width = queries.shape
    spec = pl.BlockSpec((tokens, GROUP * HEAD), lambda h: (0, h))
    return pl.pallas_call(
        _mix_kernel,
        grid=(width // (GROUP * HEAD),),
        in_specs=[
            pl.BlockSpec(memory_space=pltpu.SMEM),
            spec,
            spec,
            pl.BlockSpec((GROUP * HEAD, HEAD), lambda h: (h, 0)),
        ],
        out_specs=[spec, pl.BlockSpec((1, tokens), lambda h: (0, 0))],
        out_shape=[
            jax.ShapeDtypeStruct((tokens, width), F32),
            jax.ShapeDtypeStruct((1, tokens), F32),
        ],
        compiler_params=pltpu.CompilerParams(vmem_limit_bytes=14 << 20),
        name="mix_part",
    )(rate, intra, queries, prefix)


def _norm_kernel(features, *refs):
    *squares, mixed, gain, gates, out = refs
    tokens = mixed.shape[0]
    total = sum((part[...] for part in squares[1:]), squares[0][...])
    factor = lax.rsqrt(total / features + 1e-06)
    column = jnp.transpose(jnp.broadcast_to(factor, (HEAD, tokens)))
    for h in range(GROUP):
        at = slice(h * HEAD, (h + 1) * HEAD)
        scaled = mixed[:, at] * column * gain[:, at]
        out[:, at] = (scaled * jax.nn.sigmoid(gates[:, at].astype(F32))).astype(BF)


def norm_part(features, squares, mixed, gain, gates):
    tokens, width = mixed.shape
    spec = pl.BlockSpec((tokens, GROUP * HEAD), lambda h: (0, h))
    row = pl.BlockSpec((1, tokens), lambda h: (0, 0))
    return pl.pallas_call(
        functools.partial(_norm_kernel, features),
        grid=(width // (GROUP * HEAD),),
        in_specs=[row] * len(squares)
        + [spec, pl.BlockSpec((1, GROUP * HEAD), lambda h: (0, h)), spec],
        out_specs=spec,
        out_shape=jax.ShapeDtypeStruct((tokens, width), BF),
        compiler_params=pltpu.CompilerParams(vmem_limit_bytes=14 << 20),
        name="norm_part",
    )(*squares, mixed, gain, gates)


def _pick_kernel(ids, rows, *refs):
    outs, held, into, out_of = refs[:-3], refs[-3], refs[-2], refs[-1]
    n_exp, me_e, me_core = lax.axis_size("exp"), lax.axis_index("exp"), lax.axis_index("core")
    tiles, half = ids.shape[0], TILE // 2
    loads = []
    for k in range(len(outs)):
        target = lax.rem(me_e + k + 1, n_exp)
        seen = jnp.int32(0)
        tile = [jnp.int32(0), jnp.int32(0)]
        for t in range(tiles):
            same = ids[t] == target
            for rank in range(2):
                tile[rank] = jnp.where(same & (seen == rank), t, tile[rank])
            seen = seen + same.astype(jnp.int32)
        for rank in range(2):
            start = pl.multiple_of(tile[rank] * TILE + me_core * half, half)
            load = pltpu.make_async_copy(
                rows.at[pl.ds(start, half), :],
                held.at[k, pl.ds(rank * half, half), :],
                into.at[k, rank],
            )
            load.start()
            loads.append(load)
    stores = []
    for k in range(len(outs)):
        loads[2 * k].wait()
        loads[2 * k + 1].wait()
        store = pltpu.make_async_copy(held.at[k], outs[k], out_of.at[k])
        store.start()
        stores.append(store)
    for store in stores:
        store.wait()


def pick_tiles(ids, rows, count):
    tile = jax.ShapeDtypeStruct((TILE, rows.shape[1]), rows.dtype)
    return pl.pallas_call(
        _pick_kernel,
        in_specs=[
            pl.BlockSpec(memory_space=pltpu.SMEM),
            pl.BlockSpec(memory_space=pl.ANY),
        ],
        out_specs=[pl.BlockSpec(memory_space=pl.ANY)] * count,
        out_shape=[tile] * count,
        scratch_shapes=[
            pltpu.VMEM((count, TILE, rows.shape[1]), rows.dtype),
            pltpu.SemaphoreType.DMA((count, 2)),
            pltpu.SemaphoreType.DMA((count,)),
        ],
        compiler_params=pltpu.CompilerParams(vmem_limit_bytes=58 << 20),
        name="pick_tiles",
    )(ids, rows)


def _hidden_kernel(count, *refs):
    sources, out = refs[: count + 4], refs[count + 4]
    rows, weights, sems = refs[count + 5 :]
    units = weights.shape[1]
    targets = [rows.at[i * TILE : (i + 1) * TILE, :] for i in range(count)]
    targets += [weights.at[i] for i in range(4)]
    copies = [
        pltpu.make_async_copy(source, target, sems.at[i])
        for i, (source, target) in enumerate(zip(sources, targets))
    ]
    first = [count, count + 2, 0, 1, count + 1, count + 3]
    order = first + [i for i in range(count + 4) if i not in first]
    for i in order:
        copies[i].start()
    dims = (((1,), (1,)), ((), ()))
    wide = 2 * TILE
    for j in range(count // 2):
        ready = [2 * j, 2 * j + 1] if j else []
        for i in ready:
            copies[i].wait()
        for i in range(2):
            if j == 0:
                for n in first[:4] if i == 0 else first[4:]:
                    copies[n].wait()
            x = rows[j * wide : (j + 1) * wide, :]
            g = lax.dot_general(weights[i], x, dims, preferred_element_type=F32)
            u = lax.dot_general(weights[2 + i], x, dims, preferred_element_type=F32)
            out[i * units : (i + 1) * units, j * wide : (j + 1) * wide] = (
                jax.nn.silu(g) * u
            ).astype(BF)


def hidden_part(rows, weights):
    count, (units, model) = len(rows), weights[0].shape
    return pl.pallas_call(
        functools.partial(_hidden_kernel, count),
        in_specs=[pl.BlockSpec(memory_space=pl.ANY)] * (count + 4),
        out_specs=pl.BlockSpec(memory_space=pltpu.VMEM),
        out_shape=jax.ShapeDtypeStruct((2 * units, count * TILE), BF),
        scratch_shapes=[
            pltpu.VMEM((count * TILE, model), BF),
            pltpu.VMEM((4, units, model), BF),
            pltpu.SemaphoreType.DMA((count + 4,)),
        ],
        compiler_params=pltpu.CompilerParams(vmem_limit_bytes=58 << 20),
        name="hidden_part",
    )(*rows, *weights)


def _split_kernel(n_z, weight, *outs):
    me_x, n_x = lax.axis_index("x"), len(outs)
    units, window = weight.shape[0], weight.shape[1] // n_z
    own = window // n_x
    lane = lax.broadcasted_iota(jnp.int32, (units, window), 1)
    for g in range(n_z // n_x):
        parts = [
            weight[:, z * window : (z + 1) * window].astype(F32)
            for z in range(g * n_x, (g + 1) * n_x)
        ]
        for k, out in enumerate(outs):
            target = lax.rem(me_x + k, n_x)
            total = jnp.zeros((units, window), F32)
            for i, part in enumerate(parts):
                turn = lax.rem(i + n_x - target, n_x) * own
                here = (lane >= i * own) & (lane < (i + 1) * own)
                total = jnp.where(here, pltpu.roll(part, turn, 1), total)
            out[:, g * window : (g + 1) * window] = total.astype(BF)


def split_columns(weight, n_z, n_x):
    units, model = weight.shape
    vmem = pl.BlockSpec(memory_space=pltpu.VMEM)
    return pl.pallas_call(
        functools.partial(_split_kernel, n_z),
        in_specs=[vmem],
        out_specs=[vmem] * n_x,
        out_shape=[jax.ShapeDtypeStruct((units, model // n_x), BF)] * n_x,
        compiler_params=pltpu.CompilerParams(vmem_limit_bytes=14 << 20),
        name="split_columns",
    )(weight)


def _down_kernel(own, other, hidden, out):
    n_x = len(own)
    units = own[0].shape[0]
    blocks, slots, columns = out.shape[:3]
    me_e, wide = lax.axis_index("exp"), 2 * TILE
    for j in range(slots // 2):
        total = None
        for k in range(n_x):
            for i, part in enumerate((own[k], other[k])):
                h = hidden[k][i * units : (i + 1) * units, j * wide : (j + 1) * wide]
                term = lax.dot_general(
                    part[...], h, (((0,), (0,)), ((), ())), preferred_element_type=F32
                )
                total = term if total is None else total + term
        total = total.astype(BF)
        for i in range(2):
            block = total[:, i * TILE : (i + 1) * TILE]
            home = lax.rem(me_e + slots - (2 * j + i), slots)
            out[:, home] = block.reshape(blocks, columns, TILE)


def down_part(own, other, hidden, blocks, columns):
    n_x, slots = len(own), hidden[0].shape[1] // TILE
    vmem = pl.BlockSpec(memory_space=pltpu.VMEM)

    def kernel(*refs):
        _down_kernel(
            refs[:n_x], refs[n_x : 2 * n_x], refs[2 * n_x : 3 * n_x], refs[-1]
        )

    return pl.pallas_call(
        kernel,
        in_specs=[vmem] * (3 * n_x),
        out_specs=vmem,
        out_shape=jax.ShapeDtypeStruct((blocks, slots, columns, TILE), BF),
        compiler_params=pltpu.CompilerParams(vmem_limit_bytes=24 << 20),
        name="down_part",
    )(*own, *other, *hidden)


def _finish_kernel(ids, parts, weight, out):
    n_z, n_core, n_exp, columns, _ = parts.shape
    tiles, half = ids.shape[0], TILE // 2
    low = lax.broadcasted_iota(jnp.int32, (columns, TILE), 1) < half
    for t in range(tiles):
        rank = jnp.int32(0)
        for earlier in range(t):
            rank = rank + (ids[earlier] == ids[t]).astype(jnp.int32)
        sums = []
        for core in range(n_core):
            total = jnp.zeros((columns, TILE), F32)
            for z in range(n_z):
                total = total + parts[z, core, ids[t]].astype(F32)
            sums.append(total.astype(BF).astype(F32))
        first, second = sums
        zero = jnp.where(low, first, pltpu.roll(second, half, 1))
        one = jnp.where(low, pltpu.roll(first, half, 1), second)
        rows = jnp.where(rank == 0, zero, one)
        at = slice(t * TILE, (t + 1) * TILE)
        out[:, at] = (rows * weight[:, at]).astype(BF)


def finish_part(ids, parts, weight):
    columns = parts.shape[3]
    vmem = pl.BlockSpec(memory_space=pltpu.VMEM)
    return pl.pallas_call(
        _finish_kernel,
        in_specs=[pl.BlockSpec(memory_space=pltpu.SMEM), vmem, vmem],
        out_specs=vmem,
        out_shape=jax.ShapeDtypeStruct((columns, weight.shape[1]), BF),
        compiler_params=pltpu.CompilerParams(vmem_limit_bytes=8 << 20),
        name="finish_part",
    )(ids, parts, weight)


def shift(array, axis, by):
    n = lax.axis_size(axis)
    return lax.ppermute(array, axis, [(i, (i + by) % n) for i in range(n)])


def on_device(
    queries, keys, values, gates, decay_rate, norm_gain,
    moe_rows, tile_expert, row_weight, w_gate, w_up, w_down,
):
    n_exp, n_z = lax.axis_size("exp"), lax.axis_size("z")
    n_x, n_core = lax.axis_size("x"), lax.axis_size("core")
    n_ctx = n_z * n_x * n_core
    tokens, width = queries.shape
    model = moe_rows.shape[1]
    ids = tile_expert[:, 0]
    columns = model // n_ctx

    gate_own = jnp.swapaxes(w_gate[0], 0, 1)
    up_own = jnp.swapaxes(w_up[0], 0, 1)
    gate_other = shift(gate_own, "core", 1)
    up_other = shift(up_own, "core", 1)
    units = gate_own.shape[0]

    picked = pick_tiles(ids, moe_rows, n_exp)
    *picked, keys_late = lax.optimization_barrier((*picked, keys))
    arrived = [picked[-1]]
    arrived += [shift(picked[k - 1], "exp", k) for k in range(1, n_exp)]
    gate_other, up_other, keys_late = lax.optimization_barrier(
        (gate_other, up_other, keys_late)
    )

    states = local_states(decay_rate, keys_late, values)
    states, w_down = lax.optimization_barrier((states, w_down))
    pieces = states.reshape(n_ctx, width // n_ctx, HEAD)
    pieces = lax.all_to_all(pieces, CTX, 0, 0, tiled=True)
    pieces = scan_states(float(tokens), decay_rate, pieces)
    chunks = split_columns(w_down[0], n_z, n_x)
    down_own, down_other = [chunks[0]] + [None] * (n_x - 1), [None] * n_x
    lanes = (
        (("x", 1), ("x", 3), ("core", 1), ("core", 3)),
        (("x", 2), ("core", 0), ("core", 2)),
    )
    for lane in lanes:
        last = None
        for axis, k in lane:
            part = chunks[k] if axis == "x" else down_own[k]
            if last is not None and last is not part:
                part, last = lax.optimization_barrier((part, last))
            last = shift(part, axis, k if axis == "x" else 1)
            if axis == "x":
                down_own[k] = last
            else:
                down_other[k] = last
    arrived[LAST], pieces = lax.optimization_barrier((arrived[LAST], pieces))

    weights = (gate_own, gate_other, up_own, up_other)
    hidden = hidden_part(arrived, weights)
    hidden, queries = lax.optimization_barrier((hidden, queries))
    hidden = [hidden] + [shift(hidden, "x", k) for k in range(1, n_x)]
    intra = intra_part(decay_rate, queries, keys, values)
    hidden[1], intra = lax.optimization_barrier((hidden[1], intra))
    prefix = lax.all_to_all(pieces, CTX, 0, 0, tiled=True).reshape(width, HEAD)
    parts = down_part(down_own, down_other, hidden, n_z * n_core, columns)
    parts, prefix = lax.optimization_barrier((parts, prefix))
    parts = parts.reshape(-1, columns, TILE)
    parts = lax.all_to_all(parts, ("z", "core", "exp"), 0, 0, tiled=True)
    parts = parts.reshape(n_z, n_core, n_exp, columns, TILE)

    mixed, squares = mix_part(decay_rate, intra, queries, prefix)
    squares = [lax.psum(squares, "exp")]
    attention_out = norm_part(
        float(width * n_exp), squares, mixed, norm_gain[None, :], gates
    )
    moe_out = jnp.swapaxes(finish_part(ids, parts, row_weight[None, :]), 0, 1)
    return attention_out, moe_out


def solution(mesh):
    n_core, n_x = 2, 4
    grid = mesh.devices.reshape(-1, n_x, n_core, mesh.devices.shape[1])
    fine = Mesh(grid, ("z", "x", "core", "exp"))
    placed = (
        P(CTX, "exp"),
        P(CTX, "exp"),
        P(CTX, "exp"),
        P(CTX, "exp"),
        P("exp"),
        P("exp"),
        P("exp", None),
        P("exp", None),
        P("exp"),
        P("exp", None, CTX),
        P("exp", None, CTX),
        P("exp", CTX, None),
    )
    return jax.shard_map(
        on_device,
        mesh=fine,
        in_specs=placed,
        out_specs=(P(CTX, "exp"), P("exp", CTX)),
        check_vma=False,
    )
```

```python
import functools

import jax
import jax.numpy as jnp
from jax import lax
from jax.experimental import pallas as pl
from jax.experimental.pallas import tpu as pltpu
from jax.sharding import Mesh
from jax.sharding import PartitionSpec as P

BF = jnp.bfloat16
F32 = jnp.float32
CTX = ("z", "x", "core")
HEAD = 128
TILE = 128
GROUP = 4
LAST = 1


def _state_kernel(rate, k, v, out):
    tokens = k.shape[0]
    first = pl.program_id(0) * GROUP
    t = lax.broadcasted_iota(jnp.int32, (tokens, HEAD), 0).astype(F32)
    for h in range(GROUP):
        at = slice(h * HEAD, (h + 1) * HEAD)
        decay = jnp.exp(-rate[first + h] * (tokens - t))
        scaled = (k[:, at].astype(F32) * decay).astype(BF)
        out[at, :] = lax.dot_general(
            scaled, v[:, at], (((0,), (0,)), ((), ())), preferred_element_type=F32
        ).astype(BF)


def local_states(rate, keys, values):
    tokens, width = keys.shape
    spec = pl.BlockSpec((tokens, GROUP * HEAD), lambda h: (0, h))
    return pl.pallas_call(
        _state_kernel,
        grid=(width // (GROUP * HEAD),),
        in_specs=[pl.BlockSpec(memory_space=pltpu.SMEM), spec, spec],
        out_specs=pl.BlockSpec((GROUP * HEAD, HEAD), lambda h: (h, 0)),
        out_shape=jax.ShapeDtypeStruct((width, HEAD), BF),
        compiler_params=pltpu.CompilerParams(vmem_limit_bytes=8 << 20),
        name="local_states",
    )(rate, keys, values)


def _scan_kernel(tokens, heads, rate, states, out):
    blocks, rows, width = states.shape
    mine = lax.axis_index(CTX) * heads // blocks
    lam = jnp.exp(jnp.full((rows, width), -rate[mine] * tokens, F32))
    carry = jnp.zeros((rows, width), F32)
    for b in range(blocks):
        out[b] = carry.astype(BF)
        carry = carry * lam + states[b].astype(F32)


def scan_states(tokens, rate, states):
    return pl.pallas_call(
        functools.partial(_scan_kernel, tokens, rate.shape[0]),
        in_specs=[
            pl.BlockSpec(memory_space=pltpu.SMEM),
            pl.BlockSpec(memory_space=pltpu.VMEM),
        ],
        out_specs=pl.BlockSpec(memory_space=pltpu.VMEM),
        out_shape=jax.ShapeDtypeStruct(states.shape, BF),
        compiler_params=pltpu.CompilerParams(vmem_limit_bytes=6 << 20),
        name="scan_states",
    )(rate, states)


def _intra_kernel(rate, q, k, v, out):
    tokens = q.shape[0]
    first = pl.program_id(0) * GROUP
    i = lax.broadcasted_iota(jnp.int32, (tokens, tokens), 0)
    j = lax.broadcasted_iota(jnp.int32, (tokens, tokens), 1)
    off = (i - j).astype(F32)
    for h in range(GROUP):
        at = slice(h * HEAD, (h + 1) * HEAD)
        r = rate[first + h]
        within = jnp.where(off >= 0.0, jnp.exp(-r * jnp.maximum(off, 0.0)), 0.0)
        scores = lax.dot_general(
            q[:, at], k[:, at], (((1,), (1,)), ((), ())), preferred_element_type=F32
        )
        out[:, at] = jnp.dot(
            (scores * within).astype(BF), v[:, at], preferred_element_type=F32
        )


def intra_part(rate, queries, keys, values):
    tokens, width = keys.shape
    spec = pl.BlockSpec((tokens, GROUP * HEAD), lambda h: (0, h))
    return pl.pallas_call(
        _intra_kernel,
        grid=(width // (GROUP * HEAD),),
        in_specs=[pl.BlockSpec(memory_space=pltpu.SMEM), spec, spec, spec],
        out_specs=spec,
        out_shape=jax.ShapeDtypeStruct((tokens, width), F32),
        compiler_params=pltpu.CompilerParams(vmem_limit_bytes=14 << 20),
        name="intra_part",
    )(rate, queries, keys, values)


def _mix_kernel(rate, intra, q, prefix, mixed, squares):
    tokens = q.shape[0]
    step = pl.program_id(0)
    t = lax.broadcasted_iota(jnp.int32, (tokens, HEAD), 0).astype(F32)
    total = jnp.zeros((tokens, HEAD), F32)
    for h in range(GROUP):
        at = slice(h * HEAD, (h + 1) * HEAD)
        r = rate[step * GROUP + h]
        inter = jnp.dot(q[:, at], prefix[at, :], preferred_element_type=F32)
        value = intra[:, at] + inter * jnp.exp(-r * t)
        mixed[:, at] = value
        total += value * value

    @pl.when(step == 0)
    def _():
        squares[...] = jnp.zeros_like(squares)

    squares[...] += jnp.sum(jnp.transpose(total), axis=0, keepdims=True)


def mix_part(rate, intra, queries, prefix):
    tokens, width = queries.shape
    spec = pl.BlockSpec((tokens, GROUP * HEAD), lambda h: (0, h))
    return pl.pallas_call(
        _mix_kernel,
        grid=(width // (GROUP * HEAD),),
        in_specs=[
            pl.BlockSpec(memory_space=pltpu.SMEM),
            spec,
            spec,
            pl.BlockSpec((GROUP * HEAD, HEAD), lambda h: (h, 0)),
        ],
        out_specs=[spec, pl.BlockSpec((1, tokens), lambda h: (0, 0))],
        out_shape=[
            jax.ShapeDtypeStruct((tokens, width), F32),
            jax.ShapeDtypeStruct((1, tokens), F32),
        ],
        compiler_params=pltpu.CompilerParams(vmem_limit_bytes=14 << 20),
        name="mix_part",
    )(rate, intra, queries, prefix)


def _norm_kernel(features, *refs):
    *squares, mixed, gain, gates, out = refs
    tokens = mixed.shape[0]
    total = sum((part[...] for part in squares[1:]), squares[0][...])
    factor = lax.rsqrt(total / features + 1e-06)
    column = jnp.transpose(jnp.broadcast_to(factor, (HEAD, tokens)))
    for h in range(GROUP):
        at = slice(h * HEAD, (h + 1) * HEAD)
        scaled = mixed[:, at] * column * gain[:, at]
        out[:, at] = (scaled * jax.nn.sigmoid(gates[:, at].astype(F32))).astype(BF)


def norm_part(features, squares, mixed, gain, gates):
    tokens, width = mixed.shape
    spec = pl.BlockSpec((tokens, GROUP * HEAD), lambda h: (0, h))
    row = pl.BlockSpec((1, tokens), lambda h: (0, 0))
    return pl.pallas_call(
        functools.partial(_norm_kernel, features),
        grid=(width // (GROUP * HEAD),),
        in_specs=[row] * len(squares)
        + [spec, pl.BlockSpec((1, GROUP * HEAD), lambda h: (0, h)), spec],
        out_specs=spec,
        out_shape=jax.ShapeDtypeStruct((tokens, width), BF),
        compiler_params=pltpu.CompilerParams(vmem_limit_bytes=14 << 20),
        name="norm_part",
    )(*squares, mixed, gain, gates)


def _pick_kernel(ids, rows, *refs):
    outs, held, into, out_of = refs[:-3], refs[-3], refs[-2], refs[-1]
    n_exp, me_e, me_core = lax.axis_size("exp"), lax.axis_index("exp"), lax.axis_index("core")
    tiles, half = ids.shape[0], TILE // 2
    loads = []
    for k in range(len(outs)):
        target = lax.rem(me_e + k + 1, n_exp)
        seen = jnp.int32(0)
        tile = [jnp.int32(0), jnp.int32(0)]
        for t in range(tiles):
            same = ids[t] == target
            for rank in range(2):
                tile[rank] = jnp.where(same & (seen == rank), t, tile[rank])
            seen = seen + same.astype(jnp.int32)
        for rank in range(2):
            start = pl.multiple_of(tile[rank] * TILE + me_core * half, half)
            load = pltpu.make_async_copy(
                rows.at[pl.ds(start, half), :],
                held.at[k, pl.ds(rank * half, half), :],
                into.at[k, rank],
            )
            load.start()
            loads.append(load)
    stores = []
    for k in range(len(outs)):
        loads[2 * k].wait()
        loads[2 * k + 1].wait()
        store = pltpu.make_async_copy(held.at[k], outs[k], out_of.at[k])
        store.start()
        stores.append(store)
    for store in stores:
        store.wait()


def pick_tiles(ids, rows, count):
    tile = jax.ShapeDtypeStruct((TILE, rows.shape[1]), rows.dtype)
    return pl.pallas_call(
        _pick_kernel,
        in_specs=[
            pl.BlockSpec(memory_space=pltpu.SMEM),
            pl.BlockSpec(memory_space=pl.ANY),
        ],
        out_specs=[pl.BlockSpec(memory_space=pl.ANY)] * count,
        out_shape=[tile] * count,
        scratch_shapes=[
            pltpu.VMEM((count, TILE, rows.shape[1]), rows.dtype),
            pltpu.SemaphoreType.DMA((count, 2)),
            pltpu.SemaphoreType.DMA((count,)),
        ],
        compiler_params=pltpu.CompilerParams(vmem_limit_bytes=58 << 20),
        name="pick_tiles",
    )(ids, rows)


def _hidden_kernel(count, *refs):
    sources, out = refs[: count + 4], refs[count + 4]
    rows, weights, sems = refs[count + 5 :]
    units = weights.shape[0] // 4
    targets = [rows.at[i * TILE : (i + 1) * TILE, :] for i in range(count)]
    targets += [weights.at[i * units : (i + 1) * units, :] for i in range(4)]
    copies = [
        pltpu.make_async_copy(source, target, sems.at[i])
        for i, (source, target) in enumerate(zip(sources, targets))
    ]
    order = list(range(count, count + 4)) + list(range(count))
    for i in order:
        copies[i].start()
    for i in range(4):
        copies[count + i].wait()
    dims = (((1,), (1,)), ((), ()))
    wide = 2 * TILE
    for j in range(count // 2):
        copies[2 * j].wait()
        copies[2 * j + 1].wait()
        at = slice(j * wide, (j + 1) * wide)
        both = lax.dot_general(
            weights[...], rows[at, :], dims, preferred_element_type=F32
        )
        gate, up = both[: 2 * units], both[2 * units :]
        out[:, at] = (jax.nn.silu(gate) * up).astype(BF)


def hidden_part(rows, weights):
    count, (units, model) = len(rows), weights[0].shape
    return pl.pallas_call(
        functools.partial(_hidden_kernel, count),
        in_specs=[pl.BlockSpec(memory_space=pl.ANY)] * (count + 4),
        out_specs=pl.BlockSpec(memory_space=pltpu.VMEM),
        out_shape=jax.ShapeDtypeStruct((2 * units, count * TILE), BF),
        scratch_shapes=[
            pltpu.VMEM((count * TILE, model), BF),
            pltpu.VMEM((4 * units, model), BF),
            pltpu.SemaphoreType.DMA((count + 4,)),
        ],
        compiler_params=pltpu.CompilerParams(vmem_limit_bytes=58 << 20),
        name="hidden_part",
    )(*rows, *weights)


def _split_kernel(n_z, weight, *outs):
    me_x, n_x = lax.axis_index("x"), len(outs)
    units, window = weight.shape[0], weight.shape[1] // n_z
    own = window // n_x
    lane = lax.broadcasted_iota(jnp.int32, (units, window), 1)
    for g in range(n_z // n_x):
        parts = [
            weight[:, z * window : (z + 1) * window].astype(F32)
            for z in range(g * n_x, (g + 1) * n_x)
        ]
        for k, out in enumerate(outs):
            target = lax.rem(me_x + k, n_x)
            total = jnp.zeros((units, window), F32)
            for i, part in enumerate(parts):
                turn = lax.rem(i + n_x - target, n_x) * own
                here = (lane >= i * own) & (lane < (i + 1) * own)
                total = jnp.where(here, pltpu.roll(part, turn, 1), total)
            out[:, g * window : (g + 1) * window] = total.astype(BF)


def split_columns(weight, n_z, n_x):
    units, model = weight.shape
    vmem = pl.BlockSpec(memory_space=pltpu.VMEM)
    return pl.pallas_call(
        functools.partial(_split_kernel, n_z),
        in_specs=[vmem],
        out_specs=[vmem] * n_x,
        out_shape=[jax.ShapeDtypeStruct((units, model // n_x), BF)] * n_x,
        compiler_params=pltpu.CompilerParams(vmem_limit_bytes=14 << 20),
        name="split_columns",
    )(weight)


def _stack_kernel(*refs):
    parts, out, sems = refs[:-2], refs[-2], refs[-1]
    units = parts[0].shape[0]
    copies = [
        pltpu.make_async_copy(part, out.at[i * units : (i + 1) * units, :], sems.at[i])
        for i, part in enumerate(parts)
    ]
    for copy in copies:
        copy.start()
    for copy in copies:
        copy.wait()


def stack_rows(parts):
    units, chunk = parts[0].shape
    return pl.pallas_call(
        _stack_kernel,
        in_specs=[pl.BlockSpec(memory_space=pl.ANY)] * len(parts),
        out_specs=pl.BlockSpec(memory_space=pltpu.VMEM),
        out_shape=jax.ShapeDtypeStruct((len(parts) * units, chunk), BF),
        scratch_shapes=[pltpu.SemaphoreType.DMA((len(parts),))],
        compiler_params=pltpu.CompilerParams(vmem_limit_bytes=10 << 20),
        name="stack_rows",
    )(*parts)


def _down_kernel(weight, *refs):
    hidden, out, held = refs[:-2], refs[-2], refs[-1]
    units = hidden[0].shape[0]
    for k, part in enumerate(hidden):
        held[k * units : (k + 1) * units, :] = part[...]
    blocks, slots, columns = out.shape[:3]
    me_e = lax.axis_index("exp")
    total = lax.dot_general(
        weight[...], held[...], (((0,), (0,)), ((), ())), preferred_element_type=F32
    ).astype(BF)
    for slot in range(slots):
        home = lax.rem(me_e + slots - slot, slots)
        block = total[:, slot * TILE : (slot + 1) * TILE]
        out[:, home] = block.reshape(blocks, columns, TILE)


def down_part(weight, hidden, blocks, columns):
    rows = hidden[0].shape[1]
    vmem = pl.BlockSpec(memory_space=pltpu.VMEM)
    return pl.pallas_call(
        _down_kernel,
        in_specs=[vmem] * (1 + len(hidden)),
        out_specs=vmem,
        out_shape=jax.ShapeDtypeStruct((blocks, rows // TILE, columns, TILE), BF),
        scratch_shapes=[pltpu.VMEM((weight.shape[0], rows), BF)],
        compiler_params=pltpu.CompilerParams(vmem_limit_bytes=24 << 20),
        name="down_part",
    )(weight, *hidden)


def _finish_kernel(ids, parts, weight, out):
    n_z, n_core, n_exp, columns, _ = parts.shape
    tiles, half = ids.shape[0], TILE // 2
    low = lax.broadcasted_iota(jnp.int32, (columns, TILE), 1) < half
    for t in range(tiles):
        rank = jnp.int32(0)
        for earlier in range(t):
            rank = rank + (ids[earlier] == ids[t]).astype(jnp.int32)
        sums = []
        for core in range(n_core):
            total = jnp.zeros((columns, TILE), F32)
            for z in range(n_z):
                total = total + parts[z, core, ids[t]].astype(F32)
            sums.append(total.astype(BF).astype(F32))
        first, second = sums
        zero = jnp.where(low, first, pltpu.roll(second, half, 1))
        one = jnp.where(low, pltpu.roll(first, half, 1), second)
        rows = jnp.where(rank == 0, zero, one)
        at = slice(t * TILE, (t + 1) * TILE)
        out[:, at] = (rows * weight[:, at]).astype(BF)


def finish_part(ids, parts, weight):
    columns = parts.shape[3]
    vmem = pl.BlockSpec(memory_space=pltpu.VMEM)
    return pl.pallas_call(
        _finish_kernel,
        in_specs=[pl.BlockSpec(memory_space=pltpu.SMEM), vmem, vmem],
        out_specs=vmem,
        out_shape=jax.ShapeDtypeStruct((columns, weight.shape[1]), BF),
        compiler_params=pltpu.CompilerParams(vmem_limit_bytes=8 << 20),
        name="finish_part",
    )(ids, parts, weight)


def shift(array, axis, by):
    n = lax.axis_size(axis)
    return lax.ppermute(array, axis, [(i, (i + by) % n) for i in range(n)])


def on_device(
    queries, keys, values, gates, decay_rate, norm_gain,
    moe_rows, tile_expert, row_weight, w_gate, w_up, w_down,
):
    n_exp, n_z = lax.axis_size("exp"), lax.axis_size("z")
    n_x, n_core = lax.axis_size("x"), lax.axis_size("core")
    n_ctx = n_z * n_x * n_core
    tokens, width = queries.shape
    model = moe_rows.shape[1]
    ids = tile_expert[:, 0]
    columns = model // n_ctx

    gate_own = jnp.swapaxes(w_gate[0], 0, 1)
    up_own = jnp.swapaxes(w_up[0], 0, 1)
    gate_other = shift(gate_own, "core", 1)
    up_other = shift(up_own, "core", 1)
    units = gate_own.shape[0]

    picked = pick_tiles(ids, moe_rows, n_exp)
    *picked, keys_late = lax.optimization_barrier((*picked, keys))
    arrived = [picked[-1]]
    arrived += [shift(picked[k - 1], "exp", k) for k in range(1, n_exp)]
    gate_other, up_other, keys_late = lax.optimization_barrier(
        (gate_other, up_other, keys_late)
    )

    states = local_states(decay_rate, keys_late, values)
    states, w_down = lax.optimization_barrier((states, w_down))
    pieces = states.reshape(n_ctx, width // n_ctx, HEAD)
    pieces = lax.all_to_all(pieces, CTX, 0, 0, tiled=True)
    pieces = scan_states(float(tokens), decay_rate, pieces)
    chunks = list(split_columns(w_down[0], n_z, n_x))
    down_own, down_other = [chunks[0]] + [None] * (n_x - 1), [None] * n_x
    lanes = (
        (("x", 1), ("x", 3), ("core", 1), ("core", 3)),
        (("x", 2), ("core", 0), ("core", 2)),
    )
    for lane in lanes:
        last = None
        for axis, k in lane:
            part = chunks[k] if axis == "x" else down_own[k]
            if last is not None and last is not part:
                part, last = lax.optimization_barrier((part, last))
            last = shift(part, axis, k if axis == "x" else 1)
            if axis == "x":
                down_own[k] = last
            else:
                down_other[k] = last
    arrived[LAST], pieces = lax.optimization_barrier((arrived[LAST], pieces))

    weights = (gate_own, gate_other, up_own, up_other)
    hidden = hidden_part(arrived, weights)
    hidden, queries = lax.optimization_barrier((hidden, queries))
    hidden = [hidden] + [shift(hidden, "x", k) for k in range(1, n_x)]
    intra = intra_part(decay_rate, queries, keys, values)
    hidden[1], intra = lax.optimization_barrier((hidden[1], intra))
    prefix = lax.all_to_all(pieces, CTX, 0, 0, tiled=True).reshape(width, HEAD)
    down = stack_rows([part for pair in zip(down_own, down_other) for part in pair])
    hidden[2], down = lax.optimization_barrier((hidden[2], down))
    parts = down_part(down, hidden, n_z * n_core, columns)
    parts, prefix = lax.optimization_barrier((parts, prefix))
    parts = parts.reshape(-1, columns, TILE)
    parts = lax.all_to_all(parts, ("z", "core", "exp"), 0, 0, tiled=True)
    parts = parts.reshape(n_z, n_core, n_exp, columns, TILE)

    mixed, squares = mix_part(decay_rate, intra, queries, prefix)
    squares = [lax.psum(squares, "exp")]
    attention_out = norm_part(
        float(width * n_exp), squares, mixed, norm_gain[None, :], gates
    )
    moe_out = jnp.swapaxes(finish_part(ids, parts, row_weight[None, :]), 0, 1)
    return attention_out, moe_out


def solution(mesh):
    n_core, n_x = 2, 4
    grid = mesh.devices.reshape(-1, n_x, n_core, mesh.devices.shape[1])
    fine = Mesh(grid, ("z", "x", "core", "exp"))
    placed = (
        P(CTX, "exp"),
        P(CTX, "exp"),
        P(CTX, "exp"),
        P(CTX, "exp"),
        P("exp"),
        P("exp"),
        P("exp", None),
        P("exp", None),
        P("exp"),
        P("exp", None, CTX),
        P("exp", None, CTX),
        P("exp", CTX, None),
    )
    return jax.shard_map(
        on_device,
        mesh=fine,
        in_specs=placed,
        out_specs=(P(CTX, "exp"), P("exp", CTX)),
        check_vma=False,
    )
```

```python
import functools

import jax
import jax.numpy as jnp
from jax import lax
from jax.experimental import pallas as pl
from jax.experimental.pallas import tpu as pltpu
from jax.sharding import Mesh
from jax.sharding import PartitionSpec as P

BF = jnp.bfloat16
F32 = jnp.float32
CTX = ("z", "x", "core")
HEAD = 128
TILE = 128
GROUP = 4
LAST = 1


def _state_kernel(rate, k, v, out):
    tokens = k.shape[0]
    first = pl.program_id(0) * GROUP
    t = lax.broadcasted_iota(jnp.int32, (tokens, HEAD), 0).astype(F32)
    for h in range(GROUP):
        at = slice(h * HEAD, (h + 1) * HEAD)
        decay = jnp.exp(-rate[first + h] * (tokens - t))
        scaled = (k[:, at].astype(F32) * decay).astype(BF)
        out[at, :] = lax.dot_general(
            scaled, v[:, at], (((0,), (0,)), ((), ())), preferred_element_type=F32
        ).astype(BF)


def local_states(rate, keys, values):
    tokens, width = keys.shape
    spec = pl.BlockSpec((tokens, GROUP * HEAD), lambda h: (0, h))
    return pl.pallas_call(
        _state_kernel,
        grid=(width // (GROUP * HEAD),),
        in_specs=[pl.BlockSpec(memory_space=pltpu.SMEM), spec, spec],
        out_specs=pl.BlockSpec((GROUP * HEAD, HEAD), lambda h: (h, 0)),
        out_shape=jax.ShapeDtypeStruct((width, HEAD), BF),
        compiler_params=pltpu.CompilerParams(vmem_limit_bytes=8 << 20),
        name="local_states",
    )(rate, keys, values)


def _scan_kernel(tokens, heads, rate, states, out):
    blocks, rows, width = states.shape
    mine = lax.axis_index(CTX) * heads // blocks
    lam = jnp.exp(jnp.full((rows, width), -rate[mine] * tokens, F32))
    carry = jnp.zeros((rows, width), F32)
    for b in range(blocks):
        out[b] = carry.astype(BF)
        carry = carry * lam + states[b].astype(F32)


def scan_states(tokens, rate, states):
    return pl.pallas_call(
        functools.partial(_scan_kernel, tokens, rate.shape[0]),
        in_specs=[
            pl.BlockSpec(memory_space=pltpu.SMEM),
            pl.BlockSpec(memory_space=pltpu.VMEM),
        ],
        out_specs=pl.BlockSpec(memory_space=pltpu.VMEM),
        out_shape=jax.ShapeDtypeStruct(states.shape, BF),
        compiler_params=pltpu.CompilerParams(vmem_limit_bytes=6 << 20),
        name="scan_states",
    )(rate, states)


def _intra_kernel(rate, q, k, v, out):
    tokens = q.shape[0]
    first = pl.program_id(0) * GROUP
    i = lax.broadcasted_iota(jnp.int32, (tokens, tokens), 0)
    j = lax.broadcasted_iota(jnp.int32, (tokens, tokens), 1)
    off = (i - j).astype(F32)
    for h in range(GROUP):
        at = slice(h * HEAD, (h + 1) * HEAD)
        r = rate[first + h]
        within = jnp.where(off >= 0.0, jnp.exp(-r * jnp.maximum(off, 0.0)), 0.0)
        scores = lax.dot_general(
            q[:, at], k[:, at], (((1,), (1,)), ((), ())), preferred_element_type=F32
        )
        out[:, at] = jnp.dot(
            (scores * within).astype(BF), v[:, at], preferred_element_type=F32
        )


def intra_part(rate, queries, keys, values):
    tokens, width = keys.shape
    spec = pl.BlockSpec((tokens, GROUP * HEAD), lambda h: (0, h))
    return pl.pallas_call(
        _intra_kernel,
        grid=(width // (GROUP * HEAD),),
        in_specs=[pl.BlockSpec(memory_space=pltpu.SMEM), spec, spec, spec],
        out_specs=spec,
        out_shape=jax.ShapeDtypeStruct((tokens, width), F32),
        compiler_params=pltpu.CompilerParams(vmem_limit_bytes=14 << 20),
        name="intra_part",
    )(rate, queries, keys, values)


def _mix_kernel(rate, intra, q, prefix, mixed, squares):
    tokens = q.shape[0]
    step = pl.program_id(0)
    t = lax.broadcasted_iota(jnp.int32, (tokens, HEAD), 0).astype(F32)
    total = jnp.zeros((tokens, HEAD), F32)
    for h in range(GROUP):
        at = slice(h * HEAD, (h + 1) * HEAD)
        r = rate[step * GROUP + h]
        inter = jnp.dot(q[:, at], prefix[at, :], preferred_element_type=F32)
        value = intra[:, at] + inter * jnp.exp(-r * t)
        mixed[:, at] = value
        total += value * value

    @pl.when(step == 0)
    def _():
        squares[...] = jnp.zeros_like(squares)

    squares[...] += jnp.sum(jnp.transpose(total), axis=0, keepdims=True)


def mix_part(rate, intra, queries, prefix):
    tokens, width = queries.shape
    spec = pl.BlockSpec((tokens, GROUP * HEAD), lambda h: (0, h))
    return pl.pallas_call(
        _mix_kernel,
        grid=(width // (GROUP * HEAD),),
        in_specs=[
            pl.BlockSpec(memory_space=pltpu.SMEM),
            spec,
            spec,
            pl.BlockSpec((GROUP * HEAD, HEAD), lambda h: (h, 0)),
        ],
        out_specs=[spec, pl.BlockSpec((1, tokens), lambda h: (0, 0))],
        out_shape=[
            jax.ShapeDtypeStruct((tokens, width), F32),
            jax.ShapeDtypeStruct((1, tokens), F32),
        ],
        compiler_params=pltpu.CompilerParams(vmem_limit_bytes=14 << 20),
        name="mix_part",
    )(rate, intra, queries, prefix)


def _norm_kernel(features, *refs):
    *squares, mixed, gain, gates, out = refs
    tokens = mixed.shape[0]
    total = sum((part[...] for part in squares[1:]), squares[0][...])
    factor = lax.rsqrt(total / features + 1e-06)
    column = jnp.transpose(jnp.broadcast_to(factor, (HEAD, tokens)))
    for h in range(GROUP):
        at = slice(h * HEAD, (h + 1) * HEAD)
        scaled = mixed[:, at] * column * gain[:, at]
        out[:, at] = (scaled * jax.nn.sigmoid(gates[:, at].astype(F32))).astype(BF)


def norm_part(features, squares, mixed, gain, gates):
    tokens, width = mixed.shape
    spec = pl.BlockSpec((tokens, GROUP * HEAD), lambda h: (0, h))
    row = pl.BlockSpec((1, tokens), lambda h: (0, 0))
    return pl.pallas_call(
        functools.partial(_norm_kernel, features),
        grid=(width // (GROUP * HEAD),),
        in_specs=[row] * len(squares)
        + [spec, pl.BlockSpec((1, GROUP * HEAD), lambda h: (0, h)), spec],
        out_specs=spec,
        out_shape=jax.ShapeDtypeStruct((tokens, width), BF),
        compiler_params=pltpu.CompilerParams(vmem_limit_bytes=14 << 20),
        name="norm_part",
    )(*squares, mixed, gain, gates)


def _pick_kernel(ids, rows, *refs):
    outs, held, into, out_of = refs[:-3], refs[-3], refs[-2], refs[-1]
    n_exp, me_e, me_core = lax.axis_size("exp"), lax.axis_index("exp"), lax.axis_index("core")
    tiles, half = ids.shape[0], TILE // 2
    loads = []
    for k in range(len(outs)):
        target = lax.rem(me_e + k + 1, n_exp)
        seen = jnp.int32(0)
        tile = [jnp.int32(0), jnp.int32(0)]
        for t in range(tiles):
            same = ids[t] == target
            for rank in range(2):
                tile[rank] = jnp.where(same & (seen == rank), t, tile[rank])
            seen = seen + same.astype(jnp.int32)
        for rank in range(2):
            start = pl.multiple_of(tile[rank] * TILE + me_core * half, half)
            load = pltpu.make_async_copy(
                rows.at[pl.ds(start, half), :],
                held.at[k, pl.ds(rank * half, half), :],
                into.at[k, rank],
            )
            load.start()
            loads.append(load)
    stores = []
    for k in range(len(outs)):
        loads[2 * k].wait()
        loads[2 * k + 1].wait()
        store = pltpu.make_async_copy(held.at[k], outs[k], out_of.at[k])
        store.start()
        stores.append(store)
    for store in stores:
        store.wait()


def pick_tiles(ids, rows, count):
    tile = jax.ShapeDtypeStruct((TILE, rows.shape[1]), rows.dtype)
    return pl.pallas_call(
        _pick_kernel,
        in_specs=[
            pl.BlockSpec(memory_space=pltpu.SMEM),
            pl.BlockSpec(memory_space=pl.ANY),
        ],
        out_specs=[pl.BlockSpec(memory_space=pl.ANY)] * count,
        out_shape=[tile] * count,
        scratch_shapes=[
            pltpu.VMEM((count, TILE, rows.shape[1]), rows.dtype),
            pltpu.SemaphoreType.DMA((count, 2)),
            pltpu.SemaphoreType.DMA((count,)),
        ],
        compiler_params=pltpu.CompilerParams(vmem_limit_bytes=58 << 20),
        name="pick_tiles",
    )(ids, rows)


def _hidden_kernel(count, *refs):
    sources, out = refs[: count + 4], refs[count + 4]
    rows, weights, sems = refs[count + 5 :]
    units = weights.shape[0] // 4
    targets = [rows.at[i * TILE : (i + 1) * TILE, :] for i in range(count)]
    targets += [weights.at[i * units : (i + 1) * units, :] for i in range(4)]
    copies = [
        pltpu.make_async_copy(source, target, sems.at[i])
        for i, (source, target) in enumerate(zip(sources, targets))
    ]
    order = list(range(count, count + 4)) + list(range(count))
    for i in order:
        copies[i].start()
    for i in range(4):
        copies[count + i].wait()
    dims = (((1,), (1,)), ((), ()))
    wide = 2 * TILE
    for j in range(count // 2):
        copies[2 * j].wait()
        copies[2 * j + 1].wait()
        at = slice(j * wide, (j + 1) * wide)
        both = lax.dot_general(
            weights[...], rows[at, :], dims, preferred_element_type=F32
        )
        gate, up = both[: 2 * units], both[2 * units :]
        out[:, at] = (jax.nn.silu(gate) * up).astype(BF)


def hidden_part(rows, weights):
    count, (units, model) = len(rows), weights[0].shape
    return pl.pallas_call(
        functools.partial(_hidden_kernel, count),
        in_specs=[pl.BlockSpec(memory_space=pl.ANY)] * (count + 4),
        out_specs=pl.BlockSpec(memory_space=pltpu.VMEM),
        out_shape=jax.ShapeDtypeStruct((2 * units, count * TILE), BF),
        scratch_shapes=[
            pltpu.VMEM((count * TILE, model), BF),
            pltpu.VMEM((4 * units, model), BF),
            pltpu.SemaphoreType.DMA((count + 4,)),
        ],
        compiler_params=pltpu.CompilerParams(vmem_limit_bytes=58 << 20),
        name="hidden_part",
    )(*rows, *weights)


def _split_kernel(n_z, weight, *outs):
    me_x, n_x = lax.axis_index("x"), len(outs)
    units, window = weight.shape[0], weight.shape[1] // n_z
    own = window // n_x
    lane = lax.broadcasted_iota(jnp.int32, (units, window), 1)
    for g in range(n_z // n_x):
        parts = [
            weight[:, z * window : (z + 1) * window].astype(F32)
            for z in range(g * n_x, (g + 1) * n_x)
        ]
        for k, out in enumerate(outs):
            target = lax.rem(me_x + k, n_x)
            total = jnp.zeros((units, window), F32)
            for i, part in enumerate(parts):
                turn = lax.rem(i + n_x - target, n_x) * own
                here = (lane >= i * own) & (lane < (i + 1) * own)
                total = jnp.where(here, pltpu.roll(part, turn, 1), total)
            out[:, g * window : (g + 1) * window] = total.astype(BF)


def split_columns(weight, n_z, n_x):
    units, model = weight.shape
    vmem = pl.BlockSpec(memory_space=pltpu.VMEM)
    return pl.pallas_call(
        functools.partial(_split_kernel, n_z),
        in_specs=[vmem],
        out_specs=[vmem] * n_x,
        out_shape=[jax.ShapeDtypeStruct((units, model // n_x), BF)] * n_x,
        compiler_params=pltpu.CompilerParams(vmem_limit_bytes=14 << 20),
        name="split_columns",
    )(weight)


def _stack_kernel(*refs):
    parts, out, sems = refs[:-2], refs[-2], refs[-1]
    units = parts[0].shape[0]
    copies = [
        pltpu.make_async_copy(part, out.at[i * units : (i + 1) * units, :], sems.at[i])
        for i, part in enumerate(parts)
    ]
    for copy in copies:
        copy.start()
    for copy in copies:
        copy.wait()


def stack_rows(parts):
    units, chunk = parts[0].shape
    return pl.pallas_call(
        _stack_kernel,
        in_specs=[pl.BlockSpec(memory_space=pl.ANY)] * len(parts),
        out_specs=pl.BlockSpec(memory_space=pltpu.VMEM),
        out_shape=jax.ShapeDtypeStruct((len(parts) * units, chunk), BF),
        scratch_shapes=[pltpu.SemaphoreType.DMA((len(parts),))],
        compiler_params=pltpu.CompilerParams(vmem_limit_bytes=10 << 20),
        name="stack_rows",
    )(*parts)


def _down_kernel(weight, *refs):
    hidden, out, held = refs[:-2], refs[-2], refs[-1]
    units = hidden[0].shape[0]
    for k, part in enumerate(hidden):
        held[k * units : (k + 1) * units, :] = part[...]
    blocks, slots, columns = out.shape[:3]
    me_e = lax.axis_index("exp")
    total = lax.dot_general(
        weight[...], held[...], (((0,), (0,)), ((), ())), preferred_element_type=F32
    ).astype(BF)
    for slot in range(slots):
        home = lax.rem(me_e + slots - slot, slots)
        block = total[:, slot * TILE : (slot + 1) * TILE]
        out[:, home] = block.reshape(blocks, columns, TILE)


def down_part(weight, hidden, blocks, columns):
    rows = hidden[0].shape[1]
    vmem = pl.BlockSpec(memory_space=pltpu.VMEM)
    return pl.pallas_call(
        _down_kernel,
        in_specs=[vmem] * (1 + len(hidden)),
        out_specs=vmem,
        out_shape=jax.ShapeDtypeStruct((blocks, rows // TILE, columns, TILE), BF),
        scratch_shapes=[pltpu.VMEM((weight.shape[0], rows), BF)],
        compiler_params=pltpu.CompilerParams(vmem_limit_bytes=24 << 20),
        name="down_part",
    )(weight, *hidden)


def _finish_kernel(ids, parts, weight, out):
    n_z, n_core, n_exp, columns, _ = parts.shape
    tiles, half = ids.shape[0], TILE // 2
    low = lax.broadcasted_iota(jnp.int32, (columns, TILE), 1) < half
    for t in range(tiles):
        rank = jnp.int32(0)
        for earlier in range(t):
            rank = rank + (ids[earlier] == ids[t]).astype(jnp.int32)
        sums = []
        for core in range(n_core):
            total = jnp.zeros((columns, TILE), F32)
            for z in range(n_z):
                total = total + parts[z, core, ids[t]].astype(F32)
            sums.append(total.astype(BF).astype(F32))
        first, second = sums
        zero = jnp.where(low, first, pltpu.roll(second, half, 1))
        one = jnp.where(low, pltpu.roll(first, half, 1), second)
        rows = jnp.where(rank == 0, zero, one)
        at = slice(t * TILE, (t + 1) * TILE)
        out[:, at] = (rows * weight[:, at]).astype(BF)


def finish_part(ids, parts, weight):
    columns = parts.shape[3]
    vmem = pl.BlockSpec(memory_space=pltpu.VMEM)
    return pl.pallas_call(
        _finish_kernel,
        in_specs=[pl.BlockSpec(memory_space=pltpu.SMEM), vmem, vmem],
        out_specs=vmem,
        out_shape=jax.ShapeDtypeStruct((columns, weight.shape[1]), BF),
        compiler_params=pltpu.CompilerParams(vmem_limit_bytes=8 << 20),
        name="finish_part",
    )(ids, parts, weight)


def shift(array, axis, by):
    n = lax.axis_size(axis)
    return lax.ppermute(array, axis, [(i, (i + by) % n) for i in range(n)])


def on_device(
    queries, keys, values, gates, decay_rate, norm_gain,
    moe_rows, tile_expert, row_weight, w_gate, w_up, w_down,
):
    n_exp, n_z = lax.axis_size("exp"), lax.axis_size("z")
    n_x, n_core = lax.axis_size("x"), lax.axis_size("core")
    n_ctx = n_z * n_x * n_core
    tokens, width = queries.shape
    model = moe_rows.shape[1]
    ids = tile_expert[:, 0]
    columns = model // n_ctx

    gate_own = jnp.swapaxes(w_gate[0], 0, 1)
    up_own = jnp.swapaxes(w_up[0], 0, 1)
    gate_other = shift(gate_own, "core", 1)
    up_other = shift(up_own, "core", 1)
    units = gate_own.shape[0]

    picked = pick_tiles(ids, moe_rows, n_exp)
    *picked, keys_late = lax.optimization_barrier((*picked, keys))
    arrived = [picked[-1]]
    arrived += [shift(picked[k - 1], "exp", k) for k in range(1, n_exp)]
    gate_other, up_other, keys_late = lax.optimization_barrier(
        (gate_other, up_other, keys_late)
    )

    states = local_states(decay_rate, keys_late, values)
    states, w_down = lax.optimization_barrier((states, w_down))
    pieces = states.reshape(n_ctx, width // n_ctx, HEAD)
    pieces = lax.all_to_all(pieces, CTX, 0, 0, tiled=True)
    pieces = scan_states(float(tokens), decay_rate, pieces)
    chunks = list(split_columns(w_down[0], n_z, n_x))
    down_own, down_other = [chunks[0]] + [None] * (n_x - 1), [None] * n_x
    lanes = (
        (("x", 1), ("x", 3), ("core", 1), ("core", 3)),
        (("x", 2), ("core", 0), ("core", 2)),
    )
    for lane in lanes:
        last = None
        for axis, k in lane:
            part = chunks[k] if axis == "x" else down_own[k]
            if last is not None and last is not part:
                part, last = lax.optimization_barrier((part, last))
            last = shift(part, axis, k if axis == "x" else 1)
            if axis == "x":
                down_own[k] = last
            else:
                down_other[k] = last
    arrived[LAST], _ = lax.optimization_barrier((arrived[LAST], pieces))

    weights = (gate_own, gate_other, up_own, up_other)
    hidden = hidden_part(arrived, weights)
    hidden, queries = lax.optimization_barrier((hidden, queries))
    hidden = [hidden] + [shift(hidden, "x", k) for k in range(1, n_x)]
    intra = intra_part(decay_rate, queries, keys, values)
    hidden[1], intra = lax.optimization_barrier((hidden[1], intra))
    prefix = lax.all_to_all(pieces, CTX, 0, 0, tiled=True).reshape(width, HEAD)
    down = stack_rows([part for pair in zip(down_own, down_other) for part in pair])
    hidden[2], down = lax.optimization_barrier((hidden[2], down))
    parts = down_part(down, hidden, n_z * n_core, columns)
    parts, prefix = lax.optimization_barrier((parts, prefix))
    parts = parts.reshape(-1, columns, TILE)
    parts = lax.all_to_all(parts, ("z", "core", "exp"), 0, 0, tiled=True)
    parts = parts.reshape(n_z, n_core, n_exp, columns, TILE)

    mixed, squares = mix_part(decay_rate, intra, queries, prefix)
    squares = [lax.psum(squares, "exp")]
    attention_out = norm_part(
        float(width * n_exp), squares, mixed, norm_gain[None, :], gates
    )
    moe_out = jnp.swapaxes(finish_part(ids, parts, row_weight[None, :]), 0, 1)
    return attention_out, moe_out


def solution(mesh):
    n_core, n_x = 2, 4
    grid = mesh.devices.reshape(-1, n_x, n_core, mesh.devices.shape[1])
    fine = Mesh(grid, ("z", "x", "core", "exp"))
    placed = (
        P(CTX, "exp"),
        P(CTX, "exp"),
        P(CTX, "exp"),
        P(CTX, "exp"),
        P("exp"),
        P("exp"),
        P("exp", None),
        P("exp", None),
        P("exp"),
        P("exp", None, CTX),
        P("exp", None, CTX),
        P("exp", CTX, None),
    )
    return jax.shard_map(
        on_device,
        mesh=fine,
        in_specs=placed,
        out_specs=(P(CTX, "exp"), P("exp", CTX)),
        check_vma=False,
    )
```

```python
import functools

import jax
import jax.numpy as jnp
from jax import lax
from jax.experimental import pallas as pl
from jax.experimental.pallas import tpu as pltpu
from jax.sharding import Mesh
from jax.sharding import PartitionSpec as P

BF = jnp.bfloat16
F32 = jnp.float32
CTX = ("z", "x", "core")
HEAD = 128
TILE = 128
GROUP = 4
LAST = 1


def _state_kernel(rate, k, v, out):
    tokens = k.shape[0]
    first = pl.program_id(0) * GROUP
    t = lax.broadcasted_iota(jnp.int32, (tokens, HEAD), 0).astype(F32)
    for h in range(GROUP):
        at = slice(h * HEAD, (h + 1) * HEAD)
        decay = jnp.exp(-rate[first + h] * (tokens - t))
        scaled = (k[:, at].astype(F32) * decay).astype(BF)
        out[at, :] = lax.dot_general(
            scaled, v[:, at], (((0,), (0,)), ((), ())), preferred_element_type=F32
        ).astype(BF)


def local_states(rate, keys, values):
    tokens, width = keys.shape
    spec = pl.BlockSpec((tokens, GROUP * HEAD), lambda h: (0, h))
    return pl.pallas_call(
        _state_kernel,
        grid=(width // (GROUP * HEAD),),
        in_specs=[pl.BlockSpec(memory_space=pltpu.SMEM), spec, spec],
        out_specs=pl.BlockSpec((GROUP * HEAD, HEAD), lambda h: (h, 0)),
        out_shape=jax.ShapeDtypeStruct((width, HEAD), BF),
        compiler_params=pltpu.CompilerParams(vmem_limit_bytes=8 << 20),
        name="local_states",
    )(rate, keys, values)


def _scan_kernel(tokens, heads, rate, states, out):
    blocks, rows, width = states.shape
    mine = lax.axis_index(CTX) * heads // blocks
    lam = jnp.exp(jnp.full((rows, width), -rate[mine] * tokens, F32))
    carry = jnp.zeros((rows, width), F32)
    for b in range(blocks):
        out[b] = carry.astype(BF)
        carry = carry * lam + states[b].astype(F32)


def scan_states(tokens, rate, states):
    return pl.pallas_call(
        functools.partial(_scan_kernel, tokens, rate.shape[0]),
        in_specs=[
            pl.BlockSpec(memory_space=pltpu.SMEM),
            pl.BlockSpec(memory_space=pltpu.VMEM),
        ],
        out_specs=pl.BlockSpec(memory_space=pltpu.VMEM),
        out_shape=jax.ShapeDtypeStruct(states.shape, BF),
        compiler_params=pltpu.CompilerParams(vmem_limit_bytes=6 << 20),
        name="scan_states",
    )(rate, states)


def _intra_kernel(rate, q, k, v, out):
    tokens = q.shape[0]
    first = pl.program_id(0) * GROUP
    i = lax.broadcasted_iota(jnp.int32, (tokens, tokens), 0)
    j = lax.broadcasted_iota(jnp.int32, (tokens, tokens), 1)
    off = (i - j).astype(F32)
    for h in range(GROUP):
        at = slice(h * HEAD, (h + 1) * HEAD)
        r = rate[first + h]
        within = jnp.where(off >= 0.0, jnp.exp(-r * jnp.maximum(off, 0.0)), 0.0)
        scores = lax.dot_general(
            q[:, at], k[:, at], (((1,), (1,)), ((), ())), preferred_element_type=F32
        )
        out[:, at] = jnp.dot(
            (scores * within).astype(BF), v[:, at], preferred_element_type=F32
        )


def intra_part(rate, queries, keys, values):
    tokens, width = keys.shape
    spec = pl.BlockSpec((tokens, GROUP * HEAD), lambda h: (0, h))
    return pl.pallas_call(
        _intra_kernel,
        grid=(width // (GROUP * HEAD),),
        in_specs=[pl.BlockSpec(memory_space=pltpu.SMEM), spec, spec, spec],
        out_specs=spec,
        out_shape=jax.ShapeDtypeStruct((tokens, width), F32),
        compiler_params=pltpu.CompilerParams(vmem_limit_bytes=14 << 20),
        name="intra_part",
    )(rate, queries, keys, values)


def _mix_kernel(rate, intra, q, prefix, mixed, squares):
    tokens = q.shape[0]
    step = pl.program_id(0)
    t = lax.broadcasted_iota(jnp.int32, (tokens, HEAD), 0).astype(F32)
    total = jnp.zeros((tokens, HEAD), F32)
    for h in range(GROUP):
        at = slice(h * HEAD, (h + 1) * HEAD)
        r = rate[step * GROUP + h]
        inter = jnp.dot(q[:, at], prefix[at, :], preferred_element_type=F32)
        value = intra[:, at] + inter * jnp.exp(-r * t)
        mixed[:, at] = value
        total += value * value

    @pl.when(step == 0)
    def _():
        squares[...] = jnp.zeros_like(squares)

    squares[...] += jnp.sum(jnp.transpose(total), axis=0, keepdims=True)


def mix_part(rate, intra, queries, prefix):
    tokens, width = queries.shape
    spec = pl.BlockSpec((tokens, GROUP * HEAD), lambda h: (0, h))
    return pl.pallas_call(
        _mix_kernel,
        grid=(width // (GROUP * HEAD),),
        in_specs=[
            pl.BlockSpec(memory_space=pltpu.SMEM),
            spec,
            spec,
            pl.BlockSpec((GROUP * HEAD, HEAD), lambda h: (h, 0)),
        ],
        out_specs=[spec, pl.BlockSpec((1, tokens), lambda h: (0, 0))],
        out_shape=[
            jax.ShapeDtypeStruct((tokens, width), F32),
            jax.ShapeDtypeStruct((1, tokens), F32),
        ],
        compiler_params=pltpu.CompilerParams(vmem_limit_bytes=14 << 20),
        name="mix_part",
    )(rate, intra, queries, prefix)


def _norm_kernel(features, *refs):
    *squares, mixed, gain, gates, out = refs
    tokens = mixed.shape[0]
    total = sum((part[...] for part in squares[1:]), squares[0][...])
    factor = lax.rsqrt(total / features + 1e-06)
    column = jnp.transpose(jnp.broadcast_to(factor, (HEAD, tokens)))
    for h in range(GROUP):
        at = slice(h * HEAD, (h + 1) * HEAD)
        scaled = mixed[:, at] * column * gain[:, at]
        out[:, at] = (scaled * jax.nn.sigmoid(gates[:, at].astype(F32))).astype(BF)


def norm_part(features, squares, mixed, gain, gates):
    tokens, width = mixed.shape
    spec = pl.BlockSpec((tokens, GROUP * HEAD), lambda h: (0, h))
    row = pl.BlockSpec((1, tokens), lambda h: (0, 0))
    return pl.pallas_call(
        functools.partial(_norm_kernel, features),
        grid=(width // (GROUP * HEAD),),
        in_specs=[row] * len(squares)
        + [spec, pl.BlockSpec((1, GROUP * HEAD), lambda h: (0, h)), spec],
        out_specs=spec,
        out_shape=jax.ShapeDtypeStruct((tokens, width), BF),
        compiler_params=pltpu.CompilerParams(vmem_limit_bytes=14 << 20),
        name="norm_part",
    )(*squares, mixed, gain, gates)


def _pick_kernel(ids, rows, *refs):
    outs, held, into, out_of = refs[:-3], refs[-3], refs[-2], refs[-1]
    n_exp, me_e, me_core = lax.axis_size("exp"), lax.axis_index("exp"), lax.axis_index("core")
    tiles, half = ids.shape[0], TILE // 2
    loads = []
    for k in range(len(outs)):
        target = lax.rem(me_e + k + 1, n_exp)
        seen = jnp.int32(0)
        tile = [jnp.int32(0), jnp.int32(0)]
        for t in range(tiles):
            same = ids[t] == target
            for rank in range(2):
                tile[rank] = jnp.where(same & (seen == rank), t, tile[rank])
            seen = seen + same.astype(jnp.int32)
        for rank in range(2):
            start = pl.multiple_of(tile[rank] * TILE + me_core * half, half)
            load = pltpu.make_async_copy(
                rows.at[pl.ds(start, half), :],
                held.at[k, pl.ds(rank * half, half), :],
                into.at[k, rank],
            )
            load.start()
            loads.append(load)
    stores = []
    for k in range(len(outs)):
        loads[2 * k].wait()
        loads[2 * k + 1].wait()
        store = pltpu.make_async_copy(held.at[k], outs[k], out_of.at[k])
        store.start()
        stores.append(store)
    for store in stores:
        store.wait()


def pick_tiles(ids, rows, count):
    tile = jax.ShapeDtypeStruct((TILE, rows.shape[1]), rows.dtype)
    return pl.pallas_call(
        _pick_kernel,
        in_specs=[
            pl.BlockSpec(memory_space=pltpu.SMEM),
            pl.BlockSpec(memory_space=pl.ANY),
        ],
        out_specs=[pl.BlockSpec(memory_space=pl.ANY)] * count,
        out_shape=[tile] * count,
        scratch_shapes=[
            pltpu.VMEM((count, TILE, rows.shape[1]), rows.dtype),
            pltpu.SemaphoreType.DMA((count, 2)),
            pltpu.SemaphoreType.DMA((count,)),
        ],
        compiler_params=pltpu.CompilerParams(vmem_limit_bytes=58 << 20),
        name="pick_tiles",
    )(ids, rows)


def _turn_kernel(gate_own, gate_other, up_own, up_other, out, held):
    units, half = gate_own.shape[0], held.shape[0] // 2
    held[...] = jnp.zeros_like(held)
    for i, part in enumerate((gate_own, gate_other)):
        held[i * units : (i + 1) * units, :] = part[...]
    for i, part in enumerate((up_own, up_other)):
        at = half + i * units
        held[at : at + units, :] = part[...]
    out[...] = jnp.transpose(held[...])


def turn_weights(weights):
    units, model = weights[0].shape
    half = -(-2 * units // HEAD) * HEAD
    step = 512
    return pl.pallas_call(
        _turn_kernel,
        grid=(model // step,),
        in_specs=[pl.BlockSpec((units, step), lambda i: (0, i))] * 4,
        out_specs=pl.BlockSpec((step, 2 * half), lambda i: (i, 0)),
        out_shape=jax.ShapeDtypeStruct((model, 2 * half), BF),
        scratch_shapes=[pltpu.VMEM((2 * half, step), BF)],
        compiler_params=pltpu.CompilerParams(vmem_limit_bytes=58 << 20),
        name="turn_weights",
    )(*weights)


def _hidden_kernel(count, cuts, *refs):
    sources, weight, out, rows, held, sems = refs[:count], *refs[count:]
    deep = held.shape[0] // cuts
    copies = []
    for i, source in enumerate(sources):
        target = rows.at[i * TILE : (i + 1) * TILE, :]
        copies.append(pltpu.make_async_copy(source, target, sems.at[i]))
    for i in range(cuts):
        at = slice(i * deep, (i + 1) * deep)
        copies.append(
            pltpu.make_async_copy(weight.at[at, :], held.at[at, :], sems.at[count + i])
        )
    for copy in copies:
        copy.start()
    for copy in copies[:count]:
        copy.wait()
    both = None
    for i in range(cuts):
        copies[count + i].wait()
        at = slice(i * deep, (i + 1) * deep)
        term = jnp.dot(rows[:, at], held[at, :], preferred_element_type=F32)
        both = term if both is None else both + term
    half, units = held.shape[1] // 2, out.shape[0]
    value = (jax.nn.silu(both[:, :half]) * both[:, half:]).astype(BF)
    out[...] = jnp.transpose(value)[:units]


def hidden_part(rows, weight, units):
    count, (model, wide), cuts = len(rows), weight.shape, 4
    return pl.pallas_call(
        functools.partial(_hidden_kernel, count, cuts),
        in_specs=[pl.BlockSpec(memory_space=pl.ANY)] * (count + 1),
        out_specs=pl.BlockSpec(memory_space=pltpu.VMEM),
        out_shape=jax.ShapeDtypeStruct((units, count * TILE), BF),
        scratch_shapes=[
            pltpu.VMEM((count * TILE, model), BF),
            pltpu.VMEM((model, wide), BF),
            pltpu.SemaphoreType.DMA((count + cuts,)),
        ],
        compiler_params=pltpu.CompilerParams(vmem_limit_bytes=58 << 20),
        name="hidden_part",
    )(*rows, weight)


def _split_kernel(n_z, weight, *outs):
    me_x, n_x = lax.axis_index("x"), len(outs)
    units, window = weight.shape[0], weight.shape[1] // n_z
    own = window // n_x
    lane = lax.broadcasted_iota(jnp.int32, (units, window), 1)
    for g in range(n_z // n_x):
        parts = [
            weight[:, z * window : (z + 1) * window].astype(F32)
            for z in range(g * n_x, (g + 1) * n_x)
        ]
        for k, out in enumerate(outs):
            target = lax.rem(me_x + k, n_x)
            total = jnp.zeros((units, window), F32)
            for i, part in enumerate(parts):
                turn = lax.rem(i + n_x - target, n_x) * own
                here = (lane >= i * own) & (lane < (i + 1) * own)
                total = jnp.where(here, pltpu.roll(part, turn, 1), total)
            out[:, g * window : (g + 1) * window] = total.astype(BF)


def split_columns(weight, n_z, n_x):
    units, model = weight.shape
    vmem = pl.BlockSpec(memory_space=pltpu.VMEM)
    return pl.pallas_call(
        functools.partial(_split_kernel, n_z),
        in_specs=[vmem],
        out_specs=[vmem] * n_x,
        out_shape=[jax.ShapeDtypeStruct((units, model // n_x), BF)] * n_x,
        compiler_params=pltpu.CompilerParams(vmem_limit_bytes=14 << 20),
        name="split_columns",
    )(weight)


def _stack_kernel(*refs):
    parts, out, sems = refs[:-2], refs[-2], refs[-1]
    units = parts[0].shape[0]
    copies = [
        pltpu.make_async_copy(part, out.at[i * units : (i + 1) * units, :], sems.at[i])
        for i, part in enumerate(parts)
    ]
    for copy in copies:
        copy.start()
    for copy in copies:
        copy.wait()


def stack_rows(parts):
    units, chunk = parts[0].shape
    return pl.pallas_call(
        _stack_kernel,
        in_specs=[pl.BlockSpec(memory_space=pl.ANY)] * len(parts),
        out_specs=pl.BlockSpec(memory_space=pltpu.VMEM),
        out_shape=jax.ShapeDtypeStruct((len(parts) * units, chunk), BF),
        scratch_shapes=[pltpu.SemaphoreType.DMA((len(parts),))],
        compiler_params=pltpu.CompilerParams(vmem_limit_bytes=10 << 20),
        name="stack_rows",
    )(*parts)


def _down_kernel(weight, *refs):
    hidden, out, held = refs[:-2], refs[-2], refs[-1]
    units = hidden[0].shape[0]
    for k, part in enumerate(hidden):
        held[k * units : (k + 1) * units, :] = part[...]
    blocks, slots, columns = out.shape[:3]
    me_e = lax.axis_index("exp")
    total = lax.dot_general(
        weight[...], held[...], (((0,), (0,)), ((), ())), preferred_element_type=F32
    ).astype(BF)
    for slot in range(slots):
        home = lax.rem(me_e + slots - slot, slots)
        block = total[:, slot * TILE : (slot + 1) * TILE]
        out[:, home] = block.reshape(blocks, columns, TILE)


def down_part(weight, hidden, blocks, columns):
    rows = hidden[0].shape[1]
    vmem = pl.BlockSpec(memory_space=pltpu.VMEM)
    return pl.pallas_call(
        _down_kernel,
        in_specs=[vmem] * (1 + len(hidden)),
        out_specs=vmem,
        out_shape=jax.ShapeDtypeStruct((blocks, rows // TILE, columns, TILE), BF),
        scratch_shapes=[pltpu.VMEM((weight.shape[0], rows), BF)],
        compiler_params=pltpu.CompilerParams(vmem_limit_bytes=24 << 20),
        name="down_part",
    )(weight, *hidden)


def _finish_kernel(ids, parts, weight, out):
    n_z, n_core, n_exp, columns, _ = parts.shape
    tiles, half = ids.shape[0], TILE // 2
    low = lax.broadcasted_iota(jnp.int32, (columns, TILE), 1) < half
    for t in range(tiles):
        rank = jnp.int32(0)
        for earlier in range(t):
            rank = rank + (ids[earlier] == ids[t]).astype(jnp.int32)
        sums = []
        for core in range(n_core):
            total = jnp.zeros((columns, TILE), F32)
            for z in range(n_z):
                total = total + parts[z, core, ids[t]].astype(F32)
            sums.append(total.astype(BF).astype(F32))
        first, second = sums
        zero = jnp.where(low, first, pltpu.roll(second, half, 1))
        one = jnp.where(low, pltpu.roll(first, half, 1), second)
        rows = jnp.where(rank == 0, zero, one)
        at = slice(t * TILE, (t + 1) * TILE)
        out[:, at] = (rows * weight[:, at]).astype(BF)


def finish_part(ids, parts, weight):
    columns = parts.shape[3]
    vmem = pl.BlockSpec(memory_space=pltpu.VMEM)
    return pl.pallas_call(
        _finish_kernel,
        in_specs=[pl.BlockSpec(memory_space=pltpu.SMEM), vmem, vmem],
        out_specs=vmem,
        out_shape=jax.ShapeDtypeStruct((columns, weight.shape[1]), BF),
        compiler_params=pltpu.CompilerParams(vmem_limit_bytes=8 << 20),
        name="finish_part",
    )(ids, parts, weight)


def shift(array, axis, by):
    n = lax.axis_size(axis)
    return lax.ppermute(array, axis, [(i, (i + by) % n) for i in range(n)])


def on_device(
    queries, keys, values, gates, decay_rate, norm_gain,
    moe_rows, tile_expert, row_weight, w_gate, w_up, w_down,
):
    n_exp, n_z = lax.axis_size("exp"), lax.axis_size("z")
    n_x, n_core = lax.axis_size("x"), lax.axis_size("core")
    n_ctx = n_z * n_x * n_core
    tokens, width = queries.shape
    model = moe_rows.shape[1]
    ids = tile_expert[:, 0]
    columns = model // n_ctx

    gate_own = jnp.swapaxes(w_gate[0], 0, 1)
    up_own = jnp.swapaxes(w_up[0], 0, 1)
    gate_other = shift(gate_own, "core", 1)
    up_other = shift(up_own, "core", 1)
    units = gate_own.shape[0]

    picked = pick_tiles(ids, moe_rows, n_exp)
    *picked, keys_late = lax.optimization_barrier((*picked, keys))
    arrived = [picked[-1]]
    arrived += [shift(picked[k - 1], "exp", k) for k in range(1, n_exp)]
    gate_other, up_other, keys_late = lax.optimization_barrier(
        (gate_other, up_other, keys_late)
    )

    states = local_states(decay_rate, keys_late, values)
    states, w_down = lax.optimization_barrier((states, w_down))
    pieces = states.reshape(n_ctx, width // n_ctx, HEAD)
    pieces = lax.all_to_all(pieces, CTX, 0, 0, tiled=True)
    chunks = list(split_columns(w_down[0], n_z, n_x))
    gate_other, _ = lax.optimization_barrier((gate_other, chunks[0]))
    turned = turn_weights((gate_own, gate_other, up_own, up_other))
    chunks[3], _ = lax.optimization_barrier((chunks[3], turned))
    pieces, _ = lax.optimization_barrier((pieces, turned))
    pieces = scan_states(float(tokens), decay_rate, pieces)
    down_own, down_other = [chunks[0]] + [None] * (n_x - 1), [None] * n_x
    lanes = (
        (("x", 1), ("x", 3), ("core", 1), ("core", 3)),
        (("x", 2), ("core", 0), ("core", 2)),
    )
    for lane in lanes:
        last = None
        for axis, k in lane:
            part = chunks[k] if axis == "x" else down_own[k]
            if last is not None and last is not part:
                part, last = lax.optimization_barrier((part, last))
            last = shift(part, axis, k if axis == "x" else 1)
            if axis == "x":
                down_own[k] = last
            else:
                down_other[k] = last
    arrived[LAST], _ = lax.optimization_barrier((arrived[LAST], pieces))

    hidden = hidden_part(arrived, turned, 2 * units)
    hidden, queries = lax.optimization_barrier((hidden, queries))
    hidden = [hidden] + [shift(hidden, "x", k) for k in range(1, n_x)]
    intra = intra_part(decay_rate, queries, keys, values)
    hidden[1], intra = lax.optimization_barrier((hidden[1], intra))
    prefix = lax.all_to_all(pieces, CTX, 0, 0, tiled=True).reshape(width, HEAD)
    down = stack_rows([part for pair in zip(down_own, down_other) for part in pair])
    hidden[2], down = lax.optimization_barrier((hidden[2], down))
    parts = down_part(down, hidden, n_z * n_core, columns)
    parts, prefix = lax.optimization_barrier((parts, prefix))
    parts = parts.reshape(-1, columns, TILE)
    parts = lax.all_to_all(parts, ("z", "core", "exp"), 0, 0, tiled=True)
    parts = parts.reshape(n_z, n_core, n_exp, columns, TILE)

    mixed, squares = mix_part(decay_rate, intra, queries, prefix)
    squares = [lax.psum(squares, "exp")]
    attention_out = norm_part(
        float(width * n_exp), squares, mixed, norm_gain[None, :], gates
    )
    moe_out = jnp.swapaxes(finish_part(ids, parts, row_weight[None, :]), 0, 1)
    return attention_out, moe_out


def solution(mesh):
    n_core, n_x = 2, 4
    grid = mesh.devices.reshape(-1, n_x, n_core, mesh.devices.shape[1])
    fine = Mesh(grid, ("z", "x", "core", "exp"))
    placed = (
        P(CTX, "exp"),
        P(CTX, "exp"),
        P(CTX, "exp"),
        P(CTX, "exp"),
        P("exp"),
        P("exp"),
        P("exp", None),
        P("exp", None),
        P("exp"),
        P("exp", None, CTX),
        P("exp", None, CTX),
        P("exp", CTX, None),
    )
    return jax.shard_map(
        on_device,
        mesh=fine,
        in_specs=placed,
        out_specs=(P(CTX, "exp"), P("exp", CTX)),
        check_vma=False,
    )
```

```python
import functools

import jax
import jax.numpy as jnp
from jax import lax
from jax.experimental import pallas as pl
from jax.experimental.pallas import tpu as pltpu
from jax.sharding import Mesh
from jax.sharding import PartitionSpec as P

BF = jnp.bfloat16
F32 = jnp.float32
CTX = ("z", "x", "core")
HEAD = 128
TILE = 128
GROUP = 4
LAST = 1


def _state_kernel(rate, k, v, out):
    tokens = k.shape[0]
    first = pl.program_id(0) * GROUP
    t = lax.broadcasted_iota(jnp.int32, (tokens, HEAD), 0).astype(F32)
    for h in range(GROUP):
        at = slice(h * HEAD, (h + 1) * HEAD)
        decay = jnp.exp(-rate[first + h] * (tokens - t))
        scaled = (k[:, at].astype(F32) * decay).astype(BF)
        out[at, :] = lax.dot_general(
            scaled, v[:, at], (((0,), (0,)), ((), ())), preferred_element_type=F32
        ).astype(BF)


def local_states(rate, keys, values):
    tokens, width = keys.shape
    spec = pl.BlockSpec((tokens, GROUP * HEAD), lambda h: (0, h))
    return pl.pallas_call(
        _state_kernel,
        grid=(width // (GROUP * HEAD),),
        in_specs=[pl.BlockSpec(memory_space=pltpu.SMEM), spec, spec],
        out_specs=pl.BlockSpec((GROUP * HEAD, HEAD), lambda h: (h, 0)),
        out_shape=jax.ShapeDtypeStruct((width, HEAD), BF),
        compiler_params=pltpu.CompilerParams(vmem_limit_bytes=8 << 20),
        name="local_states",
    )(rate, keys, values)


def _scan_kernel(tokens, heads, rate, states, out):
    blocks, rows, width = states.shape
    mine = lax.axis_index(CTX) * heads // blocks
    lam = jnp.exp(jnp.full((rows, width), -rate[mine] * tokens, F32))
    carry = jnp.zeros((rows, width), F32)
    for b in range(blocks):
        out[b] = carry.astype(BF)
        carry = carry * lam + states[b].astype(F32)


def scan_states(tokens, rate, states):
    return pl.pallas_call(
        functools.partial(_scan_kernel, tokens, rate.shape[0]),
        in_specs=[
            pl.BlockSpec(memory_space=pltpu.SMEM),
            pl.BlockSpec(memory_space=pltpu.VMEM),
        ],
        out_specs=pl.BlockSpec(memory_space=pltpu.VMEM),
        out_shape=jax.ShapeDtypeStruct(states.shape, BF),
        compiler_params=pltpu.CompilerParams(vmem_limit_bytes=6 << 20),
        name="scan_states",
    )(rate, states)


def _intra_kernel(rate, q, k, v, out):
    tokens = q.shape[0]
    first = pl.program_id(0) * GROUP
    i = lax.broadcasted_iota(jnp.int32, (tokens, tokens), 0)
    j = lax.broadcasted_iota(jnp.int32, (tokens, tokens), 1)
    off = (i - j).astype(F32)
    for h in range(GROUP):
        at = slice(h * HEAD, (h + 1) * HEAD)
        r = rate[first + h]
        within = jnp.where(off >= 0.0, jnp.exp(-r * jnp.maximum(off, 0.0)), 0.0)
        scores = lax.dot_general(
            q[:, at], k[:, at], (((1,), (1,)), ((), ())), preferred_element_type=F32
        )
        out[:, at] = jnp.dot(
            (scores * within).astype(BF), v[:, at], preferred_element_type=F32
        )


def intra_part(rate, queries, keys, values):
    tokens, width = keys.shape
    spec = pl.BlockSpec((tokens, GROUP * HEAD), lambda h: (0, h))
    return pl.pallas_call(
        _intra_kernel,
        grid=(width // (GROUP * HEAD),),
        in_specs=[pl.BlockSpec(memory_space=pltpu.SMEM), spec, spec, spec],
        out_specs=spec,
        out_shape=jax.ShapeDtypeStruct((tokens, width), F32),
        compiler_params=pltpu.CompilerParams(vmem_limit_bytes=14 << 20),
        name="intra_part",
    )(rate, queries, keys, values)


def _mix_kernel(rate, intra, q, prefix, mixed, squares):
    tokens = q.shape[0]
    step = pl.program_id(0)
    t = lax.broadcasted_iota(jnp.int32, (tokens, HEAD), 0).astype(F32)
    total = jnp.zeros((tokens, HEAD), F32)
    for h in range(GROUP):
        at = slice(h * HEAD, (h + 1) * HEAD)
        r = rate[step * GROUP + h]
        inter = jnp.dot(q[:, at], prefix[at, :], preferred_element_type=F32)
        value = intra[:, at] + inter * jnp.exp(-r * t)
        mixed[:, at] = value
        total += value * value

    @pl.when(step == 0)
    def _():
        squares[...] = jnp.zeros_like(squares)

    squares[...] += jnp.sum(jnp.transpose(total), axis=0, keepdims=True)


def mix_part(rate, intra, queries, prefix):
    tokens, width = queries.shape
    spec = pl.BlockSpec((tokens, GROUP * HEAD), lambda h: (0, h))
    return pl.pallas_call(
        _mix_kernel,
        grid=(width // (GROUP * HEAD),),
        in_specs=[
            pl.BlockSpec(memory_space=pltpu.SMEM),
            spec,
            spec,
            pl.BlockSpec((GROUP * HEAD, HEAD), lambda h: (h, 0)),
        ],
        out_specs=[spec, pl.BlockSpec((1, tokens), lambda h: (0, 0))],
        out_shape=[
            jax.ShapeDtypeStruct((tokens, width), F32),
            jax.ShapeDtypeStruct((1, tokens), F32),
        ],
        compiler_params=pltpu.CompilerParams(vmem_limit_bytes=14 << 20),
        name="mix_part",
    )(rate, intra, queries, prefix)


def _norm_kernel(features, *refs):
    *squares, mixed, gain, gates, out = refs
    tokens = mixed.shape[0]
    total = sum((part[...] for part in squares[1:]), squares[0][...])
    factor = lax.rsqrt(total / features + 1e-06)
    column = jnp.transpose(jnp.broadcast_to(factor, (HEAD, tokens)))
    for h in range(GROUP):
        at = slice(h * HEAD, (h + 1) * HEAD)
        scaled = mixed[:, at] * column * gain[:, at]
        out[:, at] = (scaled * jax.nn.sigmoid(gates[:, at].astype(F32))).astype(BF)


def norm_part(features, squares, mixed, gain, gates):
    tokens, width = mixed.shape
    spec = pl.BlockSpec((tokens, GROUP * HEAD), lambda h: (0, h))
    row = pl.BlockSpec((1, tokens), lambda h: (0, 0))
    return pl.pallas_call(
        functools.partial(_norm_kernel, features),
        grid=(width // (GROUP * HEAD),),
        in_specs=[row] * len(squares)
        + [spec, pl.BlockSpec((1, GROUP * HEAD), lambda h: (0, h)), spec],
        out_specs=spec,
        out_shape=jax.ShapeDtypeStruct((tokens, width), BF),
        compiler_params=pltpu.CompilerParams(vmem_limit_bytes=14 << 20),
        name="norm_part",
    )(*squares, mixed, gain, gates)


def _pick_kernel(ids, rows, *refs):
    outs, held, into, out_of = refs[:-3], refs[-3], refs[-2], refs[-1]
    n_exp, me_e, me_core = lax.axis_size("exp"), lax.axis_index("exp"), lax.axis_index("core")
    tiles, half = ids.shape[0], TILE // 2
    loads = []
    for k in range(len(outs)):
        target = lax.rem(me_e + k + 1, n_exp)
        seen = jnp.int32(0)
        tile = [jnp.int32(0), jnp.int32(0)]
        for t in range(tiles):
            same = ids[t] == target
            for rank in range(2):
                tile[rank] = jnp.where(same & (seen == rank), t, tile[rank])
            seen = seen + same.astype(jnp.int32)
        for rank in range(2):
            start = pl.multiple_of(tile[rank] * TILE + me_core * half, half)
            load = pltpu.make_async_copy(
                rows.at[pl.ds(start, half), :],
                held.at[k, pl.ds(rank * half, half), :],
                into.at[k, rank],
            )
            load.start()
            loads.append(load)
    stores = []
    for k in range(len(outs)):
        loads[2 * k].wait()
        loads[2 * k + 1].wait()
        store = pltpu.make_async_copy(held.at[k], outs[k], out_of.at[k])
        store.start()
        stores.append(store)
    for store in stores:
        store.wait()


def pick_tiles(ids, rows, count):
    tile = jax.ShapeDtypeStruct((TILE, rows.shape[1]), rows.dtype)
    return pl.pallas_call(
        _pick_kernel,
        in_specs=[
            pl.BlockSpec(memory_space=pltpu.SMEM),
            pl.BlockSpec(memory_space=pl.ANY),
        ],
        out_specs=[pl.BlockSpec(memory_space=pl.ANY)] * count,
        out_shape=[tile] * count,
        scratch_shapes=[
            pltpu.VMEM((count, TILE, rows.shape[1]), rows.dtype),
            pltpu.SemaphoreType.DMA((count, 2)),
            pltpu.SemaphoreType.DMA((count,)),
        ],
        compiler_params=pltpu.CompilerParams(vmem_limit_bytes=58 << 20),
        name="pick_tiles",
    )(ids, rows)


def _hidden_kernel(count, *refs):
    sources, out = refs[: count + 4], refs[count + 4]
    rows, weights, sems = refs[count + 5 :]
    units = weights.shape[0] // 4
    targets = [rows.at[i * TILE : (i + 1) * TILE, :] for i in range(count)]
    targets += [weights.at[i * units : (i + 1) * units, :] for i in range(4)]
    copies = [
        pltpu.make_async_copy(source, target, sems.at[i])
        for i, (source, target) in enumerate(zip(sources, targets))
    ]
    order = list(range(count, count + 4)) + list(range(count))
    for i in order:
        copies[i].start()
    for i in range(4):
        copies[count + i].wait()
    dims = (((1,), (1,)), ((), ()))
    wide = 2 * TILE
    for j in range(count // 2):
        copies[2 * j].wait()
        copies[2 * j + 1].wait()
        at = slice(j * wide, (j + 1) * wide)
        both = lax.dot_general(
            weights[...], rows[at, :], dims, preferred_element_type=F32
        )
        gate, up = both[: 2 * units], both[2 * units :]
        out[:, at] = (jax.nn.silu(gate) * up).astype(BF)


def hidden_part(rows, weights):
    count, (units, model) = len(rows), weights[0].shape
    return pl.pallas_call(
        functools.partial(_hidden_kernel, count),
        in_specs=[pl.BlockSpec(memory_space=pl.ANY)] * (count + 4),
        out_specs=pl.BlockSpec(memory_space=pltpu.VMEM),
        out_shape=jax.ShapeDtypeStruct((2 * units, count * TILE), BF),
        scratch_shapes=[
            pltpu.VMEM((count * TILE, model), BF),
            pltpu.VMEM((4 * units, model), BF),
            pltpu.SemaphoreType.DMA((count + 4,)),
        ],
        compiler_params=pltpu.CompilerParams(vmem_limit_bytes=58 << 20),
        name="hidden_part",
    )(*rows, *weights)


def _split_kernel(n_z, weight, *outs):
    me_x, n_x = lax.axis_index("x"), len(outs)
    units, window = weight.shape[0], weight.shape[1] // n_z
    own = window // n_x
    lane = lax.broadcasted_iota(jnp.int32, (units, window), 1)
    for g in range(n_z // n_x):
        parts = [
            weight[:, z * window : (z + 1) * window].astype(F32)
            for z in range(g * n_x, (g + 1) * n_x)
        ]
        for k, out in enumerate(outs):
            target = lax.rem(me_x + k, n_x)
            total = jnp.zeros((units, window), F32)
            for i, part in enumerate(parts):
                turn = lax.rem(i + n_x - target, n_x) * own
                here = (lane >= i * own) & (lane < (i + 1) * own)
                total = jnp.where(here, pltpu.roll(part, turn, 1), total)
            out[:, g * window : (g + 1) * window] = total.astype(BF)


def split_columns(weight, n_z, n_x):
    units, model = weight.shape
    vmem = pl.BlockSpec(memory_space=pltpu.VMEM)
    return pl.pallas_call(
        functools.partial(_split_kernel, n_z),
        in_specs=[vmem],
        out_specs=[vmem] * n_x,
        out_shape=[jax.ShapeDtypeStruct((units, model // n_x), BF)] * n_x,
        compiler_params=pltpu.CompilerParams(vmem_limit_bytes=14 << 20),
        name="split_columns",
    )(weight)


def _stack_kernel(*refs):
    parts, out, sems = refs[:-2], refs[-2], refs[-1]
    units = parts[0].shape[0]
    copies = [
        pltpu.make_async_copy(part, out.at[i * units : (i + 1) * units, :], sems.at[i])
        for i, part in enumerate(parts)
    ]
    for copy in copies:
        copy.start()
    for copy in copies:
        copy.wait()


def stack_rows(parts):
    units, chunk = parts[0].shape
    return pl.pallas_call(
        _stack_kernel,
        in_specs=[pl.BlockSpec(memory_space=pl.ANY)] * len(parts),
        out_specs=pl.BlockSpec(memory_space=pltpu.VMEM),
        out_shape=jax.ShapeDtypeStruct((len(parts) * units, chunk), BF),
        scratch_shapes=[pltpu.SemaphoreType.DMA((len(parts),))],
        compiler_params=pltpu.CompilerParams(vmem_limit_bytes=10 << 20),
        name="stack_rows",
    )(*parts)


def _down_kernel(weight, *refs):
    hidden, out, held = refs[:-2], refs[-2], refs[-1]
    units = hidden[0].shape[0]
    for k, part in enumerate(hidden):
        held[k * units : (k + 1) * units, :] = part[...]
    blocks, slots, columns = out.shape[:3]
    me_e = lax.axis_index("exp")
    total = lax.dot_general(
        weight[...], held[...], (((0,), (0,)), ((), ())), preferred_element_type=F32
    ).astype(BF)
    for slot in range(slots):
        home = lax.rem(me_e + slots - slot, slots)
        block = total[:, slot * TILE : (slot + 1) * TILE]
        out[:, home] = block.reshape(blocks, columns, TILE)


def down_part(weight, hidden, blocks, columns):
    rows = hidden[0].shape[1]
    vmem = pl.BlockSpec(memory_space=pltpu.VMEM)
    return pl.pallas_call(
        _down_kernel,
        in_specs=[vmem] * (1 + len(hidden)),
        out_specs=vmem,
        out_shape=jax.ShapeDtypeStruct((blocks, rows // TILE, columns, TILE), BF),
        scratch_shapes=[pltpu.VMEM((weight.shape[0], rows), BF)],
        compiler_params=pltpu.CompilerParams(vmem_limit_bytes=24 << 20),
        name="down_part",
    )(weight, *hidden)


def _finish_kernel(ids, parts, weight, out):
    n_z, n_core, n_exp, columns, _ = parts.shape
    tiles, half = ids.shape[0], TILE // 2
    low = lax.broadcasted_iota(jnp.int32, (columns, TILE), 1) < half
    for t in range(tiles):
        rank = jnp.int32(0)
        for earlier in range(t):
            rank = rank + (ids[earlier] == ids[t]).astype(jnp.int32)
        sums = []
        for core in range(n_core):
            total = jnp.zeros((columns, TILE), F32)
            for z in range(n_z):
                total = total + parts[z, core, ids[t]].astype(F32)
            sums.append(total.astype(BF).astype(F32))
        first, second = sums
        zero = jnp.where(low, first, pltpu.roll(second, half, 1))
        one = jnp.where(low, pltpu.roll(first, half, 1), second)
        rows = jnp.where(rank == 0, zero, one)
        at = slice(t * TILE, (t + 1) * TILE)
        out[:, at] = (rows * weight[:, at]).astype(BF)


def finish_part(ids, parts, weight):
    columns = parts.shape[3]
    vmem = pl.BlockSpec(memory_space=pltpu.VMEM)
    return pl.pallas_call(
        _finish_kernel,
        in_specs=[pl.BlockSpec(memory_space=pltpu.SMEM), vmem, vmem],
        out_specs=vmem,
        out_shape=jax.ShapeDtypeStruct((columns, weight.shape[1]), BF),
        compiler_params=pltpu.CompilerParams(vmem_limit_bytes=8 << 20),
        name="finish_part",
    )(ids, parts, weight)


def shift(array, axis, by):
    n = lax.axis_size(axis)
    return lax.ppermute(array, axis, [(i, (i + by) % n) for i in range(n)])


def on_device(
    queries, keys, values, gates, decay_rate, norm_gain,
    moe_rows, tile_expert, row_weight, w_gate, w_up, w_down,
):
    n_exp, n_z = lax.axis_size("exp"), lax.axis_size("z")
    n_x, n_core = lax.axis_size("x"), lax.axis_size("core")
    n_ctx = n_z * n_x * n_core
    tokens, width = queries.shape
    model = moe_rows.shape[1]
    ids = tile_expert[:, 0]
    columns = model // n_ctx

    gate_own = jnp.swapaxes(w_gate[0], 0, 1)
    up_own = jnp.swapaxes(w_up[0], 0, 1)
    gate_other = shift(gate_own, "core", 1)
    up_other = shift(up_own, "core", 1)
    units = gate_own.shape[0]

    picked = pick_tiles(ids, moe_rows, n_exp)
    *picked, keys_late = lax.optimization_barrier((*picked, keys))
    arrived = [picked[-1]]
    arrived += [shift(picked[k - 1], "exp", k) for k in range(1, n_exp)]
    gate_other, up_other, keys_late = lax.optimization_barrier(
        (gate_other, up_other, keys_late)
    )

    states = local_states(decay_rate, keys_late, values)
    states, w_down = lax.optimization_barrier((states, w_down))
    pieces = states.reshape(n_ctx, width // n_ctx, HEAD)
    pieces = lax.all_to_all(pieces, CTX, 0, 0, tiled=True)
    pieces = scan_states(float(tokens), decay_rate, pieces)
    chunks = list(split_columns(w_down[0], n_z, n_x))
    down_own, down_other = [chunks[0]] + [None] * (n_x - 1), [None] * n_x
    lanes = (
        (("x", 1), ("x", 3), ("core", 1), ("core", 3)),
        (("x", 2), ("core", 0), ("core", 2)),
    )
    for lane in lanes:
        last = None
        for axis, k in lane:
            part = chunks[k] if axis == "x" else down_own[k]
            if last is not None and last is not part:
                part, last = lax.optimization_barrier((part, last))
            last = shift(part, axis, k if axis == "x" else 1)
            if axis == "x":
                down_own[k] = last
            else:
                down_other[k] = last
    arrived[LAST], _ = lax.optimization_barrier((arrived[LAST], pieces))

    weights = (gate_own, gate_other, up_own, up_other)
    hidden = hidden_part(arrived, weights)
    hidden, queries = lax.optimization_barrier((hidden, queries))
    hidden = [hidden] + [shift(hidden, "x", k) for k in range(1, n_x)]
    intra = intra_part(decay_rate, queries, keys, values)
    prefix = lax.all_to_all(pieces, CTX, 0, 0, tiled=True).reshape(width, HEAD)
    down = stack_rows([part for pair in zip(down_own, down_other) for part in pair])
    hidden[2], intra, down = lax.optimization_barrier((hidden[2], intra, down))
    parts = down_part(down, hidden, n_z * n_core, columns)
    parts, prefix = lax.optimization_barrier((parts, prefix))
    parts = parts.reshape(-1, columns, TILE)
    parts = lax.all_to_all(parts, ("z", "core", "exp"), 0, 0, tiled=True)
    parts = parts.reshape(n_z, n_core, n_exp, columns, TILE)

    mixed, squares = mix_part(decay_rate, intra, queries, prefix)
    squares = [lax.psum(squares, "exp")]
    attention_out = norm_part(
        float(width * n_exp), squares, mixed, norm_gain[None, :], gates
    )
    moe_out = jnp.swapaxes(finish_part(ids, parts, row_weight[None, :]), 0, 1)
    return attention_out, moe_out


def solution(mesh):
    n_core, n_x = 2, 4
    grid = mesh.devices.reshape(-1, n_x, n_core, mesh.devices.shape[1])
    fine = Mesh(grid, ("z", "x", "core", "exp"))
    placed = (
        P(CTX, "exp"),
        P(CTX, "exp"),
        P(CTX, "exp"),
        P(CTX, "exp"),
        P("exp"),
        P("exp"),
        P("exp", None),
        P("exp", None),
        P("exp"),
        P("exp", None, CTX),
        P("exp", None, CTX),
        P("exp", CTX, None),
    )
    return jax.shard_map(
        on_device,
        mesh=fine,
        in_specs=placed,
        out_specs=(P(CTX, "exp"), P("exp", CTX)),
        check_vma=False,
    )
```
